128 devices in a mesh: leaf: 32 (over y, z, core), sub: 4 (over x).
Axes of the slice: x: 4, y: 4, z: 4, core: 2. Of those that a mesh axis runs over, the one named last changes fastest.
Arguments:
- sources: bfloat16 [4096, 8, 128], P(('leaf', 'sub')), may hold values from -6 to 6
- row_basis: bfloat16 [4096, 128, 128], P(('leaf', 'sub')), may hold values from -0.5 to 0.5
- col_basis: bfloat16 [4096, 128, 128], P(('leaf', 'sub')), may hold values from -0.5 to 0.5
- up_transfer: bfloat16 [8064, 128, 128], P(('leaf', 'sub')), may hold values from -0.375 to 0.375
- down_transfer: bfloat16 [8064, 128, 128], P(('leaf', 'sub')), may hold values from -0.375 to 0.375
- near_blocks: bfloat16 [32768, 128, 128], P(('leaf', 'sub')), may hold values from -0.25 to 0.25
- near_list: int32 [4096, 8], P(('leaf', 'sub')), may hold values from -1 to 4095, as said below
- far_blocks: bfloat16 [30720, 128, 128], P(('leaf', 'sub')), may hold values from -0.25 to 0.25
- far_list: int32 [7680, 4], P(('leaf', 'sub')), may hold values from -1 to 4095, as said below
- upper_blocks: bfloat16 [1024, 128, 128], P(('leaf', 'sub')), may hold values from -0.25 to 0.25
- upper_list: int32 [256, 4], P(('leaf', 'sub')), may hold values from 0 to 255, as said below
- root_blocks: bfloat16 [512, 128, 128], P(('leaf', 'sub')), may hold values from -0.25 to 0.25
- root_list: int32 [128, 4], P(('leaf', 'sub')), may hold values from 0 to 127, as said below
- group_blocks: bfloat16 [512, 128, 128], P(('leaf', 'sub')), may hold values from -0.25 to 0.25
- group_list: int32 [128, 4], P(('leaf', 'sub')), may hold values from 0 to 31, as said below
Outputs:
- adjoint_field: float32 [4096, 8, 128], P(('leaf', 'sub'))
The draws below stay inside these ranges and needn't reach their ends.
Inputs may be any that keep to these rules, and one draw needn't show every extreme that they name: `near_list`: slot 0 of row t is t itself. Other entries are -1 for an unused slot, else a leaf s with |s // 32 - t // 32| <= 1, s != t, no leaf twice in a row; used slots come first. `far_list`: entries -1 are unused slots, used slots first and slot 0 always used. A used entry of a level-j node t is a node s of level j with |s // (32 >> j) - t // (32 >> j)| <= 1 and |s - t| >= 2, no node twice in a row. `upper_list`: targets are nodes of the level just under the roots, any subtree. `root_list`: targets are roots of any subtree. `group_list`: targets are group nodes.
All inputs are finite; a program needn't handle non-finite values.
Results may differ from the reference program's by a relative error of at most 0.024.
Values sent between devices are 32-bit elements; how exact they have to be, the bound alone decides.
No kernel may reach another device: no remote copies, remote signals or barrier semaphores. Data moves between devices by JAX's collectives and lax.ppermute only.
A program may use at most 128 MiB of HBM per device.

```python
import jax
import jax.numpy as jnp
from jax import lax

B = 128
R = 128
SRC = 8
LEAF_DEV = 32
NEAR_SLOTS = 8
FAR_SLOTS = 4
TOP_SLOTS = 4
GROUP_SLOTS = 4
ROOTS = 128
GROUPS = 32
LEAVES = 4096
NODES = 63
LOW_NODES = 60
N_SUB = 4


def window_targets(key, per_device, slots, spacing, lowest):
    total = per_device * ROOTS
    nodes = jnp.arange(total)
    owner = nodes // per_device
    offsets = jnp.arange(3 * per_device)
    candidate = (owner[:, None] - 1) * per_device + offsets[None, :]
    allowed = (candidate >= 0) & (candidate < total) & (jnp.abs(candidate - nodes[:, None]) > spacing)
    score = jax.random.randint(jax.random.fold_in(key, 1), (total, 3 * per_device), 0, 65536) * 1024
    score = jnp.where(allowed, score + offsets[None, :], -1)
    _, chosen = lax.top_k(score, slots)
    picked = jnp.take_along_axis(candidate, chosen, axis=1)
    usable = jnp.take_along_axis(allowed, chosen, axis=1)
    filled = jax.random.randint(jax.random.fold_in(key, 2), (total, 1), lowest, slots + 1)
    keep = usable & (jnp.arange(slots)[None, :] < filled)
    return jnp.where(keep, picked, -1).astype(jnp.int32)


def spread_targets(key, rows, count, slots):
    first = jax.random.permutation(jax.random.fold_in(key, 1), rows) % count
    others = jax.random.randint(jax.random.fold_in(key, 2), (rows, slots - 1), 0, count)
    return jnp.concatenate([first[:, None], others], axis=1).astype(jnp.int32)


def draw_near_list(key, part):
    key = jax.random.fold_in(key, 11)
    others = window_targets(key, LEAF_DEV, NEAR_SLOTS - 1, 0, 0)
    itself = jnp.arange(LEAVES)[:, None]
    return jnp.concatenate([itself, others], axis=1).astype(jnp.int32)


def draw_far_list(key, part):
    key = jax.random.fold_in(key, 12)
    levels = LEAF_DEV.bit_length() - 1
    pieces = []
    for level in range(levels - 1):
        width = LEAF_DEV >> level
        listed = window_targets(jax.random.fold_in(key, 20 + level), width, FAR_SLOTS, 1, 1)
        pieces.append(listed.reshape(ROOTS, width, FAR_SLOTS))
    return jnp.concatenate(pieces, axis=1).reshape(-1, FAR_SLOTS).astype(jnp.int32)


def draw_upper_list(key, part):
    key = jax.random.fold_in(key, 13)
    return spread_targets(key, 2 * ROOTS, 2 * ROOTS, TOP_SLOTS)


def draw_root_list(key, part):
    key = jax.random.fold_in(key, 14)
    return spread_targets(key, ROOTS, ROOTS, TOP_SLOTS)


def draw_group_list(key, part):
    key = jax.random.fold_in(key, 15)
    return spread_targets(key, ROOTS, GROUPS, GROUP_SLOTS)


def block_scale(own_key, extent, cuts, low, largest):
    loudness = 1.0
    for position, blocks in cuts:
        draws = jax.random.uniform(jax.random.fold_in(jax.random.fold_in(own_key, 6), position), (blocks,), jnp.float32, low / len(cuts), largest / len(cuts))
        loudness = loudness * jnp.repeat(jnp.exp(draws), extent[position] // blocks).reshape((-1,) + (1,) * (len(extent) - 1 - position))
    return loudness


def bell_draw(own_key, shape, spread, bound, cuts=(), dtype=jnp.bfloat16):
    values = jax.random.normal(own_key, shape, jnp.float32) * spread
    if len(cuts) > 0:
        values = block_scale(own_key, shape, cuts, -0.22, 0.18) * values
    return jnp.clip(values, min=-bound, max=bound).astype(dtype)


def setup_inputs(seed: int = 0) -> dict:
    key_of = jax.random.split(jax.random.key(seed), 16)
    sources = bell_draw(key_of[0], (LEAVES, SRC, B), 1.0, 6.0, ((0, 128),))
    row_basis = bell_draw(key_of[1], (LEAVES, B, R), B ** -0.5, 0.5, ((0, 128),))
    col_basis = bell_draw(key_of[2], (LEAVES, R, B), R ** -0.5, 0.5, ((0, 128),))
    up_transfer = bell_draw(key_of[3], (ROOTS * NODES, R, R), (2 * R) ** -0.5, 0.375, ((0, 128),))
    down_transfer = bell_draw(key_of[4], (ROOTS * NODES, R, R), (2 * R) ** -0.5, 0.375, ((0, 128),))
    near_blocks = bell_draw(key_of[5], (LEAVES * NEAR_SLOTS, B, B), (B * NEAR_SLOTS // 2) ** -0.5, 0.25, ((0, 128),))
    near_list = draw_near_list(jax.random.fold_in(key_of[15], 71), 0)
    far_blocks = bell_draw(key_of[7], (ROOTS * LOW_NODES * FAR_SLOTS, R, R), (R * FAR_SLOTS) ** -0.5, 0.25, ((0, 128),))
    far_list = draw_far_list(jax.random.fold_in(key_of[15], 71), 0)
    upper_blocks = bell_draw(key_of[9], (ROOTS * 2 * TOP_SLOTS, R, R), (R * TOP_SLOTS) ** -0.5, 0.25, ((0, 128),))
    upper_list = draw_upper_list(jax.random.fold_in(key_of[15], 71), 0)
    root_blocks = bell_draw(key_of[11], (ROOTS * TOP_SLOTS, R, R), (R * TOP_SLOTS) ** -0.5, 0.25, ((0, 128),))
    root_list = draw_root_list(jax.random.fold_in(key_of[15], 71), 0)
    group_blocks = bell_draw(key_of[13], (ROOTS * GROUP_SLOTS, R, R), (R * GROUP_SLOTS) ** -0.5, 0.25, ((0, 128),))
    group_list = draw_group_list(jax.random.fold_in(key_of[15], 71), 0)
    return dict(sources=sources, row_basis=row_basis, col_basis=col_basis, up_transfer=up_transfer, down_transfer=down_transfer, near_blocks=near_blocks, near_list=near_list, far_blocks=far_blocks, far_list=far_list, upper_blocks=upper_blocks, upper_list=upper_list, root_blocks=root_blocks, root_list=root_list, group_blocks=group_blocks, group_list=group_list)


def block_map(coef, mats, slots):
    total = coef.shape[0]
    per_root = total // ROOTS
    left = coef.reshape(ROOTS, per_root, coef.shape[1], coef.shape[2])
    right = mats.reshape(ROOTS, per_root, slots, mats.shape[1], mats.shape[2])

    def one_root(pair):
        return jnp.einsum('nsr,nkrq->nksq', pair[0].astype(jnp.float32), pair[1].astype(jnp.float32),
                          precision=lax.Precision.HIGHEST)

    result = lax.map(one_root, (left, right))
    return result.reshape(total * slots, coef.shape[1], mats.shape[2])


def spread_sum(terms, targets, count):
    flat = targets.reshape(-1)
    valid = (flat >= 0).astype(jnp.float32)
    return jax.ops.segment_sum(terms * valid[:, None, None], jnp.maximum(flat, 0).astype(jnp.int32),
                               num_segments=count)


def level_mats(table, level):
    width = LEAF_DEV >> level
    offset = 2 * LEAF_DEV - 2 * width
    return table[:, offset:offset + width].reshape(ROOTS * width, R, R)


def reference(sources, row_basis, col_basis, up_transfer, down_transfer, near_blocks, near_list,
              far_blocks, far_list, upper_blocks, upper_list, root_blocks, root_list, group_blocks, group_list):
    levels = LEAF_DEV.bit_length() - 1
    up_table = up_transfer.reshape(ROOTS, NODES, R, R)
    down_table = down_transfer.reshape(ROOTS, NODES, R, R)
    coefs = [block_map(sources, row_basis, 1).astype(jnp.bfloat16)]
    for level in range(levels):
        product = block_map(coefs[-1], level_mats(up_table, level), 1)
        coefs.append(product.reshape(-1, 2, SRC, R).sum(axis=1).astype(jnp.bfloat16))
    root_up = up_table[:, 2 * LEAF_DEV - 2]
    group_coef = block_map(coefs[levels], root_up, 1).reshape(GROUPS, N_SUB, SRC, R).sum(axis=1)
    near_field = spread_sum(block_map(sources, near_blocks, NEAR_SLOTS), near_list, LEAVES)
    far_table = far_blocks.reshape(ROOTS, LOW_NODES, FAR_SLOTS, R, R)
    far_ids = far_list.reshape(ROOTS, LOW_NODES, FAR_SLOTS)
    fields = []
    for level in range(levels - 1):
        width = LEAF_DEV >> level
        offset = 2 * LEAF_DEV - 2 * width
        mats = far_table[:, offset:offset + width].reshape(-1, R, R)
        ids = far_ids[:, offset:offset + width]
        fields.append(spread_sum(block_map(coefs[level], mats, FAR_SLOTS), ids, ROOTS * width))
    fields.append(spread_sum(block_map(coefs[levels - 1], upper_blocks, TOP_SLOTS), upper_list, 2 * ROOTS))
    root_field = spread_sum(block_map(coefs[levels], root_blocks, TOP_SLOTS), root_list, ROOTS)
    group_terms = block_map(jnp.repeat(group_coef, N_SUB, axis=0), group_blocks, GROUP_SLOTS)
    group_field = spread_sum(group_terms, group_list, GROUPS)
    root_down = down_table[:, 2 * LEAF_DEV - 2]
    downward = root_field + block_map(jnp.repeat(group_field, N_SUB, axis=0), root_down, 1)
    downward = downward.astype(jnp.bfloat16)
    for level in reversed(range(levels)):
        parent = jnp.repeat(downward, 2, axis=0)
        downward = (fields[level] + block_map(parent, level_mats(down_table, level), 1)).astype(jnp.bfloat16)
    return near_field + block_map(downward, col_basis, 1)
```

```python
import functools

import jax
import jax.numpy as jnp
from jax import lax
from jax.experimental import pallas as pl
from jax.experimental.pallas import tpu as pltpu
from jax.sharding import PartitionSpec as P

F32 = jnp.float32
BF16 = jnp.bfloat16
ANY = pl.BlockSpec(memory_space=pl.ANY)
VMEM = pl.BlockSpec(memory_space=pltpu.VMEM)
REPLICAS = 4
UPPER_TERMS, ROOT_TERMS, GROUP_TERMS = 8, 4, 4
TOP_TERMS = UPPER_TERMS + ROOT_TERMS
TERMS = TOP_TERMS + GROUP_TERMS


def rounded(x):
    return x.astype(BF16).astype(F32)


def dot(x, w):
    return jnp.dot(x.astype(BF16), w, preferred_element_type=F32)


def square(w00, w01, w10, w11):
    top = jnp.concatenate([w00, w01], axis=1)
    return jnp.concatenate([top, jnp.concatenate([w10, w11], axis=1)], axis=0)


def diagonal(x, y):
    zero = jnp.zeros_like(x)
    top = jnp.concatenate([x, zero], axis=1)
    return jnp.concatenate([top, jnp.concatenate([zero, y], axis=1)], axis=0)


def quad(xs, ws):
    left = jnp.concatenate([diagonal(xs[0], xs[1]), diagonal(xs[2], xs[3])], axis=0)
    out = dot(left, square(ws[0], ws[2], ws[1], ws[3]))
    n, m = xs[0].shape
    return [out[:n, :m], out[n : 2 * n, :m], out[2 * n : 3 * n, m:], out[3 * n :, m:]]


def exact_parts(x):
    high = rounded(x)
    rest = x - high
    middle = rounded(rest)
    return jnp.concatenate([high, middle, rest - middle], axis=0)


def exact_dot(parts, w):
    n = parts.shape[0] // 3
    out = dot(parts, w)
    return (out[2 * n :] + out[n : 2 * n]) + out[:n]


def level_offset(leaves, level):
    return 2 * leaves - 2 * (leaves >> level)


class Fetches:
    def __init__(self, sem):
        self.sem, self.count = sem, 0

    def __call__(self, src, dst):
        copy = pltpu.make_async_copy(src, dst, self.sem.at[self.count])
        copy.start()
        self.count += 1
        return copy

    def rows(self, src, dst, start, size):
        return self(src.at[pl.ds(start, size)], dst.at[pl.ds(start, size)])


def up_kernel(
    src_hbm, upper_list_hbm, root_list_hbm, rb_hbm, up_hbm, ub_hbm, rt_hbm,
    coef_ref, group_ref, top_ref, src, upper_list, root_list, rb, up, ub, rt, sem,
):
    leaves = src.shape[0]
    levels = leaves.bit_length() - 1
    quarter = leaves // 4
    fetch = Fetches(sem)
    src_copy = fetch(src_hbm, src)
    rb_copies = [fetch.rows(rb_hbm, rb, i * quarter, quarter) for i in range(4)]
    up_copies = [fetch.rows(up_hbm, up, i * quarter, quarter) for i in range(4)]
    rest = fetch.rows(up_hbm, up, leaves, leaves - 1)
    tail = [
        fetch(ub_hbm, ub), fetch(rt_hbm, rt),
        fetch(upper_list_hbm, upper_list), fetch(root_list_hbm, root_list),
    ]

    src_copy.wait()
    for t in range(0, leaves, 4):
        if t % quarter == 0:
            rb_copies[t // quarter].wait()
        span = range(t, t + 4)
        outs = quad([src[i].astype(F32) for i in span], [rb[i] for i in span])
        for i, out in zip(span, outs):
            coef_ref[i] = rounded(out)
    for level in range(levels):
        width = leaves >> level
        offset = level_offset(leaves, level)
        if level == 1:
            rest.wait()
        for t in range(0, width, 4):
            if level == 0 and t % quarter == 0:
                up_copies[t // quarter].wait()
            a = offset + t
            parent = offset + width + t // 2
            c = [coef_ref[a + i] for i in range(min(4, width))]
            if width == 2:
                left = jnp.concatenate(c, axis=1)
                out = dot(left, jnp.concatenate([up[a], up[a + 1]], axis=0))
                coef_ref[parent] = rounded(out)
            else:
                left = jnp.concatenate(
                    [jnp.concatenate(c[:2], axis=1), jnp.concatenate(c[2:], axis=1)], axis=0
                )
                out = dot(left, square(up[a], up[a + 2], up[a + 1], up[a + 3]))
                n, m = c[0].shape
                coef_ref[parent] = rounded(out[:n, :m])
                coef_ref[parent + 1] = rounded(out[n:, m:])
    top = 2 * leaves - 2
    group_ref[...] = dot(coef_ref[top], up[top])
    for c in tail:
        c.wait()
    n, m = src.shape[1:]
    left = diagonal(coef_ref[top - 2], coef_ref[top - 1])
    for k in range(0, 4, 2):
        out = dot(left, square(ub[k], ub[k + 1], ub[4 + k], ub[5 + k]))
        top_ref[k] = out[:n, :m]
        top_ref[k + 1] = out[:n, m:]
        top_ref[4 + k] = out[n:, :m]
        top_ref[5 + k] = out[n:, m:]
    for k in range(0, ROOT_TERMS, 2):
        out = dot(coef_ref[top], jnp.concatenate([rt[k], rt[k + 1]], axis=1))
        top_ref[UPPER_TERMS + k] = out[:, :m]
        top_ref[UPPER_TERMS + k + 1] = out[:, m:]
    top_ref[TOP_TERMS] = jnp.zeros((n, m), F32)
    top_ref[TOP_TERMS, 0:2, 0:4] = upper_list[...].astype(F32)
    top_ref[TOP_TERMS, 2:3, 0:4] = root_list[...].astype(F32)


def scatter_steps(left_of, mats, target_of, accs, slots, first, count, step, level, levels, start, span):
    own_index = lax.axis_index("leaf") * lax.axis_size("sub") + lax.axis_index("sub")
    shift = levels - level
    base = (own_index - 1) * (1 << shift)

    def add(replica, target, term):
        place = target - base
        row = lax.shift_right_arithmetic(place, shift) * span + start + (place & ((1 << shift) - 1))
        row = jnp.where(target >= 0, row, 3 * span)
        accs[replica][row] = accs[replica][row] + term

    def body(c, carry):
        for i in range(0, step, 2):
            t = c * step + i
            x, y = left_of(t), left_of(t + 1)
            n, m = x.shape
            left = diagonal(x, y)
            a, b = t * slots, (t + 1) * slots
            for k in range(0, slots, 2):
                out = dot(left, square(mats[a + k], mats[a + k + 1], mats[b + k], mats[b + k + 1]))
                add(0, target_of(t, k), out[:n, :m])
                add(1, target_of(t, k + 1), out[:n, m:])
                add(2, target_of(t + 1, k), out[n:, :m])
                add(3, target_of(t + 1, k + 1), out[n:, m:])
        return carry

    lax.fori_loop(first // step, (first + count) // step, body, 0)


def store_totals(accs, span, refs):
    for i, ref in enumerate(refs):
        parts = [acc[pl.ds(i * span, span)] for acc in accs]
        ref[0:span] = (parts[0] + parts[1]) + (parts[2] + parts[3])


def near_kernel(
    src_hbm, list_hbm, near, far_prev, far_own, far_next, order,
    prev_ref, own_ref, next_ref, src_ref, near_list, a0, a1, a2, a3, sem,
):
    leaves = src_ref.shape[0]
    slots = near_list.shape[0]
    fetch = Fetches(sem)
    first = [fetch(list_hbm, near_list), fetch(src_hbm, src_ref)]
    accs = (a0, a1, a2, a3)
    for acc in accs:
        acc[...] = jnp.zeros(acc.shape, F32)
    for out, part in ((prev_ref, far_prev), (own_ref, far_own), (next_ref, far_next)):
        out[leaves:] = part[...]
    for c in first:
        c.wait()
    scatter_steps(
        lambda t: src_ref[t].astype(F32), near, lambda t, k: near_list[k, t], accs,
        slots, 0, leaves, 8, 0, leaves.bit_length() - 1, 0, leaves,
    )
    store_totals(accs, leaves, (prev_ref, own_ref, next_ref))


def far_kernel(
    leaves, coef_ref, list_hbm, far, order, prev_ref, own_ref, next_ref, far_list, a0, a1, a2, a3, sem,
):
    levels = leaves.bit_length() - 1
    slots, nodes = far_list.shape
    fetch = Fetches(sem)
    first = fetch(list_hbm, far_list)
    accs = (a0, a1, a2, a3)
    for acc in accs:
        acc[...] = jnp.zeros(acc.shape, F32)
    first.wait()
    for level in range(levels - 1):
        offset = level_offset(leaves, level)
        scatter_steps(
            lambda t: coef_ref[t], far, lambda t, k: far_list[k, t], accs,
            slots, offset, leaves >> level, min(16, leaves >> level), level, levels, offset, nodes,
        )
    store_totals(accs, nodes, (prev_ref, own_ref, next_ref))


def group_kernel(g0, g1, g2, g3, top_ref, group_list, blocks, out_ref):
    coef = (g0[...] + g1[...]) + (g2[...] + g3[...])
    parts = exact_parts(coef)
    m = coef.shape[1]
    for k in range(0, GROUP_TERMS, 2):
        out = exact_dot(parts, jnp.concatenate([blocks[k], blocks[k + 1]], axis=1))
        out_ref[TOP_TERMS + k] = out[:, :m]
        out_ref[TOP_TERMS + k + 1] = out[:, m:]
    out_ref[0:TOP_TERMS] = top_ref[0:TOP_TERMS]
    out_ref[TERMS] = top_ref[TOP_TERMS]
    out_ref[TERMS, 3:4, 0:4] = group_list[...].astype(F32)


def pack_kernel(p0, p1, p2, p3, order, keep_ref, send_ref, ids, a0, a1, a2, a3, sem):
    half = keep_ref.shape[0]
    parts = (p0, p1, p2, p3)
    accs = (a0, a1, a2, a3)
    copies = [pltpu.make_async_copy(p.at[TERMS], ids.at[i], sem.at[i]) for i, p in enumerate(parts)]
    for c in copies:
        c.start()
    for acc in accs:
        acc[...] = jnp.zeros(acc.shape, F32)
    own_sub = lax.axis_index("sub")
    own_core = lax.axis_index("leaf") & 1
    for c in copies:
        c.wait()

    def place(leaf, entry):
        return (leaf & 1) * half + lax.shift_right_arithmetic(leaf, 1) * 4 + entry

    def add(acc, root, entry, term):
        row = place(lax.shift_right_arithmetic(root, 2), entry)
        row = jnp.where((root & 3) == own_sub, row, 2 * half)
        acc[row] = acc[row] + term

    for j in range(UPPER_TERMS):
        for i, (p, acc) in enumerate(zip(parts, accs)):
            node = ids[i, j // 4, j % 4].astype(jnp.int32)
            add(acc, lax.shift_right_arithmetic(node, 1), node & 1, p[j])
    for j in range(ROOT_TERMS):
        for i, (p, acc) in enumerate(zip(parts, accs)):
            root = ids[i, 2, j].astype(jnp.int32)
            add(acc, root, 2, p[UPPER_TERMS + j])
    for j in range(GROUP_TERMS):
        for i, (p, acc) in enumerate(zip(parts, accs)):
            row = place(ids[i, 3, j].astype(jnp.int32), 3)
            acc[row] = acc[row] + p[TOP_TERMS + j]

    def total(first):
        part = pl.ds(first, half)
        return (a0[part] + a1[part]) + (a2[part] + a3[part])

    keep_ref[...] = total(own_core * half)
    send_ref[...] = total((1 - own_core) * half)


def core_kernel(keep_ref, core_ref, out_ref):
    out_ref[...] = (keep_ref[...] + core_ref[...]).reshape(out_ref.shape)


def down_kernel(top, own, prev, after, down_hbm, col_hbm, out_ref, down, col, level_down, sem):
    leaves = out_ref.shape[0]
    levels = leaves.bit_length() - 1
    quarter = leaves // 4
    n, m = out_ref.shape[1:]
    fetch = Fetches(sem)
    rest = fetch.rows(down_hbm, down, leaves, leaves - 1)
    down_copies = [fetch.rows(down_hbm, down, i * quarter, quarter) for i in range(4)]
    col_copies = [fetch.rows(col_hbm, col, i * quarter, quarter) for i in range(4)]

    def total(i):
        return (own[i] + prev[i]) + after[i]

    fields = top[0]
    for i in range(1, top.shape[0]):
        fields = fields + top[i]
    rest.wait()
    root = 2 * leaves - 2
    level_down[root] = rounded(fields[2] + exact_dot(exact_parts(fields[3]), down[root]))
    out = dot(level_down[root], jnp.concatenate([down[root - 2], down[root - 1]], axis=1))
    level_down[root - 2] = rounded(fields[0] + out[:, :m])
    level_down[root - 1] = rounded(fields[1] + out[:, m:])
    for level in reversed(range(levels - 1)):
        width = leaves >> level
        offset = level_offset(leaves, level)
        for t in range(0, width, 4):
            if level == 0 and t % quarter == 0:
                down_copies[t // quarter].wait()
            a = offset + t
            parent = offset + width + t // 2
            left = diagonal(level_down[parent], level_down[parent + 1])
            out = dot(left, square(down[a], down[a + 1], down[a + 2], down[a + 3]))
            outs = (out[:n, :m], out[:n, m:], out[n:, :m], out[n:, m:])
            for i in range(4):
                level_down[a + i] = rounded(total(leaves + a + i) + outs[i])
    for t in range(0, leaves, 4):
        if t % quarter == 0:
            col_copies[t // quarter].wait()
        span = range(t, t + 4)
        outs = quad([level_down[i] for i in span], [col[i] for i in span])
        for i, out in zip(span, outs):
            out_ref[i] = total(i) + out


PARAMS = pltpu.CompilerParams(vmem_limit_bytes=24 * 1024 * 1024)


def cost(us):
    return pl.CostEstimate(flops=int(us * 1e9), bytes_accessed=0, transcendentals=0)


def shards(
    sources, row_basis, col_basis, up_transfer, down_transfer, near_blocks, near_list,
    far_blocks, far_list, upper_blocks, upper_list, root_blocks, root_list, group_blocks, group_list,
):
    in_hbm = functools.partial(pltpu.with_memory_space_constraint, memory_space=pltpu.HBM)
    sources, row_basis, col_basis, up_transfer, down_transfer = map(
        in_hbm, (sources, row_basis, col_basis, up_transfer, down_transfer)
    )
    near_list, far_list, upper_blocks, upper_list, root_blocks, root_list = map(
        in_hbm, (near_list.T, far_list.T, upper_blocks, upper_list, root_blocks, root_list)
    )
    leaves, columns, size = sources.shape
    nodes = up_transfer.shape[0]
    far_slots, far_nodes = far_list.shape
    near_slots = near_list.shape[0]
    groups = lax.axis_size("leaf")
    subs = lax.axis_size("sub")
    devices = groups * subs
    row = (columns, size)

    def shape(*lead):
        return jax.ShapeDtypeStruct(lead + row, F32)

    def buffer(count):
        return pltpu.VMEM((count, size, size), BF16)

    def plane(*lead):
        return pltpu.VMEM(lead + row, F32)

    def copies(count):
        return pltpu.SemaphoreType.DMA((count,))

    def around(x, axis, size, shift):
        return lax.ppermute(x, axis, [(i, (i + shift) % size) for i in range(size)])

    def call(kernel, name, us, outs, operands, specs, scratch):
        return pl.pallas_call(
            kernel,
            out_shape=outs,
            in_specs=specs,
            out_specs=jax.tree.map(lambda _: VMEM, outs),
            scratch_shapes=scratch,
            compiler_params=PARAMS,
            cost_estimate=cost(us),
            name=name,
        )(*operands)

    accumulators = lambda count: [plane(3 * count + 1)] * REPLICAS

    def permuted(x, axis, target):
        return lax.ppermute(x, axis, [(i, target(i)) for i in range(lax.axis_size(axis))])

    def gathered(x):
        return [x] + [permuted(x, "sub", lambda i, s=s: (i + s) % subs) for s in range(1, subs)]

    coef, group, top = call(
        up_kernel, "upward", 4, (shape(nodes), shape(), shape(TOP_TERMS + 1)),
        (sources, upper_list, root_list, row_basis, up_transfer, upper_blocks, root_blocks),
        [ANY] * 7,
        [
            pltpu.VMEM((leaves,) + row, BF16),
            pltpu.VMEM(upper_list.shape, jnp.int32), pltpu.VMEM(root_list.shape, jnp.int32),
            buffer(leaves), buffer(nodes), buffer(UPPER_TERMS), buffer(ROOT_TERMS), copies(14),
        ],
    )
    group_parts = gathered(group)
    far_prev, far_own, far_next = call(
        functools.partial(far_kernel, leaves), "far", 4, (shape(far_nodes),) * 3,
        (coef, far_list, far_blocks, group),
        [VMEM, ANY, VMEM, ANY],
        [pltpu.SMEM((far_slots, far_nodes), jnp.int32)] + accumulators(far_nodes) + [copies(1)],
    )
    terms = call(
        group_kernel, "group", 1, shape(TERMS + 1), (*group_parts, top, group_list, group_blocks),
        [VMEM] * 7, [],
    )
    term_parts = gathered(terms)
    to_prev, own, to_next = call(
        near_kernel, "near", 4, (shape(leaves + far_nodes),) * 3,
        (sources, near_list, near_blocks, far_prev, far_own, far_next, terms),
        [ANY, ANY, VMEM, VMEM, VMEM, VMEM, ANY],
        [pltpu.VMEM((leaves,) + row, BF16), pltpu.SMEM((near_slots, leaves), jnp.int32)]
        + accumulators(leaves) + [copies(2)],
    )
    from_prev = around(to_next, ("leaf", "sub"), devices, 1)
    from_next = around(to_prev, ("leaf", "sub"), devices, -1)

    half = groups // 2 * 4
    keep, send = call(
        pack_kernel, "pack", 0, (shape(half), shape(half)), (*term_parts, own), [VMEM] * 4 + [ANY],
        [pltpu.SMEM((subs,) + row, F32)] + [plane(2 * half + 1)] * 4 + [copies(subs)],
    )
    from_core = permuted(send, "leaf", lambda i: i ^ 1)
    planes = call(core_kernel, "core", 0, shape(groups // 2, 4), (keep, from_core), [VMEM] * 2, [])
    fields = lax.all_to_all(
        planes, "leaf", 0, 0, tiled=True, axis_index_groups=[list(range(c, groups, 2)) for c in range(2)]
    )
    return call(
        down_kernel, "downward", 0, shape(leaves),
        (fields, own, from_prev, from_next, down_transfer, col_basis), [VMEM] * 4 + [ANY] * 2,
        [buffer(nodes), buffer(leaves), plane(nodes), copies(9)],
    )


def solution(mesh):
    blocks = P(("leaf", "sub"), None, None)
    lists = P(("leaf", "sub"), None)
    in_specs = (
        blocks, blocks, blocks, blocks, blocks, blocks, lists,
        blocks, lists, blocks, lists, blocks, lists, blocks, lists,
    )
    return jax.shard_map(shards, mesh=mesh, in_specs=in_specs, out_specs=blocks, check_vma=False)
```

```python
import functools

import jax
import jax.numpy as jnp
from jax import lax
from jax.experimental import pallas as pl
from jax.experimental.pallas import tpu as pltpu
from jax.sharding import PartitionSpec as P

F32 = jnp.float32
BF16 = jnp.bfloat16
ANY = pl.BlockSpec(memory_space=pl.ANY)
VMEM = pl.BlockSpec(memory_space=pltpu.VMEM)
REPLICAS = 4
UPPER_TERMS, ROOT_TERMS, GROUP_TERMS = 8, 4, 4
TOP_TERMS = UPPER_TERMS + ROOT_TERMS
TERMS = TOP_TERMS + GROUP_TERMS


def rounded(x):
    return x.astype(BF16).astype(F32)


def dot(x, w):
    return jnp.dot(x.astype(BF16), w, preferred_element_type=F32)


def square(w00, w01, w10, w11):
    top = jnp.concatenate([w00, w01], axis=1)
    return jnp.concatenate([top, jnp.concatenate([w10, w11], axis=1)], axis=0)


def diagonal(x, y):
    zero = jnp.zeros_like(x)
    top = jnp.concatenate([x, zero], axis=1)
    return jnp.concatenate([top, jnp.concatenate([zero, y], axis=1)], axis=0)


def quad(xs, ws):
    left = jnp.concatenate([diagonal(xs[0], xs[1]), diagonal(xs[2], xs[3])], axis=0)
    out = dot(left, square(ws[0], ws[2], ws[1], ws[3]))
    n, m = xs[0].shape
    return [out[:n, :m], out[n : 2 * n, :m], out[2 * n : 3 * n, m:], out[3 * n :, m:]]


def exact_parts(x):
    high = rounded(x)
    rest = x - high
    middle = rounded(rest)
    return jnp.concatenate([high, middle, rest - middle], axis=0)


def exact_dot(parts, w):
    n = parts.shape[0] // 3
    out = dot(parts, w)
    return (out[2 * n :] + out[n : 2 * n]) + out[:n]


def level_offset(leaves, level):
    return 2 * leaves - 2 * (leaves >> level)


class Fetches:
    def __init__(self, sem):
        self.sem, self.count = sem, 0

    def __call__(self, src, dst):
        copy = pltpu.make_async_copy(src, dst, self.sem.at[self.count])
        copy.start()
        self.count += 1
        return copy

    def rows(self, src, dst, start, size):
        return self(src.at[pl.ds(start, size)], dst.at[pl.ds(start, size)])


def up_kernel(
    src_hbm, upper_list_hbm, root_list_hbm, rb_hbm, up_hbm, ub_hbm, rt_hbm,
    coef_ref, group_ref, top_ref, src, upper_list, root_list, rb, up, ub, rt, sem,
):
    leaves = src.shape[0]
    levels = leaves.bit_length() - 1
    quarter = leaves // 4
    fetch = Fetches(sem)
    src_copy = fetch(src_hbm, src)
    rb_copies = [fetch.rows(rb_hbm, rb, i * quarter, quarter) for i in range(4)]
    up_copies = [fetch.rows(up_hbm, up, i * quarter, quarter) for i in range(4)]
    rest = fetch.rows(up_hbm, up, leaves, leaves - 1)
    tail = [
        fetch(ub_hbm, ub), fetch(rt_hbm, rt),
        fetch(upper_list_hbm, upper_list), fetch(root_list_hbm, root_list),
    ]

    src_copy.wait()
    for t in range(0, leaves, 4):
        if t % quarter == 0:
            rb_copies[t // quarter].wait()
        span = range(t, t + 4)
        outs = quad([src[i].astype(F32) for i in span], [rb[i] for i in span])
        for i, out in zip(span, outs):
            coef_ref[i] = rounded(out)
    for level in range(levels):
        width = leaves >> level
        offset = level_offset(leaves, level)
        if level == 1:
            rest.wait()
        for t in range(0, width, 4):
            if level == 0 and t % quarter == 0:
                up_copies[t // quarter].wait()
            a = offset + t
            parent = offset + width + t // 2
            c = [coef_ref[a + i] for i in range(min(4, width))]
            if width == 2:
                left = jnp.concatenate(c, axis=1)
                out = dot(left, jnp.concatenate([up[a], up[a + 1]], axis=0))
                coef_ref[parent] = rounded(out)
            else:
                left = jnp.concatenate(
                    [jnp.concatenate(c[:2], axis=1), jnp.concatenate(c[2:], axis=1)], axis=0
                )
                out = dot(left, square(up[a], up[a + 2], up[a + 1], up[a + 3]))
                n, m = c[0].shape
                coef_ref[parent] = rounded(out[:n, :m])
                coef_ref[parent + 1] = rounded(out[n:, m:])
    top = 2 * leaves - 2
    group_ref[...] = dot(coef_ref[top], up[top])
    for c in tail:
        c.wait()
    n, m = src.shape[1:]
    left = diagonal(coef_ref[top - 2], coef_ref[top - 1])
    for k in range(0, 4, 2):
        out = dot(left, square(ub[k], ub[k + 1], ub[4 + k], ub[5 + k]))
        top_ref[k] = out[:n, :m]
        top_ref[k + 1] = out[:n, m:]
        top_ref[4 + k] = out[n:, :m]
        top_ref[5 + k] = out[n:, m:]
    for k in range(0, ROOT_TERMS, 2):
        out = dot(coef_ref[top], jnp.concatenate([rt[k], rt[k + 1]], axis=1))
        top_ref[UPPER_TERMS + k] = out[:, :m]
        top_ref[UPPER_TERMS + k + 1] = out[:, m:]
    top_ref[TOP_TERMS] = jnp.zeros((n, m), F32)
    top_ref[TOP_TERMS, 0:2, 0:4] = upper_list[...].astype(F32)
    top_ref[TOP_TERMS, 2:3, 0:4] = root_list[...].astype(F32)


def scatter_steps(left_of, mats, target_of, accs, slots, first, count, step, level, levels, start, span):
    own_index = lax.axis_index("leaf") * lax.axis_size("sub") + lax.axis_index("sub")
    shift = levels - level
    base = (own_index - 1) * (1 << shift)

    def add(replica, target, term):
        place = target - base
        row = lax.shift_right_arithmetic(place, shift) * span + start + (place & ((1 << shift) - 1))
        row = jnp.where(target >= 0, row, 3 * span)
        accs[replica][row] = accs[replica][row] + term

    def body(c, carry):
        for i in range(0, step, 2):
            t = c * step + i
            x, y = left_of(t), left_of(t + 1)
            n, m = x.shape
            left = diagonal(x, y)
            a, b = t * slots, (t + 1) * slots
            for k in range(0, slots, 2):
                out = dot(left, square(mats[a + k], mats[a + k + 1], mats[b + k], mats[b + k + 1]))
                add(0, target_of(t, k), out[:n, :m])
                add(1, target_of(t, k + 1), out[:n, m:])
                add(2, target_of(t + 1, k), out[n:, :m])
                add(3, target_of(t + 1, k + 1), out[n:, m:])
        return carry

    lax.fori_loop(first // step, (first + count) // step, body, 0)


def store_totals(accs, span, refs):
    odd = lax.axis_index("sub") & 1
    for first, ref in zip((2 - 2 * odd, 1, 2 * odd), refs):
        parts = [acc[pl.ds(first * span, span)] for acc in accs]
        ref[0:span] = (parts[0] + parts[1]) + (parts[2] + parts[3])


def near_kernel(
    src_ref, list_hbm, near, far_a, far_own, far_b, order,
    a_ref, own_ref, b_ref, near_list, a0, a1, a2, a3, sem,
):
    leaves = src_ref.shape[0]
    slots = near_list.shape[0]
    fetch = Fetches(sem)
    first = fetch(list_hbm, near_list)
    accs = (a0, a1, a2, a3)
    for acc in accs:
        acc[...] = jnp.zeros(acc.shape, F32)
    for out, part in ((a_ref, far_a), (own_ref, far_own), (b_ref, far_b)):
        out[leaves:] = part[...]
    first.wait()
    scatter_steps(
        lambda t: src_ref[t].astype(F32), near, lambda t, k: near_list[k, t], accs,
        slots, 0, leaves, 8, 0, leaves.bit_length() - 1, 0, leaves,
    )
    store_totals(accs, leaves, (a_ref, own_ref, b_ref))


def far_kernel(
    leaves, coef_ref, list_hbm, far, order, a_ref, own_ref, b_ref, far_list, a0, a1, a2, a3, sem,
):
    levels = leaves.bit_length() - 1
    slots, nodes = far_list.shape
    fetch = Fetches(sem)
    first = fetch(list_hbm, far_list)
    accs = (a0, a1, a2, a3)
    for acc in accs:
        acc[...] = jnp.zeros(acc.shape, F32)
    first.wait()
    for level in range(levels - 1):
        offset = level_offset(leaves, level)
        scatter_steps(
            lambda t: coef_ref[t], far, lambda t, k: far_list[k, t], accs,
            slots, offset, leaves >> level, min(16, leaves >> level), level, levels, offset, nodes,
        )
    store_totals(accs, nodes, (a_ref, own_ref, b_ref))


def group_kernel(g0, g1, g2, g3, top_ref, group_list, blocks, out_ref):
    coef = (g0[...] + g1[...]) + (g2[...] + g3[...])
    parts = exact_parts(coef)
    m = coef.shape[1]
    for k in range(0, GROUP_TERMS, 2):
        out = exact_dot(parts, jnp.concatenate([blocks[k], blocks[k + 1]], axis=1))
        out_ref[TOP_TERMS + k] = out[:, :m]
        out_ref[TOP_TERMS + k + 1] = out[:, m:]
    out_ref[0:TOP_TERMS] = top_ref[0:TOP_TERMS]
    out_ref[TERMS] = top_ref[TOP_TERMS]
    out_ref[TERMS, 3:4, 0:4] = group_list[...].astype(F32)


def pack_kernel(p0, p1, p2, p3, to_a, to_b, keep_ref, send_ref, held_a, held_b, ids, a0, a1, a2, a3, sem):
    half = keep_ref.shape[0]
    parts = (p0, p1, p2, p3)
    accs = (a0, a1, a2, a3)
    copies = [pltpu.make_async_copy(p.at[TERMS], ids.at[i], sem.at[i]) for i, p in enumerate(parts)]
    for c in copies:
        c.start()
    for acc in accs:
        acc[...] = jnp.zeros(acc.shape, F32)
    own_sub = lax.axis_index("sub")
    own_core = lax.axis_index("leaf") & 1
    for c in copies:
        c.wait()

    def place(leaf, entry):
        return (leaf & 1) * half + lax.shift_right_arithmetic(leaf, 1) * 4 + entry

    def add(acc, root, entry, term):
        row = place(lax.shift_right_arithmetic(root, 2), entry)
        row = jnp.where((root & 3) == own_sub, row, 2 * half)
        acc[row] = acc[row] + term

    for j in range(UPPER_TERMS):
        for i, (p, acc) in enumerate(zip(parts, accs)):
            node = ids[i, j // 4, j % 4].astype(jnp.int32)
            add(acc, lax.shift_right_arithmetic(node, 1), node & 1, p[j])
    for j in range(ROOT_TERMS):
        for i, (p, acc) in enumerate(zip(parts, accs)):
            root = ids[i, 2, j].astype(jnp.int32)
            add(acc, root, 2, p[UPPER_TERMS + j])
    for j in range(GROUP_TERMS):
        for i, (p, acc) in enumerate(zip(parts, accs)):
            row = place(ids[i, 3, j].astype(jnp.int32), 3)
            acc[row] = acc[row] + p[TOP_TERMS + j]

    def total(first):
        part = pl.ds(first, half)
        return (a0[part] + a1[part]) + (a2[part] + a3[part])

    keep_ref[...] = total(own_core * half)
    send_ref[...] = total((1 - own_core) * half)


def split_kernel(unit, *refs):
    parts, outs = refs[:-4], refs[-4:]
    rows = outs[0].shape[0]
    own = (lax.axis_index("leaf") // unit) & 3
    for digit, out in enumerate(outs):
        part = pl.ds((own ^ digit) * rows, rows)
        total = parts[0][part]
        for p in parts[1:]:
            total = total + p[part]
        out[...] = total


def down_kernel(t0, t1, t2, t3, own, from_a, from_b, down, col, out_ref, level_down):
    leaves = out_ref.shape[0]
    levels = leaves.bit_length() - 1
    n, m = out_ref.shape[1:]

    def total(i):
        return (own[i] + from_a[i]) + from_b[i]

    fields = (t0[...] + t1[...]) + (t2[...] + t3[...])
    root = 2 * leaves - 2
    level_down[root] = rounded(fields[2] + exact_dot(exact_parts(fields[3]), down[root]))
    out = dot(level_down[root], jnp.concatenate([down[root - 2], down[root - 1]], axis=1))
    level_down[root - 2] = rounded(fields[0] + out[:, :m])
    level_down[root - 1] = rounded(fields[1] + out[:, m:])
    for level in reversed(range(levels - 1)):
        width = leaves >> level
        offset = level_offset(leaves, level)
        for t in range(0, width, 4):
            a = offset + t
            parent = offset + width + t // 2
            left = diagonal(level_down[parent], level_down[parent + 1])
            out = dot(left, square(down[a], down[a + 1], down[a + 2], down[a + 3]))
            outs = (out[:n, :m], out[:n, m:], out[n:, :m], out[n:, m:])
            for i in range(4):
                level_down[a + i] = rounded(total(leaves + a + i) + outs[i])
    for t in range(0, leaves, 4):
        span = range(t, t + 4)
        outs = quad([level_down[i] for i in span], [col[i] for i in span])
        for i, out in zip(span, outs):
            out_ref[i] = total(i) + out


PARAMS = pltpu.CompilerParams(vmem_limit_bytes=24 * 1024 * 1024)


def cost(us):
    return pl.CostEstimate(flops=int(us * 1e9), bytes_accessed=0, transcendentals=0)


def shards(
    sources, row_basis, col_basis, up_transfer, down_transfer, near_blocks, near_list,
    far_blocks, far_list, upper_blocks, upper_list, root_blocks, root_list, group_blocks, group_list,
):
    in_hbm = functools.partial(pltpu.with_memory_space_constraint, memory_space=pltpu.HBM)
    up_sources, row_basis, up_transfer = map(in_hbm, (sources, row_basis, up_transfer))
    near_list, far_list, upper_blocks, upper_list, root_blocks, root_list = map(
        in_hbm, (near_list.T, far_list.T, upper_blocks, upper_list, root_blocks, root_list)
    )
    leaves, columns, size = sources.shape
    nodes = up_transfer.shape[0]
    far_slots, far_nodes = far_list.shape
    near_slots = near_list.shape[0]
    groups = lax.axis_size("leaf")
    subs = lax.axis_size("sub")
    devices = groups * subs
    row = (columns, size)

    def shape(*lead):
        return jax.ShapeDtypeStruct(lead + row, F32)

    def buffer(count):
        return pltpu.VMEM((count, size, size), BF16)

    def plane(*lead):
        return pltpu.VMEM(lead + row, F32)

    def copies(count):
        return pltpu.SemaphoreType.DMA((count,))

    def call(kernel, name, us, outs, operands, specs, scratch, out_specs=None, **options):
        return pl.pallas_call(
            kernel,
            out_shape=outs,
            in_specs=specs,
            out_specs=out_specs or jax.tree.map(lambda _: VMEM, outs),
            scratch_shapes=scratch,
            compiler_params=PARAMS,
            cost_estimate=cost(us),
            name=name,
            **options,
        )(*operands)

    accumulators = lambda count: [plane(3 * count + 1)] * REPLICAS

    def permuted(x, axis, target):
        count = lax.axis_size(axis)
        return lax.ppermute(x, axis, [(i, target(i)) for i in range(count)])

    def gathered(x):
        return [x] + [permuted(x, "sub", lambda i, s=s: i ^ s) for s in range(1, subs)]

    def exchanged(parts, unit):
        return parts[:1] + tuple(
            permuted(x, "leaf", lambda i, s=s: i ^ (s * unit)) for s, x in enumerate(parts[1:], 1)
        )

    coef, group, top = call(
        up_kernel, "upward", 4, (shape(nodes), shape(), shape(TOP_TERMS + 1)),
        (up_sources, upper_list, root_list, row_basis, up_transfer, upper_blocks, root_blocks),
        [ANY] * 7,
        [
            pltpu.VMEM((leaves,) + row, BF16),
            pltpu.VMEM(upper_list.shape, jnp.int32), pltpu.VMEM(root_list.shape, jnp.int32),
            buffer(leaves), buffer(nodes), buffer(UPPER_TERMS), buffer(ROOT_TERMS), copies(14),
        ],
    )
    group_parts = gathered(group)
    far_a, far_own, far_b = call(
        functools.partial(far_kernel, leaves), "far", 4, (shape(far_nodes),) * 3,
        (coef, far_list, far_blocks, group),
        [VMEM, ANY, VMEM, ANY],
        [pltpu.SMEM((far_slots, far_nodes), jnp.int32)] + accumulators(far_nodes) + [copies(1)],
    )
    terms = call(
        group_kernel, "group", 1, shape(TERMS + 1), (*group_parts, top, group_list, group_blocks),
        [VMEM] * 7, [],
    )
    term_parts = gathered(terms)
    to_a, own, to_b = call(
        near_kernel, "near", 4, (shape(leaves + far_nodes),) * 3,
        (sources, near_list, near_blocks, far_a, far_own, far_b, terms),
        [VMEM, ANY, VMEM, VMEM, VMEM, VMEM, ANY],
        [pltpu.SMEM((near_slots, leaves), jnp.int32)] + accumulators(leaves) + [copies(1)],
    )
    half = groups // 2 * 4
    window = shape(leaves + far_nodes)
    keep, send, to_a, to_b = call(
        pack_kernel, "pack", 0, (shape(half), shape(half), window, window), (*term_parts, to_a, to_b),
        [VMEM] * 4 + [ANY] * 2, [pltpu.SMEM((subs,) + row, F32)] + [plane(2 * half + 1)] * 4 + [copies(subs)],
        out_specs=(VMEM, VMEM, ANY, ANY), input_output_aliases={4: 2, 5: 3},
    )
    everyone = ("leaf", "sub")
    from_a = permuted(to_a, everyone, lambda i: i ^ 1)
    from_b = permuted(to_b, everyone, lambda i: min(max(((i + 1) ^ 1) - 1, 0), devices - 1))
    from_core = permuted(send, "leaf", lambda i: i ^ 1)
    y_unit, z_unit = groups // 4, groups // 16
    by_y = call(
        functools.partial(split_kernel, y_unit), "split_y", 1, (shape(half // 4),) * 4, (keep, from_core), [VMEM] * 2, []
    )
    by_z = call(
        functools.partial(split_kernel, z_unit), "split_z", 0, (shape(half // 16),) * 4,
        exchanged(by_y, y_unit), [VMEM] * 4, [],
    )
    return call(
        down_kernel, "downward", 0, shape(leaves),
        (*exchanged(by_z, z_unit), own, from_a, from_b, down_transfer, col_basis), [VMEM] * 9, [plane(nodes)],
    )


def solution(mesh):
    blocks = P(("leaf", "sub"), None, None)
    lists = P(("leaf", "sub"), None)
    in_specs = (
        blocks, blocks, blocks, blocks, blocks, blocks, lists,
        blocks, lists, blocks, lists, blocks, lists, blocks, lists,
    )
    return jax.shard_map(shards, mesh=mesh, in_specs=in_specs, out_specs=blocks, check_vma=False)
```

```python
import functools

import jax
import jax.numpy as jnp
from jax import lax
from jax.experimental import pallas as pl
from jax.experimental.pallas import tpu as pltpu
from jax.sharding import PartitionSpec as P

F32 = jnp.float32
BF16 = jnp.bfloat16
ANY = pl.BlockSpec(memory_space=pl.ANY)
VMEM = pl.BlockSpec(memory_space=pltpu.VMEM)
REPLICAS = 4
UPPER_TERMS, ROOT_TERMS, GROUP_TERMS = 8, 4, 4
TOP_TERMS = UPPER_TERMS + ROOT_TERMS
TERMS = TOP_TERMS + GROUP_TERMS


def rounded(x):
    return x.astype(BF16).astype(F32)


def dot(x, w):
    return jnp.dot(x.astype(BF16), w, preferred_element_type=F32)


def square(w00, w01, w10, w11):
    top = jnp.concatenate([w00, w01], axis=1)
    return jnp.concatenate([top, jnp.concatenate([w10, w11], axis=1)], axis=0)


def diagonal(x, y):
    zero = jnp.zeros_like(x)
    top = jnp.concatenate([x, zero], axis=1)
    return jnp.concatenate([top, jnp.concatenate([zero, y], axis=1)], axis=0)


def quad(xs, ws):
    left = jnp.concatenate([diagonal(xs[0], xs[1]), diagonal(xs[2], xs[3])], axis=0)
    out = dot(left, square(ws[0], ws[2], ws[1], ws[3]))
    n, m = xs[0].shape
    return [out[:n, :m], out[n : 2 * n, :m], out[2 * n : 3 * n, m:], out[3 * n :, m:]]


def exact_parts(x):
    high = rounded(x)
    rest = x - high
    middle = rounded(rest)
    return jnp.concatenate([high, middle, rest - middle], axis=0)


def exact_dot(parts, w):
    n = parts.shape[0] // 3
    out = dot(parts, w)
    return (out[2 * n :] + out[n : 2 * n]) + out[:n]


def level_offset(leaves, level):
    return 2 * leaves - 2 * (leaves >> level)


class Fetches:
    def __init__(self, sem):
        self.sem, self.count = sem, 0

    def __call__(self, src, dst):
        copy = pltpu.make_async_copy(src, dst, self.sem.at[self.count])
        copy.start()
        self.count += 1
        return copy

    def rows(self, src, dst, start, size):
        return self(src.at[pl.ds(start, size)], dst.at[pl.ds(start, size)])


def up_kernel(
    src_hbm, upper_list_hbm, root_list_hbm, rb_hbm, up_hbm, ub_hbm, rt_hbm,
    coef_ref, group_ref, top_ref, src, upper_list, root_list, rb, up, ub, rt, sem,
):
    leaves = src.shape[0]
    levels = leaves.bit_length() - 1
    quarter = leaves // 4
    fetch = Fetches(sem)
    src_copy = fetch(src_hbm, src)
    rb_copies = [fetch.rows(rb_hbm, rb, i * quarter, quarter) for i in range(4)]
    up_copies = [fetch.rows(up_hbm, up, i * quarter, quarter) for i in range(4)]
    rest = fetch.rows(up_hbm, up, leaves, leaves - 1)
    tail = [
        fetch(ub_hbm, ub), fetch(rt_hbm, rt),
        fetch(upper_list_hbm, upper_list), fetch(root_list_hbm, root_list),
    ]

    src_copy.wait()
    for t in range(0, leaves, 4):
        if t % quarter == 0:
            rb_copies[t // quarter].wait()
        span = range(t, t + 4)
        outs = quad([src[i].astype(F32) for i in span], [rb[i] for i in span])
        for i, out in zip(span, outs):
            coef_ref[i] = rounded(out)
    for level in range(levels):
        width = leaves >> level
        offset = level_offset(leaves, level)
        if level == 1:
            rest.wait()
        for t in range(0, width, 4):
            if level == 0 and t % quarter == 0:
                up_copies[t // quarter].wait()
            a = offset + t
            parent = offset + width + t // 2
            c = [coef_ref[a + i] for i in range(min(4, width))]
            if width == 2:
                left = jnp.concatenate(c, axis=1)
                out = dot(left, jnp.concatenate([up[a], up[a + 1]], axis=0))
                coef_ref[parent] = rounded(out)
            else:
                left = jnp.concatenate(
                    [jnp.concatenate(c[:2], axis=1), jnp.concatenate(c[2:], axis=1)], axis=0
                )
                out = dot(left, square(up[a], up[a + 2], up[a + 1], up[a + 3]))
                n, m = c[0].shape
                coef_ref[parent] = rounded(out[:n, :m])
                coef_ref[parent + 1] = rounded(out[n:, m:])
    top = 2 * leaves - 2
    group_ref[...] = dot(coef_ref[top], up[top])
    for c in tail:
        c.wait()
    n, m = src.shape[1:]
    left = diagonal(coef_ref[top - 2], coef_ref[top - 1])
    for k in range(0, 4, 2):
        out = dot(left, square(ub[k], ub[k + 1], ub[4 + k], ub[5 + k]))
        top_ref[k] = out[:n, :m]
        top_ref[k + 1] = out[:n, m:]
        top_ref[4 + k] = out[n:, :m]
        top_ref[5 + k] = out[n:, m:]
    for k in range(0, ROOT_TERMS, 2):
        out = dot(coef_ref[top], jnp.concatenate([rt[k], rt[k + 1]], axis=1))
        top_ref[UPPER_TERMS + k] = out[:, :m]
        top_ref[UPPER_TERMS + k + 1] = out[:, m:]
    top_ref[TOP_TERMS] = jnp.zeros((n, m), F32)
    top_ref[TOP_TERMS, 0:2, 0:4] = upper_list[...].astype(F32)
    top_ref[TOP_TERMS, 2:3, 0:4] = root_list[...].astype(F32)


def scatter_steps(left_of, mats, target_of, accs, slots, first, count, step, level, levels, start, span):
    own_index = lax.axis_index("leaf") * lax.axis_size("sub") + lax.axis_index("sub")
    shift = levels - level
    base = (own_index - 1) * (1 << shift)

    def add(replica, target, term):
        place = target - base
        row = lax.shift_right_arithmetic(place, shift) * span + start + (place & ((1 << shift) - 1))
        row = jnp.where(target >= 0, row, 3 * span)
        accs[replica][row] = accs[replica][row] + term

    def body(c, carry):
        for i in range(0, step, 2):
            t = c * step + i
            x, y = left_of(t), left_of(t + 1)
            n, m = x.shape
            left = diagonal(x, y)
            a, b = t * slots, (t + 1) * slots
            for k in range(0, slots, 2):
                out = dot(left, square(mats[a + k], mats[a + k + 1], mats[b + k], mats[b + k + 1]))
                add(0, target_of(t, k), out[:n, :m])
                add(1, target_of(t, k + 1), out[:n, m:])
                add(2, target_of(t + 1, k), out[n:, :m])
                add(3, target_of(t + 1, k + 1), out[n:, m:])
        return carry

    lax.fori_loop(first // step, (first + count) // step, body, 0)


def store_totals(accs, span, refs):
    for i, ref in enumerate(refs):
        parts = [acc[pl.ds(i * span, span)] for acc in accs]
        ref[0:span] = (parts[0] + parts[1]) + (parts[2] + parts[3])


def near_kernel(
    src_ref, list_hbm, near, far_prev, far_own, far_next, order,
    prev_ref, own_ref, next_ref, near_list, a0, a1, a2, a3, sem,
):
    leaves = src_ref.shape[0]
    slots = near_list.shape[0]
    fetch = Fetches(sem)
    first = fetch(list_hbm, near_list)
    accs = (a0, a1, a2, a3)
    for acc in accs:
        acc[...] = jnp.zeros(acc.shape, F32)
    for out, part in ((prev_ref, far_prev), (own_ref, far_own), (next_ref, far_next)):
        out[leaves:] = part[...]
    first.wait()
    scatter_steps(
        lambda t: src_ref[t].astype(F32), near, lambda t, k: near_list[k, t], accs,
        slots, 0, leaves, 8, 0, leaves.bit_length() - 1, 0, leaves,
    )
    store_totals(accs, leaves, (prev_ref, own_ref, next_ref))


def far_kernel(
    leaves, coef_ref, list_hbm, far, order, prev_ref, own_ref, next_ref, far_list, a0, a1, a2, a3, sem,
):
    levels = leaves.bit_length() - 1
    slots, nodes = far_list.shape
    fetch = Fetches(sem)
    first = fetch(list_hbm, far_list)
    accs = (a0, a1, a2, a3)
    for acc in accs:
        acc[...] = jnp.zeros(acc.shape, F32)
    first.wait()
    for level in range(levels - 1):
        offset = level_offset(leaves, level)
        scatter_steps(
            lambda t: coef_ref[t], far, lambda t, k: far_list[k, t], accs,
            slots, offset, leaves >> level, min(16, leaves >> level), level, levels, offset, nodes,
        )
    store_totals(accs, nodes, (prev_ref, own_ref, next_ref))


def group_kernel(g0, g1, g2, g3, top_ref, group_list, blocks, out_ref):
    coef = (g0[...] + g1[...]) + (g2[...] + g3[...])
    parts = exact_parts(coef)
    m = coef.shape[1]
    for k in range(0, GROUP_TERMS, 2):
        out = exact_dot(parts, jnp.concatenate([blocks[k], blocks[k + 1]], axis=1))
        out_ref[TOP_TERMS + k] = out[:, :m]
        out_ref[TOP_TERMS + k + 1] = out[:, m:]
    out_ref[0:TOP_TERMS] = top_ref[0:TOP_TERMS]
    out_ref[TERMS] = top_ref[TOP_TERMS]
    out_ref[TERMS, 3:4, 0:4] = group_list[...].astype(F32)


def pack_kernel(p0, p1, p2, p3, order, keep_ref, send_ref, ids, a0, a1, a2, a3, sem):
    half = keep_ref.shape[0]
    parts = (p0, p1, p2, p3)
    accs = (a0, a1, a2, a3)
    copies = [pltpu.make_async_copy(p.at[TERMS], ids.at[i], sem.at[i]) for i, p in enumerate(parts)]
    for c in copies:
        c.start()
    for acc in accs:
        acc[...] = jnp.zeros(acc.shape, F32)
    own_sub = lax.axis_index("sub")
    own_core = lax.axis_index("leaf") & 1
    for c in copies:
        c.wait()

    def place(leaf, entry):
        return (leaf & 1) * half + lax.shift_right_arithmetic(leaf, 1) * 4 + entry

    def add(acc, root, entry, term):
        row = place(lax.shift_right_arithmetic(root, 2), entry)
        row = jnp.where((root & 3) == own_sub, row, 2 * half)
        acc[row] = acc[row] + term

    for j in range(UPPER_TERMS):
        for i, (p, acc) in enumerate(zip(parts, accs)):
            node = ids[i, j // 4, j % 4].astype(jnp.int32)
            add(acc, lax.shift_right_arithmetic(node, 1), node & 1, p[j])
    for j in range(ROOT_TERMS):
        for i, (p, acc) in enumerate(zip(parts, accs)):
            root = ids[i, 2, j].astype(jnp.int32)
            add(acc, root, 2, p[UPPER_TERMS + j])
    for j in range(GROUP_TERMS):
        for i, (p, acc) in enumerate(zip(parts, accs)):
            row = place(ids[i, 3, j].astype(jnp.int32), 3)
            acc[row] = acc[row] + p[TOP_TERMS + j]

    def total(first):
        part = pl.ds(first, half)
        return (a0[part] + a1[part]) + (a2[part] + a3[part])

    keep_ref[...] = total(own_core * half)
    send_ref[...] = total((1 - own_core) * half)


def core_kernel(keep_ref, core_ref, out_ref):
    out_ref[...] = (keep_ref[...] + core_ref[...]).reshape(out_ref.shape)


def merge_kernel(own_ref, prev_ref, next_ref, out_ref):
    out_ref[...] = (own_ref[...] + prev_ref[...]) + next_ref[...]


def down_kernel(top, total, down, col_hbm, out_ref, col, level_down, sem):
    leaves = out_ref.shape[0]
    levels = leaves.bit_length() - 1
    quarter = leaves // 4
    n, m = out_ref.shape[1:]
    fetch = Fetches(sem)
    col_copies = [fetch.rows(col_hbm, col, i * quarter, quarter) for i in range(4)]

    fields = top[0]
    for i in range(1, top.shape[0]):
        fields = fields + top[i]
    root = 2 * leaves - 2
    level_down[root] = rounded(fields[2] + exact_dot(exact_parts(fields[3]), down[root]))
    out = dot(level_down[root], jnp.concatenate([down[root - 2], down[root - 1]], axis=1))
    level_down[root - 2] = rounded(fields[0] + out[:, :m])
    level_down[root - 1] = rounded(fields[1] + out[:, m:])
    for level in reversed(range(levels - 1)):
        width = leaves >> level
        offset = level_offset(leaves, level)
        for t in range(0, width, 4):
            a = offset + t
            parent = offset + width + t // 2
            left = diagonal(level_down[parent], level_down[parent + 1])
            out = dot(left, square(down[a], down[a + 1], down[a + 2], down[a + 3]))
            outs = (out[:n, :m], out[:n, m:], out[n:, :m], out[n:, m:])
            for i in range(4):
                level_down[a + i] = rounded(total[leaves + a + i] + outs[i])
    for t in range(0, leaves, 4):
        if t % quarter == 0:
            col_copies[t // quarter].wait()
        span = range(t, t + 4)
        outs = quad([level_down[i] for i in span], [col[i] for i in span])
        for i, out in zip(span, outs):
            out_ref[i] = total[i] + out


PARAMS = pltpu.CompilerParams(vmem_limit_bytes=24 * 1024 * 1024)


def cost(us):
    return pl.CostEstimate(flops=int(us * 1e9), bytes_accessed=0, transcendentals=0)


def shards(
    sources, row_basis, col_basis, up_transfer, down_transfer, near_blocks, near_list,
    far_blocks, far_list, upper_blocks, upper_list, root_blocks, root_list, group_blocks, group_list,
):
    in_hbm = functools.partial(pltpu.with_memory_space_constraint, memory_space=pltpu.HBM)
    up_sources, row_basis, up_transfer, col_basis = map(in_hbm, (sources, row_basis, up_transfer, col_basis))
    near_list, far_list, upper_blocks, upper_list, root_blocks, root_list = map(
        in_hbm, (near_list.T, far_list.T, upper_blocks, upper_list, root_blocks, root_list)
    )
    leaves, columns, size = sources.shape
    nodes = up_transfer.shape[0]
    far_slots, far_nodes = far_list.shape
    near_slots = near_list.shape[0]
    groups = lax.axis_size("leaf")
    subs = lax.axis_size("sub")
    devices = groups * subs
    row = (columns, size)

    def shape(*lead):
        return jax.ShapeDtypeStruct(lead + row, F32)

    def buffer(count):
        return pltpu.VMEM((count, size, size), BF16)

    def plane(*lead):
        return pltpu.VMEM(lead + row, F32)

    def copies(count):
        return pltpu.SemaphoreType.DMA((count,))

    def call(kernel, name, us, outs, operands, specs, scratch, out_specs=None, **options):
        return pl.pallas_call(
            kernel,
            out_shape=outs,
            in_specs=specs,
            out_specs=out_specs or jax.tree.map(lambda _: VMEM, outs),
            scratch_shapes=scratch,
            compiler_params=PARAMS,
            cost_estimate=cost(us),
            name=name,
            **options,
        )(*operands)

    accumulators = lambda count: [plane(3 * count + 1)] * REPLICAS

    def permuted(x, axis, target):
        count = lax.axis_size(axis)
        return lax.ppermute(x, axis, [(i, target(i)) for i in range(count)])

    def gathered(x):
        return [x] + [permuted(x, "sub", lambda i, s=s: i ^ s) for s in range(1, subs)]

    coef, group, top = call(
        up_kernel, "upward", 4, (shape(nodes), shape(), shape(TOP_TERMS + 1)),
        (up_sources, upper_list, root_list, row_basis, up_transfer, upper_blocks, root_blocks),
        [ANY] * 7,
        [
            pltpu.VMEM((leaves,) + row, BF16),
            pltpu.VMEM(upper_list.shape, jnp.int32), pltpu.VMEM(root_list.shape, jnp.int32),
            buffer(leaves), buffer(nodes), buffer(UPPER_TERMS), buffer(ROOT_TERMS), copies(14),
        ],
    )
    group_parts = gathered(group)
    far_prev, far_own, far_next = call(
        functools.partial(far_kernel, leaves), "far", 4, (shape(far_nodes),) * 3,
        (coef, far_list, far_blocks, group),
        [VMEM, ANY, VMEM, ANY],
        [pltpu.SMEM((far_slots, far_nodes), jnp.int32)] + accumulators(far_nodes) + [copies(1)],
    )
    terms = call(
        group_kernel, "group", 1, shape(TERMS + 1), (*group_parts, top, group_list, group_blocks),
        [VMEM] * 7, [],
    )
    term_parts = gathered(terms)
    to_prev, own, to_next = call(
        near_kernel, "near", 4, (shape(leaves + far_nodes),) * 3,
        (sources, near_list, near_blocks, far_prev, far_own, far_next, terms),
        [VMEM, ANY, VMEM, VMEM, VMEM, VMEM, ANY],
        [pltpu.SMEM((near_slots, leaves), jnp.int32)] + accumulators(leaves) + [copies(1)],
    )
    half = groups // 2 * 4
    everyone = ("leaf", "sub")
    window = shape(leaves + far_nodes)
    from_prev = permuted(to_next, everyone, lambda i: (i + 1) % devices)
    from_next = permuted(to_prev, everyone, lambda i: (i - 1) % devices)
    total = call(merge_kernel, "merge", 20, window, (own, from_prev, from_next), [VMEM] * 3, [])

    keep, send = call(
        pack_kernel, "pack", 0, (shape(half), shape(half)), (*term_parts, own), [VMEM] * 4 + [ANY],
        [pltpu.SMEM((subs,) + row, F32)] + [plane(2 * half + 1)] * 4 + [copies(subs)],
    )
    from_core = permuted(send, "leaf", lambda i: i ^ 1)
    planes = call(core_kernel, "core", 0, shape(groups // 2, 4), (keep, from_core), [VMEM] * 2, [])
    fields = lax.all_to_all(
        planes, "leaf", 0, 0, tiled=True, axis_index_groups=[list(range(c, groups, 2)) for c in range(2)]
    )
    return call(
        down_kernel, "downward", 0, shape(leaves), (fields, total, down_transfer, col_basis), [VMEM] * 3 + [ANY],
        [buffer(leaves), plane(nodes), copies(4)],
    )


def solution(mesh):
    blocks = P(("leaf", "sub"), None, None)
    lists = P(("leaf", "sub"), None)
    in_specs = (
        blocks, blocks, blocks, blocks, blocks, blocks, lists,
        blocks, lists, blocks, lists, blocks, lists, blocks, lists,
    )
    return jax.shard_map(shards, mesh=mesh, in_specs=in_specs, out_specs=blocks, check_vma=False)
```

```python
import functools

import jax
import jax.numpy as jnp
from jax import lax
from jax.experimental import pallas as pl
from jax.experimental.pallas import tpu as pltpu
from jax.sharding import PartitionSpec as P

F32 = jnp.float32
BF16 = jnp.bfloat16
ANY = pl.BlockSpec(memory_space=pl.ANY)
VMEM = pl.BlockSpec(memory_space=pltpu.VMEM)
REPLICAS = 4
UPPER_TERMS, ROOT_TERMS, GROUP_TERMS = 8, 4, 4
TOP_TERMS = UPPER_TERMS + ROOT_TERMS
TERMS = TOP_TERMS + GROUP_TERMS


def rounded(x):
    return x.astype(BF16).astype(F32)


def dot(x, w):
    return jnp.dot(x.astype(BF16), w, preferred_element_type=F32)


def square(w00, w01, w10, w11):
    top = jnp.concatenate([w00, w01], axis=1)
    return jnp.concatenate([top, jnp.concatenate([w10, w11], axis=1)], axis=0)


def diagonal(x, y):
    zero = jnp.zeros_like(x)
    top = jnp.concatenate([x, zero], axis=1)
    return jnp.concatenate([top, jnp.concatenate([zero, y], axis=1)], axis=0)


def quad(xs, ws):
    left = jnp.concatenate([diagonal(xs[0], xs[1]), diagonal(xs[2], xs[3])], axis=0)
    out = dot(left, square(ws[0], ws[2], ws[1], ws[3]))
    n, m = xs[0].shape
    return [out[:n, :m], out[n : 2 * n, :m], out[2 * n : 3 * n, m:], out[3 * n :, m:]]


def exact_parts(x):
    high = rounded(x)
    rest = x - high
    middle = rounded(rest)
    return jnp.concatenate([high, middle, rest - middle], axis=0)


def exact_dot(parts, w):
    n = parts.shape[0] // 3
    out = dot(parts, w)
    return (out[2 * n :] + out[n : 2 * n]) + out[:n]


def level_offset(leaves, level):
    return 2 * leaves - 2 * (leaves >> level)


class Fetches:
    def __init__(self, sem):
        self.sem, self.count = sem, 0

    def __call__(self, src, dst):
        copy = pltpu.make_async_copy(src, dst, self.sem.at[self.count])
        copy.start()
        self.count += 1
        return copy

    def rows(self, src, dst, start, size):
        return self(src.at[pl.ds(start, size)], dst.at[pl.ds(start, size)])


def up_kernel(
    src_hbm, upper_list_hbm, root_list_hbm, rb_hbm, up_hbm, ub_hbm, rt_hbm,
    coef_ref, group_ref, top_ref, src, upper_list, root_list, rb, up, ub, rt, sem,
):
    leaves = src.shape[0]
    levels = leaves.bit_length() - 1
    quarter = leaves // 4
    fetch = Fetches(sem)
    src_copy = fetch(src_hbm, src)
    rb_copies = [fetch.rows(rb_hbm, rb, i * quarter, quarter) for i in range(4)]
    up_copies = [fetch.rows(up_hbm, up, i * quarter, quarter) for i in range(4)]
    rest = fetch.rows(up_hbm, up, leaves, leaves - 1)
    tail = [
        fetch(ub_hbm, ub), fetch(rt_hbm, rt),
        fetch(upper_list_hbm, upper_list), fetch(root_list_hbm, root_list),
    ]

    src_copy.wait()
    for t in range(0, leaves, 4):
        if t % quarter == 0:
            rb_copies[t // quarter].wait()
        span = range(t, t + 4)
        outs = quad([src[i].astype(F32) for i in span], [rb[i] for i in span])
        for i, out in zip(span, outs):
            coef_ref[i] = rounded(out)
    for level in range(levels):
        width = leaves >> level
        offset = level_offset(leaves, level)
        if level == 1:
            rest.wait()
        for t in range(0, width, 4):
            if level == 0 and t % quarter == 0:
                up_copies[t // quarter].wait()
            a = offset + t
            parent = offset + width + t // 2
            c = [coef_ref[a + i] for i in range(min(4, width))]
            if width == 2:
                left = jnp.concatenate(c, axis=1)
                out = dot(left, jnp.concatenate([up[a], up[a + 1]], axis=0))
                coef_ref[parent] = rounded(out)
            else:
                left = jnp.concatenate(
                    [jnp.concatenate(c[:2], axis=1), jnp.concatenate(c[2:], axis=1)], axis=0
                )
                out = dot(left, square(up[a], up[a + 2], up[a + 1], up[a + 3]))
                n, m = c[0].shape
                coef_ref[parent] = rounded(out[:n, :m])
                coef_ref[parent + 1] = rounded(out[n:, m:])
    top = 2 * leaves - 2
    group_ref[...] = dot(coef_ref[top], up[top])
    for c in tail:
        c.wait()
    n, m = src.shape[1:]
    left = diagonal(coef_ref[top - 2], coef_ref[top - 1])
    for k in range(0, 4, 2):
        out = dot(left, square(ub[k], ub[k + 1], ub[4 + k], ub[5 + k]))
        top_ref[k] = out[:n, :m]
        top_ref[k + 1] = out[:n, m:]
        top_ref[4 + k] = out[n:, :m]
        top_ref[5 + k] = out[n:, m:]
    for k in range(0, ROOT_TERMS, 2):
        out = dot(coef_ref[top], jnp.concatenate([rt[k], rt[k + 1]], axis=1))
        top_ref[UPPER_TERMS + k] = out[:, :m]
        top_ref[UPPER_TERMS + k + 1] = out[:, m:]
    top_ref[TOP_TERMS] = jnp.zeros((n, m), F32)
    top_ref[TOP_TERMS, 0:2, 0:4] = upper_list[...].astype(F32)
    top_ref[TOP_TERMS, 2:3, 0:4] = root_list[...].astype(F32)


def scatter_steps(left_of, mats, target_of, accs, slots, first, count, step, level, levels, start, span):
    own_index = lax.axis_index("leaf") * lax.axis_size("sub") + lax.axis_index("sub")
    shift = levels - level
    base = (own_index - 1) * (1 << shift)

    def add(replica, target, term):
        place = target - base
        row = lax.shift_right_arithmetic(place, shift) * span + start + (place & ((1 << shift) - 1))
        row = jnp.where(target >= 0, row, 3 * span)
        accs[replica][row] = accs[replica][row] + term

    def body(c, carry):
        for i in range(0, step, 2):
            t = c * step + i
            x, y = left_of(t), left_of(t + 1)
            n, m = x.shape
            left = diagonal(x, y)
            a, b = t * slots, (t + 1) * slots
            for k in range(0, slots, 2):
                out = dot(left, square(mats[a + k], mats[a + k + 1], mats[b + k], mats[b + k + 1]))
                add(0, target_of(t, k), out[:n, :m])
                add(1, target_of(t, k + 1), out[:n, m:])
                add(2, target_of(t + 1, k), out[n:, :m])
                add(3, target_of(t + 1, k + 1), out[n:, m:])
        return carry

    lax.fori_loop(first // step, (first + count) // step, body, 0)


def store_totals(accs, span, refs):
    for i, ref in enumerate(refs):
        parts = [acc[pl.ds(i * span, span)] for acc in accs]
        ref[0:span] = (parts[0] + parts[1]) + (parts[2] + parts[3])


def near_kernel(
    src_ref, list_hbm, near, far_prev, far_own, far_next, order,
    prev_ref, own_ref, next_ref, near_list, a0, a1, a2, a3, sem,
):
    leaves = src_ref.shape[0]
    slots = near_list.shape[0]
    fetch = Fetches(sem)
    first = fetch(list_hbm, near_list)
    accs = (a0, a1, a2, a3)
    for acc in accs:
        acc[...] = jnp.zeros(acc.shape, F32)
    for out, part in ((prev_ref, far_prev), (own_ref, far_own), (next_ref, far_next)):
        out[leaves:] = part[...]
    first.wait()
    scatter_steps(
        lambda t: src_ref[t].astype(F32), near, lambda t, k: near_list[k, t], accs,
        slots, 0, leaves, 8, 0, leaves.bit_length() - 1, 0, leaves,
    )
    store_totals(accs, leaves, (prev_ref, own_ref, next_ref))


def far_kernel(
    leaves, coef_ref, list_hbm, far, order, prev_ref, own_ref, next_ref, far_list, a0, a1, a2, a3, sem,
):
    levels = leaves.bit_length() - 1
    slots, nodes = far_list.shape
    fetch = Fetches(sem)
    first = fetch(list_hbm, far_list)
    accs = (a0, a1, a2, a3)
    for acc in accs:
        acc[...] = jnp.zeros(acc.shape, F32)
    first.wait()
    for level in range(levels - 1):
        offset = level_offset(leaves, level)
        scatter_steps(
            lambda t: coef_ref[t], far, lambda t, k: far_list[k, t], accs,
            slots, offset, leaves >> level, min(16, leaves >> level), level, levels, offset, nodes,
        )
    store_totals(accs, nodes, (prev_ref, own_ref, next_ref))


def group_kernel(g0, g1, g2, g3, top_ref, group_list, blocks, out_ref):
    coef = (g0[...] + g1[...]) + (g2[...] + g3[...])
    parts = exact_parts(coef)
    m = coef.shape[1]
    for k in range(0, GROUP_TERMS, 2):
        out = exact_dot(parts, jnp.concatenate([blocks[k], blocks[k + 1]], axis=1))
        out_ref[TOP_TERMS + k] = out[:, :m]
        out_ref[TOP_TERMS + k + 1] = out[:, m:]
    out_ref[0:TOP_TERMS] = top_ref[0:TOP_TERMS]
    out_ref[TERMS] = top_ref[TOP_TERMS]
    out_ref[TERMS, 3:4, 0:4] = group_list[...].astype(F32)


def pack_kernel(p0, p1, p2, p3, order, keep_ref, send_ref, ids, a0, a1, a2, a3, sem):
    half = keep_ref.shape[0]
    parts = (p0, p1, p2, p3)
    accs = (a0, a1, a2, a3)
    copies = [pltpu.make_async_copy(p.at[TERMS], ids.at[i], sem.at[i]) for i, p in enumerate(parts)]
    for c in copies:
        c.start()
    for acc in accs:
        acc[...] = jnp.zeros(acc.shape, F32)
    own_sub = lax.axis_index("sub")
    own_core = lax.axis_index("leaf") & 1
    for c in copies:
        c.wait()

    def place(leaf, entry):
        return (leaf & 1) * half + lax.shift_right_arithmetic(leaf, 1) * 4 + entry

    def add(acc, root, entry, term):
        row = place(lax.shift_right_arithmetic(root, 2), entry)
        row = jnp.where((root & 3) == own_sub, row, 2 * half)
        acc[row] = acc[row] + term

    for j in range(UPPER_TERMS):
        for i, (p, acc) in enumerate(zip(parts, accs)):
            node = ids[i, j // 4, j % 4].astype(jnp.int32)
            add(acc, lax.shift_right_arithmetic(node, 1), node & 1, p[j])
    for j in range(ROOT_TERMS):
        for i, (p, acc) in enumerate(zip(parts, accs)):
            root = ids[i, 2, j].astype(jnp.int32)
            add(acc, root, 2, p[UPPER_TERMS + j])
    for j in range(GROUP_TERMS):
        for i, (p, acc) in enumerate(zip(parts, accs)):
            row = place(ids[i, 3, j].astype(jnp.int32), 3)
            acc[row] = acc[row] + p[TOP_TERMS + j]

    def total(first):
        part = pl.ds(first, half)
        return (a0[part] + a1[part]) + (a2[part] + a3[part])

    keep_ref[...] = total(own_core * half)
    send_ref[...] = total((1 - own_core) * half)


def core_kernel(keep_ref, core_ref, out_ref):
    out_ref[...] = (keep_ref[...] + core_ref[...]).reshape(out_ref.shape)


def down_kernel(top, own, from_prev, from_next, down, col_hbm, out_ref, col, level_down, sem):
    leaves = out_ref.shape[0]
    levels = leaves.bit_length() - 1
    quarter = leaves // 4
    n, m = out_ref.shape[1:]
    fetch = Fetches(sem)
    col_copies = [fetch.rows(col_hbm, col, i * quarter, quarter) for i in range(4)]

    def total(i):
        return (own[i] + from_prev[i]) + from_next[i]

    fields = top[0]
    for i in range(1, top.shape[0]):
        fields = fields + top[i]
    root = 2 * leaves - 2
    level_down[root] = rounded(fields[2] + exact_dot(exact_parts(fields[3]), down[root]))
    out = dot(level_down[root], jnp.concatenate([down[root - 2], down[root - 1]], axis=1))
    level_down[root - 2] = rounded(fields[0] + out[:, :m])
    level_down[root - 1] = rounded(fields[1] + out[:, m:])
    for level in reversed(range(levels - 1)):
        width = leaves >> level
        offset = level_offset(leaves, level)
        for t in range(0, width, 4):
            a = offset + t
            parent = offset + width + t // 2
            left = diagonal(level_down[parent], level_down[parent + 1])
            out = dot(left, square(down[a], down[a + 1], down[a + 2], down[a + 3]))
            outs = (out[:n, :m], out[:n, m:], out[n:, :m], out[n:, m:])
            for i in range(4):
                level_down[a + i] = rounded(total(leaves + a + i) + outs[i])
    for t in range(0, leaves, 4):
        if t % quarter == 0:
            col_copies[t // quarter].wait()
        span = range(t, t + 4)
        outs = quad([level_down[i] for i in span], [col[i] for i in span])
        for i, out in zip(span, outs):
            out_ref[i] = total(i) + out


PARAMS = pltpu.CompilerParams(vmem_limit_bytes=24 * 1024 * 1024)


def cost(us):
    return pl.CostEstimate(flops=int(us * 1e9), bytes_accessed=0, transcendentals=0)


def shards(
    sources, row_basis, col_basis, up_transfer, down_transfer, near_blocks, near_list,
    far_blocks, far_list, upper_blocks, upper_list, root_blocks, root_list, group_blocks, group_list,
):
    in_hbm = functools.partial(pltpu.with_memory_space_constraint, memory_space=pltpu.HBM)
    up_sources, row_basis, up_transfer, col_basis = map(in_hbm, (sources, row_basis, up_transfer, col_basis))
    near_list, far_list, upper_blocks, upper_list, root_blocks, root_list = map(
        in_hbm, (near_list.T, far_list.T, upper_blocks, upper_list, root_blocks, root_list)
    )
    leaves, columns, size = sources.shape
    nodes = up_transfer.shape[0]
    far_slots, far_nodes = far_list.shape
    near_slots = near_list.shape[0]
    groups = lax.axis_size("leaf")
    subs = lax.axis_size("sub")
    devices = groups * subs
    row = (columns, size)

    def shape(*lead):
        return jax.ShapeDtypeStruct(lead + row, F32)

    def buffer(count):
        return pltpu.VMEM((count, size, size), BF16)

    def plane(*lead):
        return pltpu.VMEM(lead + row, F32)

    def copies(count):
        return pltpu.SemaphoreType.DMA((count,))

    def call(kernel, name, us, outs, operands, specs, scratch, out_specs=None, **options):
        return pl.pallas_call(
            kernel,
            out_shape=outs,
            in_specs=specs,
            out_specs=out_specs or jax.tree.map(lambda _: VMEM, outs),
            scratch_shapes=scratch,
            compiler_params=PARAMS,
            cost_estimate=cost(us),
            name=name,
            **options,
        )(*operands)

    accumulators = lambda count: [plane(3 * count + 1)] * REPLICAS

    def permuted(x, axis, target):
        count = lax.axis_size(axis)
        return lax.ppermute(x, axis, [(i, target(i)) for i in range(count)])

    def gathered(x):
        return [x] + [permuted(x, "sub", lambda i, s=s: i ^ s) for s in (2, 1, 3)]

    coef, group, top = call(
        up_kernel, "upward", 4, (shape(nodes), shape(), shape(TOP_TERMS + 1)),
        (up_sources, upper_list, root_list, row_basis, up_transfer, upper_blocks, root_blocks),
        [ANY] * 7,
        [
            pltpu.VMEM((leaves,) + row, BF16),
            pltpu.VMEM(upper_list.shape, jnp.int32), pltpu.VMEM(root_list.shape, jnp.int32),
            buffer(leaves), buffer(nodes), buffer(UPPER_TERMS), buffer(ROOT_TERMS), copies(14),
        ],
    )
    group_parts = gathered(group)
    far_prev, far_own, far_next = call(
        functools.partial(far_kernel, leaves), "far", 4, (shape(far_nodes),) * 3,
        (coef, far_list, far_blocks, group),
        [VMEM, ANY, VMEM, ANY],
        [pltpu.SMEM((far_slots, far_nodes), jnp.int32)] + accumulators(far_nodes) + [copies(1)],
    )
    terms = call(
        group_kernel, "group", 1, shape(TERMS + 1), (*group_parts, top, group_list, group_blocks),
        [VMEM] * 7, [],
    )
    term_parts = gathered(terms)
    to_prev, own, to_next = call(
        near_kernel, "near", 4, (shape(leaves + far_nodes),) * 3,
        (sources, near_list, near_blocks, far_prev, far_own, far_next, terms),
        [VMEM, ANY, VMEM, VMEM, VMEM, VMEM, ANY],
        [pltpu.SMEM((near_slots, leaves), jnp.int32)] + accumulators(leaves) + [copies(1)],
    )
    half = groups // 2 * 4
    everyone = ("leaf", "sub")
    from_prev = permuted(to_next, everyone, lambda i: (i + 1) % devices)
    from_next = permuted(to_prev, everyone, lambda i: (i - 1) % devices)

    keep, send = call(
        pack_kernel, "pack", 0, (shape(half), shape(half)), (*term_parts, own), [VMEM] * 4 + [ANY],
        [pltpu.SMEM((subs,) + row, F32)] + [plane(2 * half + 1)] * 4 + [copies(subs)],
    )
    from_core = permuted(send, "leaf", lambda i: i ^ 1)
    planes = call(core_kernel, "core", 0, shape(groups // 2, 4), (keep, from_core), [VMEM] * 2, [])
    fields = lax.all_to_all(
        planes, "leaf", 0, 0, tiled=True, axis_index_groups=[list(range(c, groups, 2)) for c in range(2)]
    )
    return call(
        down_kernel, "downward", 0, shape(leaves), (fields, own, from_prev, from_next, down_transfer, col_basis), [VMEM] * 5 + [ANY],
        [buffer(leaves), plane(nodes), copies(4)],
    )


def solution(mesh):
    blocks = P(("leaf", "sub"), None, None)
    lists = P(("leaf", "sub"), None)
    in_specs = (
        blocks, blocks, blocks, blocks, blocks, blocks, lists,
        blocks, lists, blocks, lists, blocks, lists, blocks, lists,
    )
    return jax.shard_map(shards, mesh=mesh, in_specs=in_specs, out_specs=blocks, check_vma=False)
```

```python
import functools

import jax
import jax.numpy as jnp
from jax import lax
from jax.experimental import pallas as pl
from jax.experimental.pallas import tpu as pltpu
from jax.sharding import PartitionSpec as P

F32 = jnp.float32
BF16 = jnp.bfloat16
ANY = pl.BlockSpec(memory_space=pl.ANY)
VMEM = pl.BlockSpec(memory_space=pltpu.VMEM)
REPLICAS = 4
SUB_ORDER, PLANE_ORDER = (3, 1, 2), (2, 1, 3)
UPPER_TERMS, ROOT_TERMS, GROUP_TERMS = 8, 4, 4
TOP_TERMS = UPPER_TERMS + ROOT_TERMS
TERMS = TOP_TERMS + GROUP_TERMS


def rounded(x):
    return x.astype(BF16).astype(F32)


def dot(x, w):
    return jnp.dot(x.astype(BF16), w, preferred_element_type=F32)


def square(w00, w01, w10, w11):
    top = jnp.concatenate([w00, w01], axis=1)
    return jnp.concatenate([top, jnp.concatenate([w10, w11], axis=1)], axis=0)


def diagonal(x, y):
    zero = jnp.zeros_like(x)
    top = jnp.concatenate([x, zero], axis=1)
    return jnp.concatenate([top, jnp.concatenate([zero, y], axis=1)], axis=0)


def quad(xs, ws):
    left = jnp.concatenate([diagonal(xs[0], xs[1]), diagonal(xs[2], xs[3])], axis=0)
    out = dot(left, square(ws[0], ws[2], ws[1], ws[3]))
    n, m = xs[0].shape
    return [out[:n, :m], out[n : 2 * n, :m], out[2 * n : 3 * n, m:], out[3 * n :, m:]]


def exact_parts(x):
    high = rounded(x)
    rest = x - high
    middle = rounded(rest)
    return jnp.concatenate([high, middle, rest - middle], axis=0)


def exact_dot(parts, w):
    n = parts.shape[0] // 3
    out = dot(parts, w)
    return (out[2 * n :] + out[n : 2 * n]) + out[:n]


def level_offset(leaves, level):
    return 2 * leaves - 2 * (leaves >> level)


class Fetches:
    def __init__(self, sem):
        self.sem, self.count = sem, 0

    def __call__(self, src, dst):
        copy = pltpu.make_async_copy(src, dst, self.sem.at[self.count])
        copy.start()
        self.count += 1
        return copy

    def rows(self, src, dst, start, size):
        return self(src.at[pl.ds(start, size)], dst.at[pl.ds(start, size)])


def up_kernel(
    src_hbm, upper_list_hbm, root_list_hbm, rb_hbm, up_hbm, ub_hbm, rt_hbm,
    coef_ref, group_ref, top_ref, src, upper_list, root_list, rb, up, ub, rt, sem,
):
    leaves = src.shape[0]
    levels = leaves.bit_length() - 1
    quarter = leaves // 4
    fetch = Fetches(sem)
    src_copy = fetch(src_hbm, src)
    rb_copies = [fetch.rows(rb_hbm, rb, i * quarter, quarter) for i in range(4)]
    up_copies = [fetch.rows(up_hbm, up, i * quarter, quarter) for i in range(4)]
    rest = fetch.rows(up_hbm, up, leaves, leaves - 1)
    tail = [
        fetch(ub_hbm, ub), fetch(rt_hbm, rt),
        fetch(upper_list_hbm, upper_list), fetch(root_list_hbm, root_list),
    ]

    src_copy.wait()
    for t in range(0, leaves, 4):
        if t % quarter == 0:
            rb_copies[t // quarter].wait()
        span = range(t, t + 4)
        outs = quad([src[i].astype(F32) for i in span], [rb[i] for i in span])
        for i, out in zip(span, outs):
            coef_ref[i] = rounded(out)
    for level in range(levels):
        width = leaves >> level
        offset = level_offset(leaves, level)
        if level == 1:
            rest.wait()
        for t in range(0, width, 4):
            if level == 0 and t % quarter == 0:
                up_copies[t // quarter].wait()
            a = offset + t
            parent = offset + width + t // 2
            c = [coef_ref[a + i] for i in range(min(4, width))]
            if width == 2:
                left = jnp.concatenate(c, axis=1)
                out = dot(left, jnp.concatenate([up[a], up[a + 1]], axis=0))
                coef_ref[parent] = rounded(out)
            else:
                left = jnp.concatenate(
                    [jnp.concatenate(c[:2], axis=1), jnp.concatenate(c[2:], axis=1)], axis=0
                )
                out = dot(left, square(up[a], up[a + 2], up[a + 1], up[a + 3]))
                n, m = c[0].shape
                coef_ref[parent] = rounded(out[:n, :m])
                coef_ref[parent + 1] = rounded(out[n:, m:])
    top = 2 * leaves - 2
    group_ref[...] = dot(coef_ref[top], up[top])
    for c in tail:
        c.wait()
    n, m = src.shape[1:]
    left = diagonal(coef_ref[top - 2], coef_ref[top - 1])
    for k in range(0, 4, 2):
        out = dot(left, square(ub[k], ub[k + 1], ub[4 + k], ub[5 + k]))
        top_ref[k] = out[:n, :m]
        top_ref[k + 1] = out[:n, m:]
        top_ref[4 + k] = out[n:, :m]
        top_ref[5 + k] = out[n:, m:]
    for k in range(0, ROOT_TERMS, 2):
        out = dot(coef_ref[top], jnp.concatenate([rt[k], rt[k + 1]], axis=1))
        top_ref[UPPER_TERMS + k] = out[:, :m]
        top_ref[UPPER_TERMS + k + 1] = out[:, m:]
    top_ref[TOP_TERMS] = jnp.zeros((n, m), F32)
    top_ref[TOP_TERMS, 0:2, 0:4] = upper_list[...].astype(F32)
    top_ref[TOP_TERMS, 2:3, 0:4] = root_list[...].astype(F32)


def scatter_steps(left_of, mats, target_of, accs, slots, first, count, step, level, levels, start, span):
    own_index = lax.axis_index("leaf") * lax.axis_size("sub") + lax.axis_index("sub")
    shift = levels - level
    base = (own_index - 1) * (1 << shift)

    def add(replica, target, term):
        place = target - base
        row = lax.shift_right_arithmetic(place, shift) * span + start + (place & ((1 << shift) - 1))
        row = jnp.where(target >= 0, row, 3 * span)
        accs[replica][row] = accs[replica][row] + term

    def body(c, carry):
        for i in range(0, step, 2):
            t = c * step + i
            x, y = left_of(t), left_of(t + 1)
            n, m = x.shape
            left = diagonal(x, y)
            a, b = t * slots, (t + 1) * slots
            for k in range(0, slots, 2):
                out = dot(left, square(mats[a + k], mats[a + k + 1], mats[b + k], mats[b + k + 1]))
                add(0, target_of(t, k), out[:n, :m])
                add(1, target_of(t, k + 1), out[:n, m:])
                add(2, target_of(t + 1, k), out[n:, :m])
                add(3, target_of(t + 1, k + 1), out[n:, m:])
        return carry

    lax.fori_loop(first // step, (first + count) // step, body, 0)


def store_totals(accs, span, refs):
    for i, ref in enumerate(refs):
        parts = [acc[pl.ds(i * span, span)] for acc in accs]
        ref[0:span] = (parts[0] + parts[1]) + (parts[2] + parts[3])


def near_kernel(
    src_ref, list_hbm, near, far_prev, far_own, far_next, order,
    prev_ref, own_ref, next_ref, near_list, a0, a1, a2, a3, sem,
):
    leaves = src_ref.shape[0]
    slots = near_list.shape[0]
    fetch = Fetches(sem)
    first = fetch(list_hbm, near_list)
    accs = (a0, a1, a2, a3)
    for acc in accs:
        acc[...] = jnp.zeros(acc.shape, F32)
    for out, part in ((prev_ref, far_prev), (own_ref, far_own), (next_ref, far_next)):
        out[leaves:] = part[...]
    first.wait()
    scatter_steps(
        lambda t: src_ref[t].astype(F32), near, lambda t, k: near_list[k, t], accs,
        slots, 0, leaves, 8, 0, leaves.bit_length() - 1, 0, leaves,
    )
    store_totals(accs, leaves, (prev_ref, own_ref, next_ref))


def far_kernel(
    leaves, coef_ref, list_hbm, far, order, prev_ref, own_ref, next_ref, far_list, a0, a1, a2, a3, sem,
):
    levels = leaves.bit_length() - 1
    slots, nodes = far_list.shape
    fetch = Fetches(sem)
    first = fetch(list_hbm, far_list)
    accs = (a0, a1, a2, a3)
    for acc in accs:
        acc[...] = jnp.zeros(acc.shape, F32)
    first.wait()
    for level in range(levels - 1):
        offset = level_offset(leaves, level)
        scatter_steps(
            lambda t: coef_ref[t], far, lambda t, k: far_list[k, t], accs,
            slots, offset, leaves >> level, min(16, leaves >> level), level, levels, offset, nodes,
        )
    store_totals(accs, nodes, (prev_ref, own_ref, next_ref))


def group_kernel(g0, g1, g2, g3, top_ref, group_list, blocks, out_ref):
    coef = (g0[...] + g1[...]) + (g2[...] + g3[...])
    parts = exact_parts(coef)
    m = coef.shape[1]
    for k in range(0, GROUP_TERMS, 2):
        out = exact_dot(parts, jnp.concatenate([blocks[k], blocks[k + 1]], axis=1))
        out_ref[TOP_TERMS + k] = out[:, :m]
        out_ref[TOP_TERMS + k + 1] = out[:, m:]
    out_ref[0:TOP_TERMS] = top_ref[0:TOP_TERMS]
    out_ref[TERMS] = top_ref[TOP_TERMS]
    out_ref[TERMS, 3:4, 0:4] = group_list[...].astype(F32)


def pack_kernel(p0, p1, p2, p3, order, keep_ref, send_ref, ids, a0, a1, a2, a3, sem):
    half = keep_ref.shape[0]
    parts = (p0, p1, p2, p3)
    accs = (a0, a1, a2, a3)
    copies = [pltpu.make_async_copy(p.at[TERMS], ids.at[i], sem.at[i]) for i, p in enumerate(parts)]
    for c in copies:
        c.start()
    for acc in accs:
        acc[...] = jnp.zeros(acc.shape, F32)
    own_sub = lax.axis_index("sub")
    own_core = lax.axis_index("leaf") & 1
    for c in copies:
        c.wait()

    def place(leaf, entry):
        return (leaf & 1) * half + lax.shift_right_arithmetic(leaf, 1) * 4 + entry

    def add(acc, root, entry, term):
        row = place(lax.shift_right_arithmetic(root, 2), entry)
        row = jnp.where((root & 3) == own_sub, row, 2 * half)
        acc[row] = acc[row] + term

    for j in range(UPPER_TERMS):
        for i, (p, acc) in enumerate(zip(parts, accs)):
            node = ids[i, j // 4, j % 4].astype(jnp.int32)
            add(acc, lax.shift_right_arithmetic(node, 1), node & 1, p[j])
    for j in range(ROOT_TERMS):
        for i, (p, acc) in enumerate(zip(parts, accs)):
            root = ids[i, 2, j].astype(jnp.int32)
            add(acc, root, 2, p[UPPER_TERMS + j])
    for j in range(GROUP_TERMS):
        for i, (p, acc) in enumerate(zip(parts, accs)):
            row = place(ids[i, 3, j].astype(jnp.int32), 3)
            acc[row] = acc[row] + p[TOP_TERMS + j]

    def total(first):
        part = pl.ds(first, half)
        return (a0[part] + a1[part]) + (a2[part] + a3[part])

    keep_ref[...] = total(own_core * half)
    send_ref[...] = total((1 - own_core) * half)


def merge_kernel(own_ref, prev_ref, out_ref):
    out_ref[...] = own_ref[...] + prev_ref[...]


def split_kernel(unit, held, *refs):
    refs = refs[: len(refs) - held]
    parts, outs = refs[: -4 - held], refs[-4:]
    rows = outs[0].shape[0]
    own = (lax.axis_index("leaf") // unit) & 3
    for digit, out in enumerate(outs):
        part = pl.ds((own ^ digit) * rows, rows)
        total = parts[0][part]
        for p in parts[1:]:
            total = total + p[part]
        out[...] = total


def down_kernel(t0, t1, t2, t3, own, from_next, down, col, out_ref, level_down):
    leaves = out_ref.shape[0]
    levels = leaves.bit_length() - 1
    n, m = out_ref.shape[1:]

    def total(i):
        return own[i] + from_next[i]

    fields = (t0[...] + t1[...]) + (t2[...] + t3[...])
    root = 2 * leaves - 2
    level_down[root] = rounded(fields[2] + exact_dot(exact_parts(fields[3]), down[root]))
    out = dot(level_down[root], jnp.concatenate([down[root - 2], down[root - 1]], axis=1))
    level_down[root - 2] = rounded(fields[0] + out[:, :m])
    level_down[root - 1] = rounded(fields[1] + out[:, m:])
    for level in reversed(range(levels - 1)):
        width = leaves >> level
        offset = level_offset(leaves, level)
        for t in range(0, width, 4):
            a = offset + t
            parent = offset + width + t // 2
            left = diagonal(level_down[parent], level_down[parent + 1])
            out = dot(left, square(down[a], down[a + 1], down[a + 2], down[a + 3]))
            outs = (out[:n, :m], out[:n, m:], out[n:, :m], out[n:, m:])
            for i in range(4):
                level_down[a + i] = rounded(total(leaves + a + i) + outs[i])
    for t in range(0, leaves, 4):
        span = range(t, t + 4)
        outs = quad([level_down[i] for i in span], [col[i] for i in span])
        for i, out in zip(span, outs):
            out_ref[i] = total(i) + out


PARAMS = pltpu.CompilerParams(vmem_limit_bytes=24 * 1024 * 1024)


def cost(us):
    return pl.CostEstimate(flops=int(us * 1e9), bytes_accessed=0, transcendentals=0)


def shards(
    sources, row_basis, col_basis, up_transfer, down_transfer, near_blocks, near_list,
    far_blocks, far_list, upper_blocks, upper_list, root_blocks, root_list, group_blocks, group_list,
):
    in_hbm = functools.partial(pltpu.with_memory_space_constraint, memory_space=pltpu.HBM)
    up_sources, row_basis, up_transfer = map(in_hbm, (sources, row_basis, up_transfer))
    upper_blocks, upper_list, root_blocks, root_list = map(
        in_hbm, (upper_blocks, upper_list, root_blocks, root_list)
    )
    near_list, far_list = near_list.T, far_list.T
    leaves, columns, size = sources.shape
    nodes = up_transfer.shape[0]
    far_slots, far_nodes = far_list.shape
    near_slots = near_list.shape[0]
    groups = lax.axis_size("leaf")
    subs = lax.axis_size("sub")
    devices = groups * subs
    row = (columns, size)

    def shape(*lead):
        return jax.ShapeDtypeStruct(lead + row, F32)

    def buffer(count):
        return pltpu.VMEM((count, size, size), BF16)

    def plane(*lead):
        return pltpu.VMEM(lead + row, F32)

    def copies(count):
        return pltpu.SemaphoreType.DMA((count,))

    def call(kernel, name, us, outs, operands, specs, scratch, out_specs=None, **options):
        return pl.pallas_call(
            kernel,
            out_shape=outs,
            in_specs=specs,
            out_specs=out_specs or jax.tree.map(lambda _: VMEM, outs),
            scratch_shapes=scratch,
            compiler_params=PARAMS,
            cost_estimate=cost(us),
            name=name,
            **options,
        )(*operands)

    accumulators = lambda count: [plane(3 * count + 1)] * REPLICAS

    def permuted(x, axis, target):
        count = lax.axis_size(axis)
        return lax.ppermute(x, axis, [(i, target(i)) for i in range(count)])

    def gathered(x):
        return [x] + [permuted(x, "sub", lambda i, s=s: i ^ s) for s in SUB_ORDER]

    def exchanged(parts, unit):
        return (parts[0],) + tuple(permuted(parts[s], "leaf", lambda i, s=s: i ^ (s * unit)) for s in PLANE_ORDER)

    coef, group, top = call(
        up_kernel, "upward", 4, (shape(nodes), shape(), shape(TOP_TERMS + 1)),
        (up_sources, upper_list, root_list, row_basis, up_transfer, upper_blocks, root_blocks),
        [ANY] * 7,
        [
            pltpu.VMEM((leaves,) + row, BF16),
            pltpu.VMEM(upper_list.shape, jnp.int32), pltpu.VMEM(root_list.shape, jnp.int32),
            buffer(leaves), buffer(nodes), buffer(UPPER_TERMS), buffer(ROOT_TERMS), copies(14),
        ],
    )
    group_parts = gathered(group)
    far_prev, far_own, far_next = call(
        functools.partial(far_kernel, leaves), "far", 4, (shape(far_nodes),) * 3,
        (coef, far_list, far_blocks, group),
        [VMEM, ANY, VMEM, ANY],
        [pltpu.SMEM((far_slots, far_nodes), jnp.int32)] + accumulators(far_nodes) + [copies(1)],
    )
    terms = call(
        group_kernel, "group", 1, shape(TERMS + 1), (*group_parts, top, group_list, group_blocks),
        [VMEM] * 7, [],
    )
    term_parts = gathered(terms)
    to_prev, own, to_next = call(
        near_kernel, "near", 4, (shape(leaves + far_nodes),) * 3,
        (sources, near_list, near_blocks, far_prev, far_own, far_next, terms),
        [VMEM, ANY, VMEM, VMEM, VMEM, VMEM, ANY],
        [pltpu.SMEM((near_slots, leaves), jnp.int32)] + accumulators(leaves) + [copies(1)],
    )
    half = groups // 2 * 4
    window = shape(leaves + far_nodes)
    everyone = ("leaf", "sub")
    from_prev = permuted(to_next, everyone, lambda i: (i + 1) % devices)
    total = call(merge_kernel, "merge", 4, window, (own, from_prev), [VMEM] * 2, [])
    keep, send = call(
        pack_kernel, "pack", 0, (shape(half), shape(half)), (*term_parts, own), [VMEM] * 4 + [ANY],
        [pltpu.SMEM((subs,) + row, F32)] + [plane(2 * half + 1)] * 4 + [copies(subs)],
    )
    from_core = permuted(send, "leaf", lambda i: i ^ 1)
    y_unit, z_unit = groups // 4, groups // 16
    *by_y, to_prev = call(
        functools.partial(split_kernel, y_unit, 1), "split_y", 1, (shape(half // 4),) * 4 + (window,),
        (keep, from_core, to_prev), [VMEM] * 2 + [ANY], [],
        out_specs=(VMEM,) * 4 + (ANY,), input_output_aliases={2: 4},
    )
    from_next = permuted(to_prev, everyone, lambda i: (i - 1) % devices)
    by_z = call(
        functools.partial(split_kernel, z_unit, 0), "split_z", 1, (shape(half // 16),) * 4,
        exchanged(by_y, y_unit), [VMEM] * 4, [],
    )
    return call(
        down_kernel, "downward", 0, shape(leaves),
        (*exchanged(by_z, z_unit), total, from_next, down_transfer, col_basis), [VMEM] * 8, [plane(nodes)],
    )


def solution(mesh):
    blocks = P(("leaf", "sub"), None, None)
    lists = P(("leaf", "sub"), None)
    in_specs = (
        blocks, blocks, blocks, blocks, blocks, blocks, lists,
        blocks, lists, blocks, lists, blocks, lists, blocks, lists,
    )
    return jax.shard_map(shards, mesh=mesh, in_specs=in_specs, out_specs=blocks, check_vma=False)
```

```python
import functools

import jax
import jax.numpy as jnp
from jax import lax
from jax.experimental import pallas as pl
from jax.experimental.pallas import tpu as pltpu
from jax.sharding import PartitionSpec as P

F32 = jnp.float32
BF16 = jnp.bfloat16
ANY = pl.BlockSpec(memory_space=pl.ANY)
VMEM = pl.BlockSpec(memory_space=pltpu.VMEM)
REPLICAS = 4
UPPER_TERMS, ROOT_TERMS, GROUP_TERMS = 8, 4, 4
TOP_TERMS = UPPER_TERMS + ROOT_TERMS
GROUP_ROW, ID_ROW, PAYLOAD = TOP_TERMS, TOP_TERMS + 1, TOP_TERMS + 2


def rounded(x):
    return x.astype(BF16).astype(F32)


def dot(x, w):
    return jnp.dot(x.astype(BF16), w, preferred_element_type=F32)


def square(w00, w01, w10, w11):
    top = jnp.concatenate([w00, w01], axis=1)
    return jnp.concatenate([top, jnp.concatenate([w10, w11], axis=1)], axis=0)


def diagonal(x, y):
    zero = jnp.zeros_like(x)
    top = jnp.concatenate([x, zero], axis=1)
    return jnp.concatenate([top, jnp.concatenate([zero, y], axis=1)], axis=0)


def quad(xs, ws):
    left = jnp.concatenate([diagonal(xs[0], xs[1]), diagonal(xs[2], xs[3])], axis=0)
    out = dot(left, square(ws[0], ws[2], ws[1], ws[3]))
    n, m = xs[0].shape
    return [out[:n, :m], out[n : 2 * n, :m], out[2 * n : 3 * n, m:], out[3 * n :, m:]]


def exact_parts(x):
    high = rounded(x)
    rest = x - high
    middle = rounded(rest)
    return jnp.concatenate([high, middle, rest - middle], axis=0)


def exact_dot(parts, w):
    n = parts.shape[0] // 3
    out = dot(parts, w)
    return (out[2 * n :] + out[n : 2 * n]) + out[:n]


def level_offset(leaves, level):
    return 2 * leaves - 2 * (leaves >> level)


class Fetches:
    def __init__(self, sem):
        self.sem, self.count = sem, 0

    def __call__(self, src, dst):
        copy = pltpu.make_async_copy(src, dst, self.sem.at[self.count])
        copy.start()
        self.count += 1
        return copy

    def rows(self, src, dst, start, size):
        return self(src.at[pl.ds(start, size)], dst.at[pl.ds(start, size)])


def up_kernel(
    src_hbm, upper_list_hbm, root_list_hbm, group_list_hbm, rb_hbm, up_hbm, ub_hbm, rt_hbm,
    coef_ref, top_ref, src, upper_list, root_list, group_list, rb, up, ub, rt, sem,
):
    leaves = src.shape[0]
    levels = leaves.bit_length() - 1
    quarter = leaves // 4
    fetch = Fetches(sem)
    src_copy = fetch(src_hbm, src)
    rb_copies = [fetch.rows(rb_hbm, rb, i * quarter, quarter) for i in range(4)]
    up_copies = [fetch.rows(up_hbm, up, i * quarter, quarter) for i in range(4)]
    rest = [fetch.rows(up_hbm, up, leaves, leaves // 2), fetch.rows(up_hbm, up, leaves + leaves // 2, leaves // 2 - 1)]
    tail = [
        fetch(ub_hbm, ub), fetch(rt_hbm, rt),
        fetch(upper_list_hbm, upper_list), fetch(root_list_hbm, root_list), fetch(group_list_hbm, group_list),
    ]

    src_copy.wait()
    for t in range(0, leaves, 4):
        if t % quarter == 0:
            rb_copies[t // quarter].wait()
        span = range(t, t + 4)
        outs = quad([src[i].astype(F32) for i in span], [rb[i] for i in span])
        for i, out in zip(span, outs):
            coef_ref[i] = rounded(out)
    for level in range(levels):
        width = leaves >> level
        offset = level_offset(leaves, level)
        if level in (1, 2):
            rest[level - 1].wait()
        for t in range(0, width, 4):
            if level == 0 and t % quarter == 0:
                up_copies[t // quarter].wait()
            a = offset + t
            parent = offset + width + t // 2
            c = [coef_ref[a + i] for i in range(min(4, width))]
            if width == 2:
                left = jnp.concatenate(c, axis=1)
                out = dot(left, jnp.concatenate([up[a], up[a + 1]], axis=0))
                coef_ref[parent] = rounded(out)
            else:
                left = jnp.concatenate(
                    [jnp.concatenate(c[:2], axis=1), jnp.concatenate(c[2:], axis=1)], axis=0
                )
                out = dot(left, square(up[a], up[a + 2], up[a + 1], up[a + 3]))
                n, m = c[0].shape
                coef_ref[parent] = rounded(out[:n, :m])
                coef_ref[parent + 1] = rounded(out[n:, m:])
    top = 2 * leaves - 2
    top_ref[GROUP_ROW] = dot(coef_ref[top], up[top])
    for c in tail:
        c.wait()
    n, m = src.shape[1:]
    left = diagonal(coef_ref[top - 2], coef_ref[top - 1])
    for k in range(0, 4, 2):
        out = dot(left, square(ub[k], ub[k + 1], ub[4 + k], ub[5 + k]))
        top_ref[k] = out[:n, :m]
        top_ref[k + 1] = out[:n, m:]
        top_ref[4 + k] = out[n:, :m]
        top_ref[5 + k] = out[n:, m:]
    for k in range(0, ROOT_TERMS, 2):
        out = dot(coef_ref[top], jnp.concatenate([rt[k], rt[k + 1]], axis=1))
        top_ref[UPPER_TERMS + k] = out[:, :m]
        top_ref[UPPER_TERMS + k + 1] = out[:, m:]
    top_ref[ID_ROW] = jnp.zeros((n, m), F32)
    top_ref[ID_ROW, 0:2, 0:4] = upper_list[...].astype(F32)
    top_ref[ID_ROW, 2:3, 0:4] = root_list[...].astype(F32)
    top_ref[ID_ROW, 3:4, 0:4] = group_list[...].astype(F32)


def scatter_steps(left_of, mats, target_of, accs, slots, first, count, step, level, levels, start, span):
    own_index = lax.axis_index("leaf") * lax.axis_size("sub") + lax.axis_index("sub")
    shift = levels - level
    base = (own_index - 1) * (1 << shift)

    def add(replica, target, term):
        place = target - base
        row = lax.shift_right_arithmetic(place, shift) * span + start + (place & ((1 << shift) - 1))
        row = jnp.where(target >= 0, row, 3 * span)
        accs[replica][row] = accs[replica][row] + term

    def body(c, carry):
        for i in range(0, step, 2):
            t = c * step + i
            x, y = left_of(t), left_of(t + 1)
            n, m = x.shape
            left = diagonal(x, y)
            a, b = t * slots, (t + 1) * slots
            for k in range(0, slots, 2):
                out = dot(left, square(mats[a + k], mats[a + k + 1], mats[b + k], mats[b + k + 1]))
                add(0, target_of(t, k), out[:n, :m])
                add(1, target_of(t, k + 1), out[:n, m:])
                add(2, target_of(t + 1, k), out[n:, :m])
                add(3, target_of(t + 1, k + 1), out[n:, m:])
        return carry

    lax.fori_loop(first // step, (first + count) // step, body, 0)


def store_totals(accs, span, refs):
    for i, ref in enumerate(refs):
        parts = [acc[pl.ds(i * span, span)] for acc in accs]
        ref[0:span] = (parts[0] + parts[1]) + (parts[2] + parts[3])


def near_kernel(
    src_ref, list_hbm, near, far_prev, far_own, far_next, order,
    prev_ref, own_ref, next_ref, near_list, a0, a1, a2, a3, sem,
):
    leaves = src_ref.shape[0]
    slots = near_list.shape[0]
    fetch = Fetches(sem)
    first = fetch(list_hbm, near_list)
    accs = (a0, a1, a2, a3)
    for acc in accs:
        acc[...] = jnp.zeros(acc.shape, F32)
    for out, part in ((prev_ref, far_prev), (own_ref, far_own), (next_ref, far_next)):
        out[leaves:] = part[...]
    first.wait()
    scatter_steps(
        lambda t: src_ref[t].astype(F32), near, lambda t, k: near_list[k, t], accs,
        slots, 0, leaves, 8, 0, leaves.bit_length() - 1, 0, leaves,
    )
    store_totals(accs, leaves, (prev_ref, own_ref, next_ref))


def far_kernel(
    leaves, coef_ref, list_hbm, far, order, prev_ref, own_ref, next_ref, far_list, a0, a1, a2, a3, sem,
):
    levels = leaves.bit_length() - 1
    slots, nodes = far_list.shape
    fetch = Fetches(sem)
    first = fetch(list_hbm, far_list)
    accs = (a0, a1, a2, a3)
    for acc in accs:
        acc[...] = jnp.zeros(acc.shape, F32)
    first.wait()
    for level in range(levels - 1):
        offset = level_offset(leaves, level)
        scatter_steps(
            lambda t: coef_ref[t], far, lambda t, k: far_list[k, t], accs,
            slots, offset, leaves >> level, min(16, leaves >> level), level, levels, offset, nodes,
        )
    store_totals(accs, nodes, (prev_ref, own_ref, next_ref))


def group_kernel(p0, p1, p2, p3, blocks, out_ref):
    coef = (p0[GROUP_ROW] + p1[GROUP_ROW]) + (p2[GROUP_ROW] + p3[GROUP_ROW])
    parts = exact_parts(coef)
    m = coef.shape[1]
    for k in range(0, GROUP_TERMS, 2):
        out = exact_dot(parts, jnp.concatenate([blocks[k], blocks[k + 1]], axis=1))
        out_ref[k] = out[:, :m]
        out_ref[k + 1] = out[:, m:]


def pack_kernel(p0, p1, p2, p3, g0, g1, g2, g3, order, keep_ref, send_ref, ids, a0, a1, a2, a3, sem):
    half = keep_ref.shape[0]
    parts = (p0, p1, p2, p3)
    accs = (a0, a1, a2, a3)
    copies = [pltpu.make_async_copy(p.at[ID_ROW], ids.at[i], sem.at[i]) for i, p in enumerate(parts)]
    for c in copies:
        c.start()
    for acc in accs:
        acc[...] = jnp.zeros(acc.shape, F32)
    own_sub = lax.axis_index("sub")
    own_core = lax.axis_index("leaf") & 1
    for c in copies:
        c.wait()

    def place(leaf, entry):
        return (leaf & 1) * half + lax.shift_right_arithmetic(leaf, 1) * 4 + entry

    def add(acc, root, entry, term):
        row = place(lax.shift_right_arithmetic(root, 2), entry)
        row = jnp.where((root & 3) == own_sub, row, 2 * half)
        acc[row] = acc[row] + term

    for j in range(UPPER_TERMS):
        for i, (p, acc) in enumerate(zip(parts, accs)):
            node = ids[i, j // 4, j % 4].astype(jnp.int32)
            add(acc, lax.shift_right_arithmetic(node, 1), node & 1, p[j])
    for j in range(ROOT_TERMS):
        for i, (p, acc) in enumerate(zip(parts, accs)):
            root = ids[i, 2, j].astype(jnp.int32)
            add(acc, root, 2, p[UPPER_TERMS + j])
    for j in range(GROUP_TERMS):
        for i, (g, acc) in enumerate(zip((g0, g1, g2, g3), accs)):
            row = place(ids[i, 3, j].astype(jnp.int32), 3)
            acc[row] = acc[row] + g[j]

    def total(first):
        part = pl.ds(first, half)
        return (a0[part] + a1[part]) + (a2[part] + a3[part])

    keep_ref[...] = total(own_core * half)
    send_ref[...] = total((1 - own_core) * half)


def core_kernel(keep_ref, core_ref, out_ref):
    out_ref[...] = (keep_ref[...] + core_ref[...]).reshape(out_ref.shape)


def down_kernel(top, own, from_prev, from_next, down, col_hbm, out_ref, col, level_down, sem):
    leaves = out_ref.shape[0]
    levels = leaves.bit_length() - 1
    quarter = leaves // 4
    n, m = out_ref.shape[1:]
    fetch = Fetches(sem)
    col_copies = [fetch.rows(col_hbm, col, i * quarter, quarter) for i in range(4)]

    def total(i):
        return (own[i] + from_prev[i]) + from_next[i]

    fields = top[0]
    for i in range(1, top.shape[0]):
        fields = fields + top[i]
    root = 2 * leaves - 2
    level_down[root] = rounded(fields[2] + exact_dot(exact_parts(fields[3]), down[root]))
    out = dot(level_down[root], jnp.concatenate([down[root - 2], down[root - 1]], axis=1))
    level_down[root - 2] = rounded(fields[0] + out[:, :m])
    level_down[root - 1] = rounded(fields[1] + out[:, m:])
    for level in reversed(range(levels - 1)):
        width = leaves >> level
        offset = level_offset(leaves, level)
        for t in range(0, width, 4):
            a = offset + t
            parent = offset + width + t // 2
            left = diagonal(level_down[parent], level_down[parent + 1])
            out = dot(left, square(down[a], down[a + 1], down[a + 2], down[a + 3]))
            outs = (out[:n, :m], out[:n, m:], out[n:, :m], out[n:, m:])
            for i in range(4):
                level_down[a + i] = rounded(total(leaves + a + i) + outs[i])
    for t in range(0, leaves, 4):
        if t % quarter == 0:
            col_copies[t // quarter].wait()
        span = range(t, t + 4)
        outs = quad([level_down[i] for i in span], [col[i] for i in span])
        for i, out in zip(span, outs):
            out_ref[i] = total(i) + out


PARAMS = pltpu.CompilerParams(vmem_limit_bytes=24 * 1024 * 1024)


def cost(us):
    return pl.CostEstimate(flops=int(us * 1e9), bytes_accessed=0, transcendentals=0)


def shards(
    sources, row_basis, col_basis, up_transfer, down_transfer, near_blocks, near_list,
    far_blocks, far_list, upper_blocks, upper_list, root_blocks, root_list, group_blocks, group_list,
):
    in_hbm = functools.partial(pltpu.with_memory_space_constraint, memory_space=pltpu.HBM)
    up_sources, row_basis, up_transfer, col_basis = map(in_hbm, (sources, row_basis, up_transfer, col_basis))
    upper_blocks, upper_list, root_blocks, root_list, group_list = map(
        in_hbm, (upper_blocks, upper_list, root_blocks, root_list, group_list)
    )
    near_list, far_list = near_list.T, far_list.T
    leaves, columns, size = sources.shape
    nodes = up_transfer.shape[0]
    far_slots, far_nodes = far_list.shape
    near_slots = near_list.shape[0]
    groups = lax.axis_size("leaf")
    subs = lax.axis_size("sub")
    devices = groups * subs
    row = (columns, size)

    def shape(*lead):
        return jax.ShapeDtypeStruct(lead + row, F32)

    def buffer(count):
        return pltpu.VMEM((count, size, size), BF16)

    def plane(*lead):
        return pltpu.VMEM(lead + row, F32)

    def copies(count):
        return pltpu.SemaphoreType.DMA((count,))

    def call(kernel, name, us, outs, operands, specs, scratch, out_specs=None, **options):
        return pl.pallas_call(
            kernel,
            out_shape=outs,
            in_specs=specs,
            out_specs=out_specs or jax.tree.map(lambda _: VMEM, outs),
            scratch_shapes=scratch,
            compiler_params=PARAMS,
            cost_estimate=cost(us),
            name=name,
            **options,
        )(*operands)

    accumulators = lambda count: [plane(3 * count + 1)] * REPLICAS

    def permuted(x, axis, target):
        count = lax.axis_size(axis)
        return lax.ppermute(x, axis, [(i, target(i)) for i in range(count)])

    def gathered(x):
        return [x] + [permuted(x, "sub", lambda i, s=s: i ^ s) for s in (2, 1, 3)]

    coef, top = call(
        up_kernel, "upward", 4, (shape(nodes), shape(PAYLOAD)),
        (up_sources, upper_list, root_list, group_list, row_basis, up_transfer, upper_blocks, root_blocks),
        [ANY] * 8,
        [
            pltpu.VMEM((leaves,) + row, BF16),
            pltpu.VMEM(upper_list.shape, jnp.int32), pltpu.VMEM(root_list.shape, jnp.int32),
            pltpu.VMEM(group_list.shape, jnp.int32),
            buffer(leaves), buffer(nodes), buffer(UPPER_TERMS), buffer(ROOT_TERMS), copies(16),
        ],
    )
    top_parts = gathered(top)
    far_prev, far_own, far_next = call(
        functools.partial(far_kernel, leaves), "far", 4, (shape(far_nodes),) * 3,
        (coef, far_list, far_blocks, top),
        [VMEM, ANY, VMEM, ANY],
        [pltpu.SMEM((far_slots, far_nodes), jnp.int32)] + accumulators(far_nodes) + [copies(1)],
    )
    terms = call(
        group_kernel, "group", 1, shape(GROUP_TERMS), (*top_parts, group_blocks), [VMEM] * 5, []
    )
    term_parts = gathered(terms)
    to_prev, own, to_next = call(
        near_kernel, "near", 4, (shape(leaves + far_nodes),) * 3,
        (sources, near_list, near_blocks, far_prev, far_own, far_next, terms),
        [VMEM, ANY, VMEM, VMEM, VMEM, VMEM, ANY],
        [pltpu.SMEM((near_slots, leaves), jnp.int32)] + accumulators(leaves) + [copies(1)],
    )
    half = groups // 2 * 4
    everyone = ("leaf", "sub")
    from_prev = permuted(to_next, everyone, lambda i: (i + 1) % devices)
    from_next = permuted(to_prev, everyone, lambda i: (i - 1) % devices)

    keep, send = call(
        pack_kernel, "pack", 0, (shape(half), shape(half)), (*top_parts, *term_parts, own), [VMEM] * 8 + [ANY],
        [pltpu.SMEM((subs,) + row, F32)] + [plane(2 * half + 1)] * 4 + [copies(subs)],
    )
    from_core = permuted(send, "leaf", lambda i: i ^ 1)
    planes = call(core_kernel, "core", 0, shape(groups // 2, 4), (keep, from_core), [VMEM] * 2, [])
    fields = lax.all_to_all(
        planes, "leaf", 0, 0, tiled=True, axis_index_groups=[list(range(c, groups, 2)) for c in range(2)]
    )
    return call(
        down_kernel, "downward", 0, shape(leaves), (fields, own, from_prev, from_next, down_transfer, col_basis), [VMEM] * 5 + [ANY],
        [buffer(leaves), plane(nodes), copies(4)],
    )


def solution(mesh):
    blocks = P(("leaf", "sub"), None, None)
    lists = P(("leaf", "sub"), None)
    in_specs = (
        blocks, blocks, blocks, blocks, blocks, blocks, lists,
        blocks, lists, blocks, lists, blocks, lists, blocks, lists,
    )
    return jax.shard_map(shards, mesh=mesh, in_specs=in_specs, out_specs=blocks, check_vma=False)
```

```python
import functools

import jax
import jax.numpy as jnp
from jax import lax
from jax.experimental import pallas as pl
from jax.experimental.pallas import tpu as pltpu
from jax.sharding import PartitionSpec as P

F32 = jnp.float32
BF16 = jnp.bfloat16
ANY = pl.BlockSpec(memory_space=pl.ANY)
VMEM = pl.BlockSpec(memory_space=pltpu.VMEM)
REPLICAS = 4
UPPER_TERMS, ROOT_TERMS, GROUP_TERMS = 8, 4, 4
TOP_TERMS = UPPER_TERMS + ROOT_TERMS
GROUP_ROW, ID_ROW, PAYLOAD = TOP_TERMS, TOP_TERMS + 1, TOP_TERMS + 2


def rounded(x):
    return x.astype(BF16).astype(F32)


def dot(x, w):
    return jnp.dot(x.astype(BF16), w, preferred_element_type=F32)


def square(w00, w01, w10, w11):
    top = jnp.concatenate([w00, w01], axis=1)
    return jnp.concatenate([top, jnp.concatenate([w10, w11], axis=1)], axis=0)


def diagonal(x, y):
    zero = jnp.zeros_like(x)
    top = jnp.concatenate([x, zero], axis=1)
    return jnp.concatenate([top, jnp.concatenate([zero, y], axis=1)], axis=0)


def quad(xs, ws):
    left = jnp.concatenate([diagonal(xs[0], xs[1]), diagonal(xs[2], xs[3])], axis=0)
    out = dot(left, square(ws[0], ws[2], ws[1], ws[3]))
    n, m = xs[0].shape
    return [out[:n, :m], out[n : 2 * n, :m], out[2 * n : 3 * n, m:], out[3 * n :, m:]]


def exact_parts(x):
    high = rounded(x)
    rest = x - high
    middle = rounded(rest)
    return jnp.concatenate([high, middle, rest - middle], axis=0)


def exact_dot(parts, w):
    n = parts.shape[0] // 3
    out = dot(parts, w)
    return (out[2 * n :] + out[n : 2 * n]) + out[:n]


def level_offset(leaves, level):
    return 2 * leaves - 2 * (leaves >> level)


class Fetches:
    def __init__(self, sem):
        self.sem, self.count = sem, 0

    def __call__(self, src, dst):
        copy = pltpu.make_async_copy(src, dst, self.sem.at[self.count])
        copy.start()
        self.count += 1
        return copy

    def rows(self, src, dst, start, size):
        return self(src.at[pl.ds(start, size)], dst.at[pl.ds(start, size)])


def up_kernel(
    src_hbm, upper_list_hbm, root_list_hbm, group_list_hbm, rb_hbm, up_hbm, ub_hbm, rt_hbm,
    coef_ref, top_ref, src, upper_list, root_list, group_list, rb, up, ub, rt, sem,
):
    leaves = src.shape[0]
    levels = leaves.bit_length() - 1
    quarter = leaves // 4
    fetch = Fetches(sem)
    src_copy = fetch(src_hbm, src)
    rb_copies = [fetch.rows(rb_hbm, rb, i * quarter, quarter) for i in range(4)]
    up_copies = [fetch.rows(up_hbm, up, i * quarter, quarter) for i in range(4)]
    rest = [fetch.rows(up_hbm, up, leaves, leaves // 2), fetch.rows(up_hbm, up, leaves + leaves // 2, leaves // 2 - 1)]
    tail = [
        fetch(ub_hbm, ub), fetch(rt_hbm, rt),
        fetch(upper_list_hbm, upper_list), fetch(root_list_hbm, root_list), fetch(group_list_hbm, group_list),
    ]

    src_copy.wait()
    for t in range(0, leaves, 4):
        if t % quarter == 0:
            rb_copies[t // quarter].wait()
        span = range(t, t + 4)
        outs = quad([src[i].astype(F32) for i in span], [rb[i] for i in span])
        for i, out in zip(span, outs):
            coef_ref[i] = rounded(out)
    for level in range(levels):
        width = leaves >> level
        offset = level_offset(leaves, level)
        if level in (1, 2):
            rest[level - 1].wait()
        for t in range(0, width, 4):
            if level == 0 and t % quarter == 0:
                up_copies[t // quarter].wait()
            a = offset + t
            parent = offset + width + t // 2
            c = [coef_ref[a + i] for i in range(min(4, width))]
            if width == 2:
                left = jnp.concatenate(c, axis=1)
                out = dot(left, jnp.concatenate([up[a], up[a + 1]], axis=0))
                coef_ref[parent] = rounded(out)
            else:
                left = jnp.concatenate(
                    [jnp.concatenate(c[:2], axis=1), jnp.concatenate(c[2:], axis=1)], axis=0
                )
                out = dot(left, square(up[a], up[a + 2], up[a + 1], up[a + 3]))
                n, m = c[0].shape
                coef_ref[parent] = rounded(out[:n, :m])
                coef_ref[parent + 1] = rounded(out[n:, m:])
    top = 2 * leaves - 2
    top_ref[GROUP_ROW] = dot(coef_ref[top], up[top])
    for c in tail:
        c.wait()
    n, m = src.shape[1:]
    left = diagonal(coef_ref[top - 2], coef_ref[top - 1])
    for k in range(0, 4, 2):
        out = dot(left, square(ub[k], ub[k + 1], ub[4 + k], ub[5 + k]))
        top_ref[k] = out[:n, :m]
        top_ref[k + 1] = out[:n, m:]
        top_ref[4 + k] = out[n:, :m]
        top_ref[5 + k] = out[n:, m:]
    for k in range(0, ROOT_TERMS, 2):
        out = dot(coef_ref[top], jnp.concatenate([rt[k], rt[k + 1]], axis=1))
        top_ref[UPPER_TERMS + k] = out[:, :m]
        top_ref[UPPER_TERMS + k + 1] = out[:, m:]
    top_ref[ID_ROW] = jnp.zeros((n, m), F32)
    top_ref[ID_ROW, 0:2, 0:4] = upper_list[...].astype(F32)
    top_ref[ID_ROW, 2:3, 0:4] = root_list[...].astype(F32)
    top_ref[ID_ROW, 3:4, 0:4] = group_list[...].astype(F32)


def scatter_steps(left_of, mats, target_of, accs, slots, first, count, step, level, levels, start, span):
    own_index = lax.axis_index("leaf") * lax.axis_size("sub") + lax.axis_index("sub")
    shift = levels - level
    base = (own_index - 1) * (1 << shift)

    def add(replica, target, term):
        place = target - base
        row = lax.shift_right_arithmetic(place, shift) * span + start + (place & ((1 << shift) - 1))
        row = jnp.where(target >= 0, row, 3 * span)
        accs[replica][row] = accs[replica][row] + term

    def body(c, carry):
        for i in range(0, step, 2):
            t = c * step + i
            x, y = left_of(t), left_of(t + 1)
            n, m = x.shape
            left = diagonal(x, y)
            a, b = t * slots, (t + 1) * slots
            for k in range(0, slots, 2):
                out = dot(left, square(mats[a + k], mats[a + k + 1], mats[b + k], mats[b + k + 1]))
                add(0, target_of(t, k), out[:n, :m])
                add(1, target_of(t, k + 1), out[:n, m:])
                add(2, target_of(t + 1, k), out[n:, :m])
                add(3, target_of(t + 1, k + 1), out[n:, m:])
        return carry

    lax.fori_loop(first // step, (first + count) // step, body, 0)


def store_totals(accs, span, refs):
    for i, ref in enumerate(refs):
        parts = [acc[pl.ds(i * span, span)] for acc in accs]
        ref[0:span] = (parts[0] + parts[1]) + (parts[2] + parts[3])


def near_kernel(
    src_ref, list_hbm, near, far_prev, order, prev_ref, own_ref, next_ref, near_list, a0, a1, a2, a3, sem,
):
    leaves = src_ref.shape[0]
    slots = near_list.shape[0]
    fetch = Fetches(sem)
    first = fetch(list_hbm, near_list)
    accs = (a0, a1, a2, a3)
    for acc in accs:
        acc[...] = jnp.zeros(acc.shape, F32)
    prev_ref[leaves:] = far_prev[...]
    first.wait()
    scatter_steps(
        lambda t: src_ref[t].astype(F32), near, lambda t, k: near_list[k, t], accs,
        slots, 0, leaves, 8, 0, leaves.bit_length() - 1, 0, leaves,
    )
    store_totals(accs, leaves, (prev_ref, own_ref, next_ref))


def far_kernel(
    leaves, coef_ref, list_hbm, far, order, prev_ref, own_ref, next_ref, far_list, a0, a1, a2, a3, sem,
):
    levels = leaves.bit_length() - 1
    slots, nodes = far_list.shape
    fetch = Fetches(sem)
    first = fetch(list_hbm, far_list)
    accs = (a0, a1, a2, a3)
    for acc in accs:
        acc[...] = jnp.zeros(acc.shape, F32)
    first.wait()
    for level in range(levels - 1):
        offset = level_offset(leaves, level)
        scatter_steps(
            lambda t: coef_ref[t], far, lambda t, k: far_list[k, t], accs,
            slots, offset, leaves >> level, min(16, leaves >> level), level, levels, offset, nodes,
        )
    store_totals(accs, nodes, (prev_ref, own_ref, next_ref))


def group_kernel(p0, p1, p2, p3, blocks, out_ref):
    coef = (p0[GROUP_ROW] + p1[GROUP_ROW]) + (p2[GROUP_ROW] + p3[GROUP_ROW])
    parts = exact_parts(coef)
    m = coef.shape[1]
    for k in range(0, GROUP_TERMS, 2):
        out = exact_dot(parts, jnp.concatenate([blocks[k], blocks[k + 1]], axis=1))
        out_ref[k] = out[:, :m]
        out_ref[k + 1] = out[:, m:]


def pack_kernel(p0, p1, p2, p3, g0, g1, g2, g3, order, arrived, keep_ref, send_ref, ids, a0, a1, a2, a3, sem):
    half = keep_ref.shape[0]
    parts = (p0, p1, p2, p3)
    accs = (a0, a1, a2, a3)
    copies = [pltpu.make_async_copy(p.at[ID_ROW], ids.at[i], sem.at[i]) for i, p in enumerate(parts)]
    for c in copies:
        c.start()
    for acc in accs:
        acc[...] = jnp.zeros(acc.shape, F32)
    own_sub = lax.axis_index("sub")
    own_core = lax.axis_index("leaf") & 1
    for c in copies:
        c.wait()

    def place(leaf, entry):
        return (leaf & 1) * half + lax.shift_right_arithmetic(leaf, 1) * 4 + entry

    def add(acc, root, entry, term):
        row = place(lax.shift_right_arithmetic(root, 2), entry)
        row = jnp.where((root & 3) == own_sub, row, 2 * half)
        acc[row] = acc[row] + term

    for j in range(UPPER_TERMS):
        for i, (p, acc) in enumerate(zip(parts, accs)):
            node = ids[i, j // 4, j % 4].astype(jnp.int32)
            add(acc, lax.shift_right_arithmetic(node, 1), node & 1, p[j])
    for j in range(ROOT_TERMS):
        for i, (p, acc) in enumerate(zip(parts, accs)):
            root = ids[i, 2, j].astype(jnp.int32)
            add(acc, root, 2, p[UPPER_TERMS + j])
    for j in range(GROUP_TERMS):
        for i, (g, acc) in enumerate(zip((g0, g1, g2, g3), accs)):
            row = place(ids[i, 3, j].astype(jnp.int32), 3)
            acc[row] = acc[row] + g[j]

    def total(first):
        part = pl.ds(first, half)
        return (a0[part] + a1[part]) + (a2[part] + a3[part])

    keep_ref[...] = total(own_core * half)
    send_ref[...] = total((1 - own_core) * half)


def core_kernel(keep_ref, core_ref, near_next, out_ref, held):
    out_ref[...] = (keep_ref[...] + core_ref[...]).reshape(out_ref.shape)


def down_kernel(
    top, far_own, far_from_prev, near_own, near_from_prev, from_next, down, col_hbm, out_ref, col, level_down, sem,
):
    leaves = out_ref.shape[0]
    levels = leaves.bit_length() - 1
    quarter = leaves // 4
    n, m = out_ref.shape[1:]
    fetch = Fetches(sem)
    col_copies = [fetch.rows(col_hbm, col, i * quarter, quarter) for i in range(4)]

    def far_total(i):
        return (far_own[i] + far_from_prev[i]) + from_next[leaves + i]

    fields = top[0]
    for i in range(1, top.shape[0]):
        fields = fields + top[i]
    root = 2 * leaves - 2
    level_down[root] = rounded(fields[2] + exact_dot(exact_parts(fields[3]), down[root]))
    out = dot(level_down[root], jnp.concatenate([down[root - 2], down[root - 1]], axis=1))
    level_down[root - 2] = rounded(fields[0] + out[:, :m])
    level_down[root - 1] = rounded(fields[1] + out[:, m:])
    for level in reversed(range(levels - 1)):
        width = leaves >> level
        offset = level_offset(leaves, level)
        for t in range(0, width, 4):
            a = offset + t
            parent = offset + width + t // 2
            left = diagonal(level_down[parent], level_down[parent + 1])
            out = dot(left, square(down[a], down[a + 1], down[a + 2], down[a + 3]))
            outs = (out[:n, :m], out[:n, m:], out[n:, :m], out[n:, m:])
            for i in range(4):
                level_down[a + i] = rounded(far_total(a + i) + outs[i])
    for t in range(0, leaves, 4):
        if t % quarter == 0:
            col_copies[t // quarter].wait()
        span = range(t, t + 4)
        outs = quad([level_down[i] for i in span], [col[i] for i in span])
        for i, out in zip(span, outs):
            out_ref[i] = ((near_own[i] + near_from_prev[i]) + from_next[i]) + out


PARAMS = pltpu.CompilerParams(vmem_limit_bytes=24 * 1024 * 1024)


def cost(us):
    return pl.CostEstimate(flops=int(us * 1e9), bytes_accessed=0, transcendentals=0)


def shards(
    sources, row_basis, col_basis, up_transfer, down_transfer, near_blocks, near_list,
    far_blocks, far_list, upper_blocks, upper_list, root_blocks, root_list, group_blocks, group_list,
):
    in_hbm = functools.partial(pltpu.with_memory_space_constraint, memory_space=pltpu.HBM)
    up_sources, row_basis, up_transfer, col_basis = map(in_hbm, (sources, row_basis, up_transfer, col_basis))
    upper_blocks, upper_list, root_blocks, root_list, group_list = map(
        in_hbm, (upper_blocks, upper_list, root_blocks, root_list, group_list)
    )
    near_list, far_list = near_list.T, far_list.T
    leaves, columns, size = sources.shape
    nodes = up_transfer.shape[0]
    far_slots, far_nodes = far_list.shape
    near_slots = near_list.shape[0]
    groups = lax.axis_size("leaf")
    subs = lax.axis_size("sub")
    devices = groups * subs
    row = (columns, size)

    def shape(*lead):
        return jax.ShapeDtypeStruct(lead + row, F32)

    def buffer(count):
        return pltpu.VMEM((count, size, size), BF16)

    def plane(*lead):
        return pltpu.VMEM(lead + row, F32)

    def copies(count):
        return pltpu.SemaphoreType.DMA((count,))

    def call(kernel, name, us, outs, operands, specs, scratch, out_specs=None, **options):
        return pl.pallas_call(
            kernel,
            out_shape=outs,
            in_specs=specs,
            out_specs=out_specs or jax.tree.map(lambda _: VMEM, outs),
            scratch_shapes=scratch,
            compiler_params=PARAMS,
            cost_estimate=cost(us),
            name=name,
            **options,
        )(*operands)

    accumulators = lambda count: [plane(3 * count + 1)] * REPLICAS

    def permuted(x, axis, target):
        count = lax.axis_size(axis)
        return lax.ppermute(x, axis, [(i, target(i)) for i in range(count)])

    def gathered(x):
        return [x] + [permuted(x, "sub", lambda i, s=s: i ^ s) for s in (3, 1, 2)]

    coef, top = call(
        up_kernel, "upward", 4, (shape(nodes), shape(PAYLOAD)),
        (up_sources, upper_list, root_list, group_list, row_basis, up_transfer, upper_blocks, root_blocks),
        [ANY] * 8,
        [
            pltpu.VMEM((leaves,) + row, BF16),
            pltpu.VMEM(upper_list.shape, jnp.int32), pltpu.VMEM(root_list.shape, jnp.int32),
            pltpu.VMEM(group_list.shape, jnp.int32),
            buffer(leaves), buffer(nodes), buffer(UPPER_TERMS), buffer(ROOT_TERMS), copies(16),
        ],
    )
    top_parts = gathered(top)
    far_prev, far_own, far_next = call(
        functools.partial(far_kernel, leaves), "far", 4, (shape(far_nodes),) * 3,
        (coef, far_list, far_blocks, top),
        [VMEM, ANY, VMEM, ANY],
        [pltpu.SMEM((far_slots, far_nodes), jnp.int32)] + accumulators(far_nodes) + [copies(1)],
    )
    terms = call(
        group_kernel, "group", 1, shape(GROUP_TERMS), (*top_parts, group_blocks), [VMEM] * 5, []
    )
    term_parts = gathered(terms)
    to_prev, near_own, near_next = call(
        near_kernel, "near", 4, (shape(leaves + far_nodes), shape(leaves), shape(leaves)),
        (sources, near_list, near_blocks, far_prev, terms), [VMEM, ANY, VMEM, VMEM, ANY],
        [pltpu.SMEM((near_slots, leaves), jnp.int32)] + accumulators(leaves) + [copies(1)],
    )
    half = groups // 2 * 4
    everyone = ("leaf", "sub")
    def ahead(x):
        return permuted(x, everyone, lambda i: (i + 1) % devices)

    def back(x):
        return permuted(x, everyone, lambda i: (i - 1) % devices)

    far_from_prev, from_next = ahead(far_next), back(to_prev)
    keep, send = call(
        pack_kernel, "pack", 10, (shape(half), shape(half)), (*top_parts, *term_parts, near_own, far_from_prev), [VMEM] * 8 + [ANY] * 2,
        [pltpu.SMEM((subs,) + row, F32)] + [plane(2 * half + 1)] * 4 + [copies(subs)],
    )
    from_core = permuted(send, "leaf", lambda i: i ^ 1)
    planes, near_next = call(
        core_kernel, "core", 10, (shape(groups // 2, 4), shape(leaves)), (keep, from_core, near_next),
        [VMEM] * 2 + [ANY], [], out_specs=(VMEM, ANY), input_output_aliases={2: 1},
    )
    near_from_prev = ahead(near_next)
    fields = lax.all_to_all(
        planes, "leaf", 0, 0, tiled=True, axis_index_groups=[list(range(c, groups, 2)) for c in range(2)]
    )
    return call(
        down_kernel, "downward", 0, shape(leaves), (fields, far_own, far_from_prev, near_own, near_from_prev, from_next, down_transfer, col_basis),
        [VMEM] * 7 + [ANY],
        [buffer(leaves), plane(nodes), copies(4)],
    )


def solution(mesh):
    blocks = P(("leaf", "sub"), None, None)
    lists = P(("leaf", "sub"), None)
    in_specs = (
        blocks, blocks, blocks, blocks, blocks, blocks, lists,
        blocks, lists, blocks, lists, blocks, lists, blocks, lists,
    )
    return jax.shard_map(shards, mesh=mesh, in_specs=in_specs, out_specs=blocks, check_vma=False)
```

```python
import functools

import jax
import jax.numpy as jnp
from jax import lax
from jax.experimental import pallas as pl
from jax.experimental.pallas import tpu as pltpu
from jax.sharding import PartitionSpec as P

F32 = jnp.float32
BF16 = jnp.bfloat16
ANY = pl.BlockSpec(memory_space=pl.ANY)
VMEM = pl.BlockSpec(memory_space=pltpu.VMEM)
REPLICAS = 4
UPPER_TERMS, ROOT_TERMS, GROUP_TERMS = 8, 4, 4
TOP_TERMS = UPPER_TERMS + ROOT_TERMS
TERMS = TOP_TERMS + GROUP_TERMS


def rounded(x):
    return x.astype(BF16).astype(F32)


def dot(x, w):
    return jnp.dot(x.astype(BF16), w, preferred_element_type=F32)


def square(w00, w01, w10, w11):
    top = jnp.concatenate([w00, w01], axis=1)
    return jnp.concatenate([top, jnp.concatenate([w10, w11], axis=1)], axis=0)


def diagonal(x, y):
    zero = jnp.zeros_like(x)
    top = jnp.concatenate([x, zero], axis=1)
    return jnp.concatenate([top, jnp.concatenate([zero, y], axis=1)], axis=0)


def quad(xs, ws):
    left = jnp.concatenate([diagonal(xs[0], xs[1]), diagonal(xs[2], xs[3])], axis=0)
    out = dot(left, square(ws[0], ws[2], ws[1], ws[3]))
    n, m = xs[0].shape
    return [out[:n, :m], out[n : 2 * n, :m], out[2 * n : 3 * n, m:], out[3 * n :, m:]]


def exact_parts(x):
    high = rounded(x)
    rest = x - high
    middle = rounded(rest)
    return jnp.concatenate([high, middle, rest - middle], axis=0)


def exact_dot(parts, w):
    n = parts.shape[0] // 3
    out = dot(parts, w)
    return (out[2 * n :] + out[n : 2 * n]) + out[:n]


def level_offset(leaves, level):
    return 2 * leaves - 2 * (leaves >> level)


class Fetches:
    def __init__(self, sem):
        self.sem, self.count = sem, 0

    def __call__(self, src, dst):
        copy = pltpu.make_async_copy(src, dst, self.sem.at[self.count])
        copy.start()
        self.count += 1
        return copy

    def rows(self, src, dst, start, size):
        return self(src.at[pl.ds(start, size)], dst.at[pl.ds(start, size)])


def up_kernel(
    src_hbm, upper_list_hbm, root_list_hbm, rb_hbm, up_hbm, ub_hbm, rt_hbm,
    coef_ref, group_ref, top_ref, src, upper_list, root_list, rb, up, ub, rt, sem,
):
    leaves = src.shape[0]
    levels = leaves.bit_length() - 1
    quarter = leaves // 4
    fetch = Fetches(sem)
    src_copy = fetch(src_hbm, src)
    rb_copies = [fetch.rows(rb_hbm, rb, i * quarter, quarter) for i in range(4)]
    up_copies = [fetch.rows(up_hbm, up, i * quarter, quarter) for i in range(4)]
    rest = fetch.rows(up_hbm, up, leaves, leaves - 1)
    tail = [
        fetch(ub_hbm, ub), fetch(rt_hbm, rt),
        fetch(upper_list_hbm, upper_list), fetch(root_list_hbm, root_list),
    ]

    src_copy.wait()
    for t in range(0, leaves, 4):
        if t % quarter == 0:
            rb_copies[t // quarter].wait()
        span = range(t, t + 4)
        outs = quad([src[i].astype(F32) for i in span], [rb[i] for i in span])
        for i, out in zip(span, outs):
            coef_ref[i] = rounded(out)
    for level in range(levels):
        width = leaves >> level
        offset = level_offset(leaves, level)
        if level == 1:
            rest.wait()
        for t in range(0, width, 4):
            if level == 0 and t % quarter == 0:
                up_copies[t // quarter].wait()
            a = offset + t
            parent = offset + width + t // 2
            c = [coef_ref[a + i] for i in range(min(4, width))]
            if width == 2:
                left = jnp.concatenate(c, axis=1)
                out = dot(left, jnp.concatenate([up[a], up[a + 1]], axis=0))
                coef_ref[parent] = rounded(out)
            else:
                left = jnp.concatenate(
                    [jnp.concatenate(c[:2], axis=1), jnp.concatenate(c[2:], axis=1)], axis=0
                )
                out = dot(left, square(up[a], up[a + 2], up[a + 1], up[a + 3]))
                n, m = c[0].shape
                coef_ref[parent] = rounded(out[:n, :m])
                coef_ref[parent + 1] = rounded(out[n:, m:])
    top = 2 * leaves - 2
    group_ref[...] = dot(coef_ref[top], up[top])
    for c in tail:
        c.wait()
    n, m = src.shape[1:]
    left = diagonal(coef_ref[top - 2], coef_ref[top - 1])
    for k in range(0, 4, 2):
        out = dot(left, square(ub[k], ub[k + 1], ub[4 + k], ub[5 + k]))
        top_ref[k] = out[:n, :m]
        top_ref[k + 1] = out[:n, m:]
        top_ref[4 + k] = out[n:, :m]
        top_ref[5 + k] = out[n:, m:]
    for k in range(0, ROOT_TERMS, 2):
        out = dot(coef_ref[top], jnp.concatenate([rt[k], rt[k + 1]], axis=1))
        top_ref[UPPER_TERMS + k] = out[:, :m]
        top_ref[UPPER_TERMS + k + 1] = out[:, m:]
    top_ref[TOP_TERMS] = jnp.zeros((n, m), F32)
    top_ref[TOP_TERMS, 0:2, 0:4] = upper_list[...].astype(F32)
    top_ref[TOP_TERMS, 2:3, 0:4] = root_list[...].astype(F32)


def scatter_steps(left_of, mats, target_of, accs, slots, first, count, step, level, levels, start, span):
    own_index = lax.axis_index("leaf") * lax.axis_size("sub") + lax.axis_index("sub")
    shift = levels - level
    base = (own_index - 1) * (1 << shift)

    def add(replica, target, term):
        place = target - base
        row = lax.shift_right_arithmetic(place, shift) * span + start + (place & ((1 << shift) - 1))
        row = jnp.where(target >= 0, row, 3 * span)
        accs[replica][row] = accs[replica][row] + term

    def body(c, carry):
        for i in range(0, step, 2):
            t = c * step + i
            x, y = left_of(t), left_of(t + 1)
            n, m = x.shape
            left = diagonal(x, y)
            a, b = t * slots, (t + 1) * slots
            for k in range(0, slots, 2):
                out = dot(left, square(mats[a + k], mats[a + k + 1], mats[b + k], mats[b + k + 1]))
                add(0, target_of(t, k), out[:n, :m])
                add(1, target_of(t, k + 1), out[:n, m:])
                add(2, target_of(t + 1, k), out[n:, :m])
                add(3, target_of(t + 1, k + 1), out[n:, m:])
        return carry

    lax.fori_loop(first // step, (first + count) // step, body, 0)


def store_totals(accs, span, refs):
    odd = lax.axis_index("sub") & 1
    for first, ref in zip((2 - 2 * odd, 1, 2 * odd), refs):
        parts = [acc[pl.ds(first * span, span)] for acc in accs]
        ref[0:span] = (parts[0] + parts[1]) + (parts[2] + parts[3])


def near_kernel(
    src_ref, list_hbm, near, far_a, far_own, far_b, order,
    a_ref, own_ref, b_ref, near_list, a0, a1, a2, a3, sem,
):
    leaves = src_ref.shape[0]
    slots = near_list.shape[0]
    fetch = Fetches(sem)
    first = fetch(list_hbm, near_list)
    accs = (a0, a1, a2, a3)
    for acc in accs:
        acc[...] = jnp.zeros(acc.shape, F32)
    for out, part in ((a_ref, far_a), (own_ref, far_own), (b_ref, far_b)):
        out[leaves:] = part[...]
    first.wait()
    scatter_steps(
        lambda t: src_ref[t].astype(F32), near, lambda t, k: near_list[k, t], accs,
        slots, 0, leaves, 8, 0, leaves.bit_length() - 1, 0, leaves,
    )
    store_totals(accs, leaves, (a_ref, own_ref, b_ref))


def far_kernel(
    leaves, coef_ref, list_hbm, far, order, a_ref, own_ref, b_ref, far_list, a0, a1, a2, a3, sem,
):
    levels = leaves.bit_length() - 1
    slots, nodes = far_list.shape
    fetch = Fetches(sem)
    first = fetch(list_hbm, far_list)
    accs = (a0, a1, a2, a3)
    for acc in accs:
        acc[...] = jnp.zeros(acc.shape, F32)
    first.wait()
    for level in range(levels - 1):
        offset = level_offset(leaves, level)
        scatter_steps(
            lambda t: coef_ref[t], far, lambda t, k: far_list[k, t], accs,
            slots, offset, leaves >> level, min(16, leaves >> level), level, levels, offset, nodes,
        )
    store_totals(accs, nodes, (a_ref, own_ref, b_ref))


def group_kernel(g0, g1, g2, g3, top_ref, group_list, blocks, out_ref):
    coef = (g0[...] + g1[...]) + (g2[...] + g3[...])
    parts = exact_parts(coef)
    m = coef.shape[1]
    for k in range(0, GROUP_TERMS, 2):
        out = exact_dot(parts, jnp.concatenate([blocks[k], blocks[k + 1]], axis=1))
        out_ref[TOP_TERMS + k] = out[:, :m]
        out_ref[TOP_TERMS + k + 1] = out[:, m:]
    out_ref[0:TOP_TERMS] = top_ref[0:TOP_TERMS]
    out_ref[TERMS] = top_ref[TOP_TERMS]
    out_ref[TERMS, 3:4, 0:4] = group_list[...].astype(F32)


def pack_kernel(p0, p1, p2, p3, order, keep_ref, send_ref, ids, a0, a1, a2, a3, sem):
    half = keep_ref.shape[0]
    parts = (p0, p1, p2, p3)
    accs = (a0, a1, a2, a3)
    copies = [pltpu.make_async_copy(p.at[TERMS], ids.at[i], sem.at[i]) for i, p in enumerate(parts)]
    for c in copies:
        c.start()
    for acc in accs:
        acc[...] = jnp.zeros(acc.shape, F32)
    own_sub = lax.axis_index("sub")
    own_core = lax.axis_index("leaf") & 1
    for c in copies:
        c.wait()

    def place(leaf, entry):
        return (leaf & 1) * half + lax.shift_right_arithmetic(leaf, 1) * 4 + entry

    def add(acc, root, entry, term):
        row = place(lax.shift_right_arithmetic(root, 2), entry)
        row = jnp.where((root & 3) == own_sub, row, 2 * half)
        acc[row] = acc[row] + term

    for j in range(UPPER_TERMS):
        for i, (p, acc) in enumerate(zip(parts, accs)):
            node = ids[i, j // 4, j % 4].astype(jnp.int32)
            add(acc, lax.shift_right_arithmetic(node, 1), node & 1, p[j])
    for j in range(ROOT_TERMS):
        for i, (p, acc) in enumerate(zip(parts, accs)):
            root = ids[i, 2, j].astype(jnp.int32)
            add(acc, root, 2, p[UPPER_TERMS + j])
    for j in range(GROUP_TERMS):
        for i, (p, acc) in enumerate(zip(parts, accs)):
            row = place(ids[i, 3, j].astype(jnp.int32), 3)
            acc[row] = acc[row] + p[TOP_TERMS + j]

    def total(first):
        part = pl.ds(first, half)
        return (a0[part] + a1[part]) + (a2[part] + a3[part])

    keep_ref[...] = total(own_core * half)
    send_ref[...] = total((1 - own_core) * half)


def core_kernel(keep_ref, core_ref, out_ref):
    out_ref[...] = (keep_ref[...] + core_ref[...]).reshape(out_ref.shape)


def down_kernel(top, own, from_a, from_b, down, col_hbm, out_ref, col, level_down, sem):
    leaves = out_ref.shape[0]
    levels = leaves.bit_length() - 1
    quarter = leaves // 4
    n, m = out_ref.shape[1:]
    fetch = Fetches(sem)
    col_copies = [fetch.rows(col_hbm, col, i * quarter, quarter) for i in range(4)]

    def total(i):
        return (own[i] + from_a[i]) + from_b[i]

    fields = top[0]
    for i in range(1, top.shape[0]):
        fields = fields + top[i]
    root = 2 * leaves - 2
    level_down[root] = rounded(fields[2] + exact_dot(exact_parts(fields[3]), down[root]))
    out = dot(level_down[root], jnp.concatenate([down[root - 2], down[root - 1]], axis=1))
    level_down[root - 2] = rounded(fields[0] + out[:, :m])
    level_down[root - 1] = rounded(fields[1] + out[:, m:])
    for level in reversed(range(levels - 1)):
        width = leaves >> level
        offset = level_offset(leaves, level)
        for t in range(0, width, 4):
            a = offset + t
            parent = offset + width + t // 2
            left = diagonal(level_down[parent], level_down[parent + 1])
            out = dot(left, square(down[a], down[a + 1], down[a + 2], down[a + 3]))
            outs = (out[:n, :m], out[:n, m:], out[n:, :m], out[n:, m:])
            for i in range(4):
                level_down[a + i] = rounded(total(leaves + a + i) + outs[i])
    for t in range(0, leaves, 4):
        if t % quarter == 0:
            col_copies[t // quarter].wait()
        span = range(t, t + 4)
        outs = quad([level_down[i] for i in span], [col[i] for i in span])
        for i, out in zip(span, outs):
            out_ref[i] = total(i) + out


PARAMS = pltpu.CompilerParams(vmem_limit_bytes=24 * 1024 * 1024)


def cost(us):
    return pl.CostEstimate(flops=int(us * 1e9), bytes_accessed=0, transcendentals=0)


def shards(
    sources, row_basis, col_basis, up_transfer, down_transfer, near_blocks, near_list,
    far_blocks, far_list, upper_blocks, upper_list, root_blocks, root_list, group_blocks, group_list,
):
    in_hbm = functools.partial(pltpu.with_memory_space_constraint, memory_space=pltpu.HBM)
    up_sources, row_basis, up_transfer, col_basis = map(in_hbm, (sources, row_basis, up_transfer, col_basis))
    near_list, far_list, upper_blocks, upper_list, root_blocks, root_list = map(
        in_hbm, (near_list.T, far_list.T, upper_blocks, upper_list, root_blocks, root_list)
    )
    leaves, columns, size = sources.shape
    nodes = up_transfer.shape[0]
    far_slots, far_nodes = far_list.shape
    near_slots = near_list.shape[0]
    groups = lax.axis_size("leaf")
    subs = lax.axis_size("sub")
    devices = groups * subs
    row = (columns, size)

    def shape(*lead):
        return jax.ShapeDtypeStruct(lead + row, F32)

    def buffer(count):
        return pltpu.VMEM((count, size, size), BF16)

    def plane(*lead):
        return pltpu.VMEM(lead + row, F32)

    def copies(count):
        return pltpu.SemaphoreType.DMA((count,))

    def call(kernel, name, us, outs, operands, specs, scratch, out_specs=None, **options):
        return pl.pallas_call(
            kernel,
            out_shape=outs,
            in_specs=specs,
            out_specs=out_specs or jax.tree.map(lambda _: VMEM, outs),
            scratch_shapes=scratch,
            compiler_params=PARAMS,
            cost_estimate=cost(us),
            name=name,
            **options,
        )(*operands)

    accumulators = lambda count: [plane(3 * count + 1)] * REPLICAS

    def permuted(x, axis, target):
        count = lax.axis_size(axis)
        return lax.ppermute(x, axis, [(i, target(i)) for i in range(count)])

    def gathered(x):
        return [x] + [permuted(x, "sub", lambda i, s=s: i ^ s) for s in (2, 1, 3)]

    coef, group, top = call(
        up_kernel, "upward", 4, (shape(nodes), shape(), shape(TOP_TERMS + 1)),
        (up_sources, upper_list, root_list, row_basis, up_transfer, upper_blocks, root_blocks),
        [ANY] * 7,
        [
            pltpu.VMEM((leaves,) + row, BF16),
            pltpu.VMEM(upper_list.shape, jnp.int32), pltpu.VMEM(root_list.shape, jnp.int32),
            buffer(leaves), buffer(nodes), buffer(UPPER_TERMS), buffer(ROOT_TERMS), copies(14),
        ],
    )
    group_parts = gathered(group)
    far_a, far_own, far_b = call(
        functools.partial(far_kernel, leaves), "far", 4, (shape(far_nodes),) * 3,
        (coef, far_list, far_blocks, group),
        [VMEM, ANY, VMEM, ANY],
        [pltpu.SMEM((far_slots, far_nodes), jnp.int32)] + accumulators(far_nodes) + [copies(1)],
    )
    terms = call(
        group_kernel, "group", 1, shape(TERMS + 1), (*group_parts, top, group_list, group_blocks),
        [VMEM] * 7, [],
    )
    term_parts = gathered(terms)
    to_a, own, to_b = call(
        near_kernel, "near", 4, (shape(leaves + far_nodes),) * 3,
        (sources, near_list, near_blocks, far_a, far_own, far_b, terms),
        [VMEM, ANY, VMEM, VMEM, VMEM, VMEM, ANY],
        [pltpu.SMEM((near_slots, leaves), jnp.int32)] + accumulators(leaves) + [copies(1)],
    )
    half = groups // 2 * 4
    everyone = ("leaf", "sub")
    from_a = permuted(to_a, everyone, lambda i: i ^ 1)
    from_b = permuted(to_b, everyone, lambda i: (((i + 1) ^ 1) - 1) % devices)

    keep, send = call(
        pack_kernel, "pack", 0, (shape(half), shape(half)), (*term_parts, own), [VMEM] * 4 + [ANY],
        [pltpu.SMEM((subs,) + row, F32)] + [plane(2 * half + 1)] * 4 + [copies(subs)],
    )
    from_core = permuted(send, "leaf", lambda i: i ^ 1)
    planes = call(core_kernel, "core", 0, shape(groups // 2, 4), (keep, from_core), [VMEM] * 2, [])
    fields = lax.all_to_all(
        pltpu.with_memory_space_constraint(planes, pltpu.VMEM), "leaf", 0, 0, tiled=True, axis_index_groups=[list(range(c, groups, 2)) for c in range(2)]
    )
    return call(
        down_kernel, "downward", 0, shape(leaves), (fields, own, from_a, from_b, down_transfer, col_basis), [VMEM] * 5 + [ANY],
        [buffer(leaves), plane(nodes), copies(4)],
    )


def solution(mesh):
    blocks = P(("leaf", "sub"), None, None)
    lists = P(("leaf", "sub"), None)
    in_specs = (
        blocks, blocks, blocks, blocks, blocks, blocks, lists,
        blocks, lists, blocks, lists, blocks, lists, blocks, lists,
    )
    return jax.shard_map(shards, mesh=mesh, in_specs=in_specs, out_specs=blocks, check_vma=False)
```

```python
import functools

import jax
import jax.numpy as jnp
from jax import lax
from jax.experimental import pallas as pl
from jax.experimental.pallas import tpu as pltpu
from jax.sharding import PartitionSpec as P

F32 = jnp.float32
BF16 = jnp.bfloat16
ANY = pl.BlockSpec(memory_space=pl.ANY)
VMEM = pl.BlockSpec(memory_space=pltpu.VMEM)
REPLICAS = 4
UPPER_TERMS, ROOT_TERMS, GROUP_TERMS = 8, 4, 4
TOP_TERMS = UPPER_TERMS + ROOT_TERMS
TERMS = TOP_TERMS + GROUP_TERMS


def rounded(x):
    return x.astype(BF16).astype(F32)


def dot(x, w):
    return jnp.dot(x.astype(BF16), w, preferred_element_type=F32)


def square(w00, w01, w10, w11):
    top = jnp.concatenate([w00, w01], axis=1)
    return jnp.concatenate([top, jnp.concatenate([w10, w11], axis=1)], axis=0)


def diagonal(x, y):
    zero = jnp.zeros_like(x)
    top = jnp.concatenate([x, zero], axis=1)
    return jnp.concatenate([top, jnp.concatenate([zero, y], axis=1)], axis=0)


def quad(xs, ws):
    left = jnp.concatenate([diagonal(xs[0], xs[1]), diagonal(xs[2], xs[3])], axis=0)
    out = dot(left, square(ws[0], ws[2], ws[1], ws[3]))
    n, m = xs[0].shape
    return [out[:n, :m], out[n : 2 * n, :m], out[2 * n : 3 * n, m:], out[3 * n :, m:]]


def exact_parts(x):
    high = rounded(x)
    rest = x - high
    middle = rounded(rest)
    return jnp.concatenate([high, middle, rest - middle], axis=0)


def exact_dot(parts, w):
    n = parts.shape[0] // 3
    out = dot(parts, w)
    return (out[2 * n :] + out[n : 2 * n]) + out[:n]


def level_offset(leaves, level):
    return 2 * leaves - 2 * (leaves >> level)


class Fetches:
    def __init__(self, sem):
        self.sem, self.count = sem, 0

    def __call__(self, src, dst):
        copy = pltpu.make_async_copy(src, dst, self.sem.at[self.count])
        copy.start()
        self.count += 1
        return copy

    def rows(self, src, dst, start, size):
        return self(src.at[pl.ds(start, size)], dst.at[pl.ds(start, size)])


def up_kernel(
    src_hbm, upper_list_hbm, root_list_hbm, rb_hbm, up_hbm, ub_hbm, rt_hbm,
    coef_ref, group_ref, top_ref, src, upper_list, root_list, rb, up, ub, rt, sem,
):
    leaves = src.shape[0]
    levels = leaves.bit_length() - 1
    quarter = leaves // 4
    fetch = Fetches(sem)
    src_copy = fetch(src_hbm, src)
    rb_copies = [fetch.rows(rb_hbm, rb, i * quarter, quarter) for i in range(4)]
    up_copies = [fetch.rows(up_hbm, up, i * quarter, quarter) for i in range(4)]
    rest = fetch.rows(up_hbm, up, leaves, leaves - 1)
    tail = [
        fetch(ub_hbm, ub), fetch(rt_hbm, rt),
        fetch(upper_list_hbm, upper_list), fetch(root_list_hbm, root_list),
    ]

    src_copy.wait()
    for t in range(0, leaves, 4):
        if t % quarter == 0:
            rb_copies[t // quarter].wait()
        span = range(t, t + 4)
        outs = quad([src[i].astype(F32) for i in span], [rb[i] for i in span])
        for i, out in zip(span, outs):
            coef_ref[i] = rounded(out)
    for level in range(levels):
        width = leaves >> level
        offset = level_offset(leaves, level)
        if level == 1:
            rest.wait()
        for t in range(0, width, 4):
            if level == 0 and t % quarter == 0:
                up_copies[t // quarter].wait()
            a = offset + t
            parent = offset + width + t // 2
            c = [coef_ref[a + i] for i in range(min(4, width))]
            if width == 2:
                left = jnp.concatenate(c, axis=1)
                out = dot(left, jnp.concatenate([up[a], up[a + 1]], axis=0))
                coef_ref[parent] = rounded(out)
            else:
                left = jnp.concatenate(
                    [jnp.concatenate(c[:2], axis=1), jnp.concatenate(c[2:], axis=1)], axis=0
                )
                out = dot(left, square(up[a], up[a + 2], up[a + 1], up[a + 3]))
                n, m = c[0].shape
                coef_ref[parent] = rounded(out[:n, :m])
                coef_ref[parent + 1] = rounded(out[n:, m:])
    top = 2 * leaves - 2
    group_ref[...] = dot(coef_ref[top], up[top])
    for c in tail:
        c.wait()
    n, m = src.shape[1:]
    left = diagonal(coef_ref[top - 2], coef_ref[top - 1])
    for k in range(0, 4, 2):
        out = dot(left, square(ub[k], ub[k + 1], ub[4 + k], ub[5 + k]))
        top_ref[k] = out[:n, :m]
        top_ref[k + 1] = out[:n, m:]
        top_ref[4 + k] = out[n:, :m]
        top_ref[5 + k] = out[n:, m:]
    for k in range(0, ROOT_TERMS, 2):
        out = dot(coef_ref[top], jnp.concatenate([rt[k], rt[k + 1]], axis=1))
        top_ref[UPPER_TERMS + k] = out[:, :m]
        top_ref[UPPER_TERMS + k + 1] = out[:, m:]
    top_ref[TOP_TERMS] = jnp.zeros((n, m), F32)
    top_ref[TOP_TERMS, 0:2, 0:4] = upper_list[...].astype(F32)
    top_ref[TOP_TERMS, 2:3, 0:4] = root_list[...].astype(F32)


def scatter_steps(left_of, mats, target_of, accs, slots, first, count, step, level, levels, start, span):
    own_index = lax.axis_index("leaf") * lax.axis_size("sub") + lax.axis_index("sub")
    shift = levels - level
    base = (own_index - 1) * (1 << shift)

    def add(replica, target, term):
        place = target - base
        row = lax.shift_right_arithmetic(place, shift) * span + start + (place & ((1 << shift) - 1))
        row = jnp.where(target >= 0, row, 3 * span)
        accs[replica][row] = accs[replica][row] + term

    def body(c, carry):
        for i in range(0, step, 2):
            t = c * step + i
            x, y = left_of(t), left_of(t + 1)
            n, m = x.shape
            left = diagonal(x, y)
            a, b = t * slots, (t + 1) * slots
            for k in range(0, slots, 2):
                out = dot(left, square(mats[a + k], mats[a + k + 1], mats[b + k], mats[b + k + 1]))
                add(0, target_of(t, k), out[:n, :m])
                add(1, target_of(t, k + 1), out[:n, m:])
                add(2, target_of(t + 1, k), out[n:, :m])
                add(3, target_of(t + 1, k + 1), out[n:, m:])
        return carry

    lax.fori_loop(first // step, (first + count) // step, body, 0)


def store_totals(accs, span, refs):
    odd = lax.axis_index("sub") & 1
    for first, ref in zip((2 - 2 * odd, 1, 2 * odd), refs):
        parts = [acc[pl.ds(first * span, span)] for acc in accs]
        ref[0:span] = (parts[0] + parts[1]) + (parts[2] + parts[3])


def near_kernel(
    src_ref, list_hbm, near, far_a, far_own, far_b, order,
    a_ref, own_ref, b_ref, near_list, a0, a1, a2, a3, sem,
):
    leaves = src_ref.shape[0]
    slots = near_list.shape[0]
    fetch = Fetches(sem)
    first = fetch(list_hbm, near_list)
    accs = (a0, a1, a2, a3)
    for acc in accs:
        acc[...] = jnp.zeros(acc.shape, F32)
    for out, part in ((a_ref, far_a), (own_ref, far_own), (b_ref, far_b)):
        out[leaves:] = part[...]
    first.wait()
    scatter_steps(
        lambda t: src_ref[t].astype(F32), near, lambda t, k: near_list[k, t], accs,
        slots, 0, leaves, 8, 0, leaves.bit_length() - 1, 0, leaves,
    )
    store_totals(accs, leaves, (a_ref, own_ref, b_ref))


def far_kernel(
    leaves, coef_ref, list_hbm, far, order, a_ref, own_ref, b_ref, far_list, a0, a1, a2, a3, sem,
):
    levels = leaves.bit_length() - 1
    slots, nodes = far_list.shape
    fetch = Fetches(sem)
    first = fetch(list_hbm, far_list)
    accs = (a0, a1, a2, a3)
    for acc in accs:
        acc[...] = jnp.zeros(acc.shape, F32)
    first.wait()
    for level in range(levels - 1):
        offset = level_offset(leaves, level)
        scatter_steps(
            lambda t: coef_ref[t], far, lambda t, k: far_list[k, t], accs,
            slots, offset, leaves >> level, min(16, leaves >> level), level, levels, offset, nodes,
        )
    store_totals(accs, nodes, (a_ref, own_ref, b_ref))


def group_kernel(g0, g1, g2, g3, top_ref, group_list, blocks, out_ref):
    coef = (g0[...] + g1[...]) + (g2[...] + g3[...])
    parts = exact_parts(coef)
    m = coef.shape[1]
    for k in range(0, GROUP_TERMS, 2):
        out = exact_dot(parts, jnp.concatenate([blocks[k], blocks[k + 1]], axis=1))
        out_ref[TOP_TERMS + k] = out[:, :m]
        out_ref[TOP_TERMS + k + 1] = out[:, m:]
    out_ref[0:TOP_TERMS] = top_ref[0:TOP_TERMS]
    out_ref[TERMS] = top_ref[TOP_TERMS]
    out_ref[TERMS, 3:4, 0:4] = group_list[...].astype(F32)


def pack_kernel(p0, p1, p2, p3, order, keep_ref, send_ref, whole, ids, a0, a1, a2, a3, sem):
    half = keep_ref.shape[0]
    parts = (p0, p1, p2, p3)
    accs = (a0, a1, a2, a3)
    for i, p in enumerate(parts):
        whole[i] = p[TERMS].astype(jnp.int32)
    copy = pltpu.make_async_copy(whole, ids, sem.at[0])
    copy.start()
    for acc in accs:
        acc[...] = jnp.zeros(acc.shape, F32)
    own_sub = lax.axis_index("sub")
    own_core = lax.axis_index("leaf") & 1
    copy.wait()

    def place(leaf, entry):
        return (leaf & 1) * half + lax.shift_right_arithmetic(leaf, 1) * 4 + entry

    def add(acc, root, entry, term):
        row = place(lax.shift_right_arithmetic(root, 2), entry)
        row = jnp.where((root & 3) == own_sub, row, 2 * half)
        acc[row] = acc[row] + term

    for j in range(UPPER_TERMS):
        for i, (p, acc) in enumerate(zip(parts, accs)):
            node = ids[i, j // 4, j % 4]
            add(acc, lax.shift_right_arithmetic(node, 1), node & 1, p[j])
    for j in range(ROOT_TERMS):
        for i, (p, acc) in enumerate(zip(parts, accs)):
            root = ids[i, 2, j]
            add(acc, root, 2, p[UPPER_TERMS + j])
    for j in range(GROUP_TERMS):
        for i, (p, acc) in enumerate(zip(parts, accs)):
            row = place(ids[i, 3, j], 3)
            acc[row] = acc[row] + p[TOP_TERMS + j]

    def total(first):
        part = pl.ds(first, half)
        return (a0[part] + a1[part]) + (a2[part] + a3[part])

    keep_ref[...] = total(own_core * half)
    send_ref[...] = total((1 - own_core) * half)


def core_kernel(keep_ref, core_ref, out_ref):
    out_ref[...] = (keep_ref[...] + core_ref[...]).reshape(out_ref.shape)


def down_kernel(top, own, from_a, from_b, down, col_hbm, out_ref, col, level_down, sem):
    leaves = out_ref.shape[0]
    levels = leaves.bit_length() - 1
    quarter = leaves // 4
    n, m = out_ref.shape[1:]
    fetch = Fetches(sem)
    col_copies = [fetch.rows(col_hbm, col, i * quarter, quarter) for i in range(4)]

    def total(i):
        return (own[i] + from_a[i]) + from_b[i]

    fields = top[0]
    for i in range(1, top.shape[0]):
        fields = fields + top[i]
    root = 2 * leaves - 2
    level_down[root] = rounded(fields[2] + exact_dot(exact_parts(fields[3]), down[root]))
    out = dot(level_down[root], jnp.concatenate([down[root - 2], down[root - 1]], axis=1))
    level_down[root - 2] = rounded(fields[0] + out[:, :m])
    level_down[root - 1] = rounded(fields[1] + out[:, m:])
    for level in reversed(range(levels - 1)):
        width = leaves >> level
        offset = level_offset(leaves, level)
        for t in range(0, width, 4):
            a = offset + t
            parent = offset + width + t // 2
            left = diagonal(level_down[parent], level_down[parent + 1])
            out = dot(left, square(down[a], down[a + 1], down[a + 2], down[a + 3]))
            outs = (out[:n, :m], out[:n, m:], out[n:, :m], out[n:, m:])
            for i in range(4):
                level_down[a + i] = rounded(total(leaves + a + i) + outs[i])
    for t in range(0, leaves, 4):
        if t % quarter == 0:
            col_copies[t // quarter].wait()
        span = range(t, t + 4)
        outs = quad([level_down[i] for i in span], [col[i] for i in span])
        for i, out in zip(span, outs):
            out_ref[i] = total(i) + out


PARAMS = pltpu.CompilerParams(vmem_limit_bytes=24 * 1024 * 1024)


def cost(us):
    return pl.CostEstimate(flops=int(us * 1e9), bytes_accessed=0, transcendentals=0)


def shards(
    sources, row_basis, col_basis, up_transfer, down_transfer, near_blocks, near_list,
    far_blocks, far_list, upper_blocks, upper_list, root_blocks, root_list, group_blocks, group_list,
):
    in_hbm = functools.partial(pltpu.with_memory_space_constraint, memory_space=pltpu.HBM)
    up_sources, row_basis, up_transfer, col_basis = map(in_hbm, (sources, row_basis, up_transfer, col_basis))
    near_list, far_list, upper_blocks, upper_list, root_blocks, root_list = map(
        in_hbm, (near_list.T, far_list.T, upper_blocks, upper_list, root_blocks, root_list)
    )
    leaves, columns, size = sources.shape
    nodes = up_transfer.shape[0]
    far_slots, far_nodes = far_list.shape
    near_slots = near_list.shape[0]
    groups = lax.axis_size("leaf")
    subs = lax.axis_size("sub")
    devices = groups * subs
    row = (columns, size)

    def shape(*lead):
        return jax.ShapeDtypeStruct(lead + row, F32)

    def buffer(count):
        return pltpu.VMEM((count, size, size), BF16)

    def plane(*lead):
        return pltpu.VMEM(lead + row, F32)

    def copies(count):
        return pltpu.SemaphoreType.DMA((count,))

    def call(kernel, name, us, outs, operands, specs, scratch, out_specs=None, **options):
        return pl.pallas_call(
            kernel,
            out_shape=outs,
            in_specs=specs,
            out_specs=out_specs or jax.tree.map(lambda _: VMEM, outs),
            scratch_shapes=scratch,
            compiler_params=PARAMS,
            cost_estimate=cost(us),
            name=name,
            **options,
        )(*operands)

    accumulators = lambda count: [plane(3 * count + 1)] * REPLICAS

    def permuted(x, axis, target):
        count = lax.axis_size(axis)
        return lax.ppermute(x, axis, [(i, target(i)) for i in range(count)])

    def gathered(x):
        return [x] + [permuted(x, "sub", lambda i, s=s: i ^ s) for s in (2, 1, 3)]

    coef, group, top = call(
        up_kernel, "upward", 4, (shape(nodes), shape(), shape(TOP_TERMS + 1)),
        (up_sources, upper_list, root_list, row_basis, up_transfer, upper_blocks, root_blocks),
        [ANY] * 7,
        [
            pltpu.VMEM((leaves,) + row, BF16),
            pltpu.VMEM(upper_list.shape, jnp.int32), pltpu.VMEM(root_list.shape, jnp.int32),
            buffer(leaves), buffer(nodes), buffer(UPPER_TERMS), buffer(ROOT_TERMS), copies(14),
        ],
    )
    group_parts = gathered(group)
    far_a, far_own, far_b = call(
        functools.partial(far_kernel, leaves), "far", 4, (shape(far_nodes),) * 3,
        (coef, far_list, far_blocks, group),
        [VMEM, ANY, VMEM, ANY],
        [pltpu.SMEM((far_slots, far_nodes), jnp.int32)] + accumulators(far_nodes) + [copies(1)],
    )
    terms = call(
        group_kernel, "group", 1, shape(TERMS + 1), (*group_parts, top, group_list, group_blocks),
        [VMEM] * 7, [],
    )
    term_parts = gathered(terms)
    to_a, own, to_b = call(
        near_kernel, "near", 4, (shape(leaves + far_nodes),) * 3,
        (sources, near_list, near_blocks, far_a, far_own, far_b, terms),
        [VMEM, ANY, VMEM, VMEM, VMEM, VMEM, ANY],
        [pltpu.SMEM((near_slots, leaves), jnp.int32)] + accumulators(leaves) + [copies(1)],
    )
    half = groups // 2 * 4
    everyone = ("leaf", "sub")
    from_a = permuted(to_a, everyone, lambda i: i ^ 1)
    from_b = permuted(to_b, everyone, lambda i: (((i + 1) ^ 1) - 1) % devices)

    keep, send = call(
        pack_kernel, "pack", 0, (shape(half), shape(half)), (*term_parts, own), [VMEM] * 4 + [ANY],
        [pltpu.VMEM((subs,) + row, jnp.int32), pltpu.SMEM((subs,) + row, jnp.int32)] + [plane(2 * half + 1)] * 4
        + [copies(1)],
    )
    from_core = permuted(send, "leaf", lambda i: i ^ 1)
    planes = call(core_kernel, "core", 0, shape(groups // 2, 4), (keep, from_core), [VMEM] * 2, [])
    fields = lax.all_to_all(
        pltpu.with_memory_space_constraint(planes, pltpu.VMEM), "leaf", 0, 0, tiled=True, axis_index_groups=[list(range(c, groups, 2)) for c in range(2)]
    )
    return call(
        down_kernel, "downward", 0, shape(leaves), (fields, own, from_a, from_b, down_transfer, col_basis), [VMEM] * 5 + [ANY],
        [buffer(leaves), plane(nodes), copies(4)],
    )


def solution(mesh):
    blocks = P(("leaf", "sub"), None, None)
    lists = P(("leaf", "sub"), None)
    in_specs = (
        blocks, blocks, blocks, blocks, blocks, blocks, lists,
        blocks, lists, blocks, lists, blocks, lists, blocks, lists,
    )
    return jax.shard_map(shards, mesh=mesh, in_specs=in_specs, out_specs=blocks, check_vma=False)
```

```python
import functools

import jax
import jax.numpy as jnp
from jax import lax
from jax.experimental import pallas as pl
from jax.experimental.pallas import tpu as pltpu
from jax.sharding import PartitionSpec as P

F32 = jnp.float32
BF16 = jnp.bfloat16
ANY = pl.BlockSpec(memory_space=pl.ANY)
VMEM = pl.BlockSpec(memory_space=pltpu.VMEM)
REPLICAS = 4
UPPER_TERMS, ROOT_TERMS, GROUP_TERMS = 8, 4, 4
TOP_TERMS = UPPER_TERMS + ROOT_TERMS
TERMS = TOP_TERMS + GROUP_TERMS


def rounded(x):
    return x.astype(BF16).astype(F32)


def dot(x, w):
    return jnp.dot(x.astype(BF16), w, preferred_element_type=F32)


def square(w00, w01, w10, w11):
    top = jnp.concatenate([w00, w01], axis=1)
    return jnp.concatenate([top, jnp.concatenate([w10, w11], axis=1)], axis=0)


def diagonal(x, y):
    zero = jnp.zeros_like(x)
    top = jnp.concatenate([x, zero], axis=1)
    return jnp.concatenate([top, jnp.concatenate([zero, y], axis=1)], axis=0)


def quad(xs, ws):
    left = jnp.concatenate([diagonal(xs[0], xs[1]), diagonal(xs[2], xs[3])], axis=0)
    out = dot(left, square(ws[0], ws[2], ws[1], ws[3]))
    n, m = xs[0].shape
    return [out[:n, :m], out[n : 2 * n, :m], out[2 * n : 3 * n, m:], out[3 * n :, m:]]


def exact_parts(x):
    high = rounded(x)
    rest = x - high
    middle = rounded(rest)
    return jnp.concatenate([high, middle, rest - middle], axis=0)


def exact_dot(parts, w):
    n = parts.shape[0] // 3
    out = dot(parts, w)
    return (out[2 * n :] + out[n : 2 * n]) + out[:n]


def level_offset(leaves, level):
    return 2 * leaves - 2 * (leaves >> level)


class Fetches:
    def __init__(self, sem):
        self.sem, self.count = sem, 0

    def __call__(self, src, dst):
        copy = pltpu.make_async_copy(src, dst, self.sem.at[self.count])
        copy.start()
        self.count += 1
        return copy

    def rows(self, src, dst, start, size):
        return self(src.at[pl.ds(start, size)], dst.at[pl.ds(start, size)])


def up_kernel(
    src_hbm, upper_list_hbm, root_list_hbm, rb_hbm, up_hbm, ub_hbm, rt_hbm,
    coef_ref, group_ref, top_ref, src, upper_list, root_list, rb, up, ub, rt, sem,
):
    leaves = src.shape[0]
    levels = leaves.bit_length() - 1
    quarter = leaves // 4
    fetch = Fetches(sem)
    src_copy = fetch(src_hbm, src)
    rb_copies = [fetch.rows(rb_hbm, rb, i * quarter, quarter) for i in range(4)]
    up_copies = [fetch.rows(up_hbm, up, i * quarter, quarter) for i in range(4)]
    rest = fetch.rows(up_hbm, up, leaves, leaves - 1)
    tail = [
        fetch(ub_hbm, ub), fetch(rt_hbm, rt),
        fetch(upper_list_hbm, upper_list), fetch(root_list_hbm, root_list),
    ]

    src_copy.wait()
    for t in range(0, leaves, 4):
        if t % quarter == 0:
            rb_copies[t // quarter].wait()
        span = range(t, t + 4)
        outs = quad([src[i].astype(F32) for i in span], [rb[i] for i in span])
        for i, out in zip(span, outs):
            coef_ref[i] = rounded(out)
    for level in range(levels):
        width = leaves >> level
        offset = level_offset(leaves, level)
        if level == 1:
            rest.wait()
        for t in range(0, width, 4):
            if level == 0 and t % quarter == 0:
                up_copies[t // quarter].wait()
            a = offset + t
            parent = offset + width + t // 2
            c = [coef_ref[a + i] for i in range(min(4, width))]
            if width == 2:
                left = jnp.concatenate(c, axis=1)
                out = dot(left, jnp.concatenate([up[a], up[a + 1]], axis=0))
                coef_ref[parent] = rounded(out)
            else:
                left = jnp.concatenate(
                    [jnp.concatenate(c[:2], axis=1), jnp.concatenate(c[2:], axis=1)], axis=0
                )
                out = dot(left, square(up[a], up[a + 2], up[a + 1], up[a + 3]))
                n, m = c[0].shape
                coef_ref[parent] = rounded(out[:n, :m])
                coef_ref[parent + 1] = rounded(out[n:, m:])
    top = 2 * leaves - 2
    group_ref[...] = dot(coef_ref[top], up[top])
    for c in tail:
        c.wait()
    n, m = src.shape[1:]
    left = diagonal(coef_ref[top - 2], coef_ref[top - 1])
    for k in range(0, 4, 2):
        out = dot(left, square(ub[k], ub[k + 1], ub[4 + k], ub[5 + k]))
        top_ref[k] = out[:n, :m]
        top_ref[k + 1] = out[:n, m:]
        top_ref[4 + k] = out[n:, :m]
        top_ref[5 + k] = out[n:, m:]
    for k in range(0, ROOT_TERMS, 2):
        out = dot(coef_ref[top], jnp.concatenate([rt[k], rt[k + 1]], axis=1))
        top_ref[UPPER_TERMS + k] = out[:, :m]
        top_ref[UPPER_TERMS + k + 1] = out[:, m:]
    top_ref[TOP_TERMS] = jnp.zeros((n, m), F32)
    top_ref[TOP_TERMS, 0:2, 0:4] = upper_list[...].astype(F32)
    top_ref[TOP_TERMS, 2:3, 0:4] = root_list[...].astype(F32)


def scatter_steps(left_of, mats, target_of, accs, slots, first, count, step, level, levels, start, span):
    own_index = lax.axis_index("leaf") * lax.axis_size("sub") + lax.axis_index("sub")
    shift = levels - level
    base = (own_index - 1) * (1 << shift)

    def add(replica, target, term):
        place = target - base
        row = lax.shift_right_arithmetic(place, shift) * span + start + (place & ((1 << shift) - 1))
        row = jnp.where(target >= 0, row, 3 * span)
        accs[replica][row] = accs[replica][row] + term

    def body(c, carry):
        for i in range(0, step, 2):
            t = c * step + i
            x, y = left_of(t), left_of(t + 1)
            n, m = x.shape
            left = diagonal(x, y)
            a, b = t * slots, (t + 1) * slots
            for k in range(0, slots, 2):
                out = dot(left, square(mats[a + k], mats[a + k + 1], mats[b + k], mats[b + k + 1]))
                add(0, target_of(t, k), out[:n, :m])
                add(1, target_of(t, k + 1), out[:n, m:])
                add(2, target_of(t + 1, k), out[n:, :m])
                add(3, target_of(t + 1, k + 1), out[n:, m:])
        return carry

    lax.fori_loop(first // step, (first + count) // step, body, 0)


def store_totals(accs, span, refs):
    odd = lax.axis_index("sub") & 1
    for first, ref in zip((2 - 2 * odd, 1, 2 * odd), refs):
        parts = [acc[pl.ds(first * span, span)] for acc in accs]
        ref[0:span] = (parts[0] + parts[1]) + (parts[2] + parts[3])


def near_kernel(
    src_ref, list_hbm, near, far_a, far_own, far_b, order,
    a_ref, own_ref, b_ref, near_list, a0, a1, a2, a3, sem,
):
    leaves = src_ref.shape[0]
    slots = near_list.shape[0]
    fetch = Fetches(sem)
    first = fetch(list_hbm, near_list)
    accs = (a0, a1, a2, a3)
    for acc in accs:
        acc[...] = jnp.zeros(acc.shape, F32)
    for out, part in ((a_ref, far_a), (own_ref, far_own), (b_ref, far_b)):
        out[leaves:] = part[...]
    first.wait()
    scatter_steps(
        lambda t: src_ref[t].astype(F32), near, lambda t, k: near_list[k, t], accs,
        slots, 0, leaves, 8, 0, leaves.bit_length() - 1, 0, leaves,
    )
    store_totals(accs, leaves, (a_ref, own_ref, b_ref))


def far_kernel(
    leaves, coef_ref, list_hbm, far, order, a_ref, own_ref, b_ref, far_list, a0, a1, a2, a3, sem,
):
    levels = leaves.bit_length() - 1
    slots, nodes = far_list.shape
    fetch = Fetches(sem)
    first = fetch(list_hbm, far_list)
    accs = (a0, a1, a2, a3)
    for acc in accs:
        acc[...] = jnp.zeros(acc.shape, F32)
    first.wait()
    for level in range(levels - 1):
        offset = level_offset(leaves, level)
        scatter_steps(
            lambda t: coef_ref[t], far, lambda t, k: far_list[k, t], accs,
            slots, offset, leaves >> level, min(16, leaves >> level), level, levels, offset, nodes,
        )
    store_totals(accs, nodes, (a_ref, own_ref, b_ref))


def group_kernel(g0, g1, g2, g3, top_ref, group_list, blocks, out_ref):
    coef = (g0[...] + g1[...]) + (g2[...] + g3[...])
    parts = exact_parts(coef)
    m = coef.shape[1]
    for k in range(0, GROUP_TERMS, 2):
        out = exact_dot(parts, jnp.concatenate([blocks[k], blocks[k + 1]], axis=1))
        out_ref[TOP_TERMS + k] = out[:, :m]
        out_ref[TOP_TERMS + k + 1] = out[:, m:]
    out_ref[0:TOP_TERMS] = top_ref[0:TOP_TERMS]
    out_ref[TERMS] = top_ref[TOP_TERMS]
    out_ref[TERMS, 3:4, 0:4] = group_list[...].astype(F32)


def pack_kernel(p0, p1, p2, p3, order, keep_ref, send_ref, whole, ids, a0, a1, a2, a3, sem):
    half = keep_ref.shape[0]
    parts = (p0, p1, p2, p3)
    accs = (a0, a1, a2, a3)
    for i, p in enumerate(parts):
        whole[i] = p[TERMS].astype(jnp.int32)
    copy = pltpu.make_async_copy(whole, ids, sem.at[0])
    copy.start()
    for acc in accs:
        acc[...] = jnp.zeros(acc.shape, F32)
    own_sub = lax.axis_index("sub")
    own_core = lax.axis_index("leaf") & 1
    copy.wait()

    def place(leaf, entry):
        return (leaf & 1) * half + lax.shift_right_arithmetic(leaf, 1) * 4 + entry

    def add(acc, root, entry, term):
        row = place(lax.shift_right_arithmetic(root, 2), entry)
        row = jnp.where((root & 3) == own_sub, row, 2 * half)
        acc[row] = acc[row] + term

    for j in range(UPPER_TERMS):
        for i, (p, acc) in enumerate(zip(parts, accs)):
            node = ids[i, j // 4, j % 4]
            add(acc, lax.shift_right_arithmetic(node, 1), node & 1, p[j])
    for j in range(ROOT_TERMS):
        for i, (p, acc) in enumerate(zip(parts, accs)):
            root = ids[i, 2, j]
            add(acc, root, 2, p[UPPER_TERMS + j])
    for j in range(GROUP_TERMS):
        for i, (p, acc) in enumerate(zip(parts, accs)):
            row = place(ids[i, 3, j], 3)
            acc[row] = acc[row] + p[TOP_TERMS + j]

    def total(first):
        part = pl.ds(first, half)
        return (a0[part] + a1[part]) + (a2[part] + a3[part])

    keep_ref[...] = total(own_core * half)
    send_ref[...] = total((1 - own_core) * half)


def down_kernel(top, own, from_a, from_b, down, col_hbm, out_ref, col, level_down, sem):
    leaves = out_ref.shape[0]
    levels = leaves.bit_length() - 1
    quarter = leaves // 4
    n, m = out_ref.shape[1:]
    fetch = Fetches(sem)
    col_copies = [fetch.rows(col_hbm, col, i * quarter, quarter) for i in range(4)]

    def total(i):
        return (own[i] + from_a[i]) + from_b[i]

    fields = top[0]
    for i in range(1, top.shape[0]):
        fields = fields + top[i]
    root = 2 * leaves - 2
    level_down[root] = rounded(fields[2] + exact_dot(exact_parts(fields[3]), down[root]))
    out = dot(level_down[root], jnp.concatenate([down[root - 2], down[root - 1]], axis=1))
    level_down[root - 2] = rounded(fields[0] + out[:, :m])
    level_down[root - 1] = rounded(fields[1] + out[:, m:])
    for level in reversed(range(levels - 1)):
        width = leaves >> level
        offset = level_offset(leaves, level)
        for t in range(0, width, 4):
            a = offset + t
            parent = offset + width + t // 2
            left = diagonal(level_down[parent], level_down[parent + 1])
            out = dot(left, square(down[a], down[a + 1], down[a + 2], down[a + 3]))
            outs = (out[:n, :m], out[:n, m:], out[n:, :m], out[n:, m:])
            for i in range(4):
                level_down[a + i] = rounded(total(leaves + a + i) + outs[i])
    for t in range(0, leaves, 4):
        if t % quarter == 0:
            col_copies[t // quarter].wait()
        span = range(t, t + 4)
        outs = quad([level_down[i] for i in span], [col[i] for i in span])
        for i, out in zip(span, outs):
            out_ref[i] = total(i) + out


PARAMS = pltpu.CompilerParams(vmem_limit_bytes=24 * 1024 * 1024)


def cost(us):
    return pl.CostEstimate(flops=int(us * 1e9), bytes_accessed=0, transcendentals=0)


def shards(
    sources, row_basis, col_basis, up_transfer, down_transfer, near_blocks, near_list,
    far_blocks, far_list, upper_blocks, upper_list, root_blocks, root_list, group_blocks, group_list,
):
    in_hbm = functools.partial(pltpu.with_memory_space_constraint, memory_space=pltpu.HBM)
    up_sources, row_basis, up_transfer, col_basis = map(in_hbm, (sources, row_basis, up_transfer, col_basis))
    near_list, far_list, upper_blocks, upper_list, root_blocks, root_list = map(
        in_hbm, (near_list.T, far_list.T, upper_blocks, upper_list, root_blocks, root_list)
    )
    leaves, columns, size = sources.shape
    nodes = up_transfer.shape[0]
    far_slots, far_nodes = far_list.shape
    near_slots = near_list.shape[0]
    groups = lax.axis_size("leaf")
    subs = lax.axis_size("sub")
    devices = groups * subs
    row = (columns, size)

    def shape(*lead):
        return jax.ShapeDtypeStruct(lead + row, F32)

    def buffer(count):
        return pltpu.VMEM((count, size, size), BF16)

    def plane(*lead):
        return pltpu.VMEM(lead + row, F32)

    def copies(count):
        return pltpu.SemaphoreType.DMA((count,))

    def call(kernel, name, us, outs, operands, specs, scratch, out_specs=None, **options):
        return pl.pallas_call(
            kernel,
            out_shape=outs,
            in_specs=specs,
            out_specs=out_specs or jax.tree.map(lambda _: VMEM, outs),
            scratch_shapes=scratch,
            compiler_params=PARAMS,
            cost_estimate=cost(us),
            name=name,
            **options,
        )(*operands)

    accumulators = lambda count: [plane(3 * count + 1)] * REPLICAS

    def permuted(x, axis, target):
        count = lax.axis_size(axis)
        return lax.ppermute(x, axis, [(i, target(i)) for i in range(count)])

    def gathered(x):
        return [x] + [permuted(x, "sub", lambda i, s=s: i ^ s) for s in (2, 1, 3)]

    coef, group, top = call(
        up_kernel, "upward", 4, (shape(nodes), shape(), shape(TOP_TERMS + 1)),
        (up_sources, upper_list, root_list, row_basis, up_transfer, upper_blocks, root_blocks),
        [ANY] * 7,
        [
            pltpu.VMEM((leaves,) + row, BF16),
            pltpu.VMEM(upper_list.shape, jnp.int32), pltpu.VMEM(root_list.shape, jnp.int32),
            buffer(leaves), buffer(nodes), buffer(UPPER_TERMS), buffer(ROOT_TERMS), copies(14),
        ],
    )
    group_parts = gathered(group)
    far_a, far_own, far_b = call(
        functools.partial(far_kernel, leaves), "far", 4, (shape(far_nodes),) * 3,
        (coef, far_list, far_blocks, group),
        [VMEM, ANY, VMEM, ANY],
        [pltpu.SMEM((far_slots, far_nodes), jnp.int32)] + accumulators(far_nodes) + [copies(1)],
    )
    terms = call(
        group_kernel, "group", 1, shape(TERMS + 1), (*group_parts, top, group_list, group_blocks),
        [VMEM] * 7, [],
    )
    term_parts = gathered(terms)
    to_a, own, to_b = call(
        near_kernel, "near", 4, (shape(leaves + far_nodes),) * 3,
        (sources, near_list, near_blocks, far_a, far_own, far_b, terms),
        [VMEM, ANY, VMEM, VMEM, VMEM, VMEM, ANY],
        [pltpu.SMEM((near_slots, leaves), jnp.int32)] + accumulators(leaves) + [copies(1)],
    )
    half = groups // 2 * 4
    everyone = ("leaf", "sub")
    from_a = permuted(to_a, everyone, lambda i: i ^ 1)
    from_b = permuted(to_b, everyone, lambda i: (((i + 1) ^ 1) - 1) % devices)

    keep, send = call(
        pack_kernel, "pack", 0, (shape(half), shape(half)), (*term_parts, own), [VMEM] * 4 + [ANY],
        [pltpu.VMEM((subs,) + row, jnp.int32), pltpu.SMEM((subs,) + row, jnp.int32)] + [plane(2 * half + 1)] * 4
        + [copies(1)],
    )
    from_core = permuted(send, "leaf", lambda i: i ^ 1)
    planes = (keep + from_core).reshape((groups // 2, 4) + row)
    fields = lax.all_to_all(
        pltpu.with_memory_space_constraint(planes, pltpu.VMEM), "leaf", 0, 0, tiled=True, axis_index_groups=[list(range(c, groups, 2)) for c in range(2)]
    )
    return call(
        down_kernel, "downward", 0, shape(leaves), (fields, own, from_a, from_b, down_transfer, col_basis), [VMEM] * 5 + [ANY],
        [buffer(leaves), plane(nodes), copies(4)],
    )


def solution(mesh):
    blocks = P(("leaf", "sub"), None, None)
    lists = P(("leaf", "sub"), None)
    in_specs = (
        blocks, blocks, blocks, blocks, blocks, blocks, lists,
        blocks, lists, blocks, lists, blocks, lists, blocks, lists,
    )
    return jax.shard_map(shards, mesh=mesh, in_specs=in_specs, out_specs=blocks, check_vma=False)
```

```python
import functools

import jax
import jax.numpy as jnp
from jax import lax
from jax.experimental import pallas as pl
from jax.experimental.pallas import tpu as pltpu
from jax.sharding import PartitionSpec as P

F32 = jnp.float32
BF16 = jnp.bfloat16
ANY = pl.BlockSpec(memory_space=pl.ANY)
VMEM = pl.BlockSpec(memory_space=pltpu.VMEM)
REPLICAS = 4
UPPER_TERMS, ROOT_TERMS, GROUP_TERMS = 8, 4, 4
TOP_TERMS = UPPER_TERMS + ROOT_TERMS
TERMS = TOP_TERMS + GROUP_TERMS


def rounded(x):
    return x.astype(BF16).astype(F32)


def dot(x, w):
    return jnp.dot(x.astype(BF16), w, preferred_element_type=F32)


def square(w00, w01, w10, w11):
    top = jnp.concatenate([w00, w01], axis=1)
    return jnp.concatenate([top, jnp.concatenate([w10, w11], axis=1)], axis=0)


def diagonal(x, y):
    zero = jnp.zeros_like(x)
    top = jnp.concatenate([x, zero], axis=1)
    return jnp.concatenate([top, jnp.concatenate([zero, y], axis=1)], axis=0)


def quad(xs, ws):
    left = jnp.concatenate([diagonal(xs[0], xs[1]), diagonal(xs[2], xs[3])], axis=0)
    out = dot(left, square(ws[0], ws[2], ws[1], ws[3]))
    n, m = xs[0].shape
    return [out[:n, :m], out[n : 2 * n, :m], out[2 * n : 3 * n, m:], out[3 * n :, m:]]


def exact_parts(x):
    high = rounded(x)
    rest = x - high
    middle = rounded(rest)
    return jnp.concatenate([high, middle, rest - middle], axis=0)


def exact_dot(parts, w):
    n = parts.shape[0] // 3
    out = dot(parts, w)
    return (out[2 * n :] + out[n : 2 * n]) + out[:n]


def level_offset(leaves, level):
    return 2 * leaves - 2 * (leaves >> level)


class Fetches:
    def __init__(self, sem):
        self.sem, self.count = sem, 0

    def __call__(self, src, dst):
        copy = pltpu.make_async_copy(src, dst, self.sem.at[self.count])
        copy.start()
        self.count += 1
        return copy

    def rows(self, src, dst, start, size):
        return self(src.at[pl.ds(start, size)], dst.at[pl.ds(start, size)])


def up_kernel(
    src_hbm, upper_list_hbm, root_list_hbm, rb_hbm, up_hbm, ub_hbm, rt_hbm,
    coef_ref, group_ref, top_ref, src, upper_list, root_list, rb, up, ub, rt, sem,
):
    leaves = src.shape[0]
    levels = leaves.bit_length() - 1
    quarter = leaves // 4
    fetch = Fetches(sem)
    src_copy = fetch(src_hbm, src)
    rb_copies = [fetch.rows(rb_hbm, rb, i * quarter, quarter) for i in range(4)]
    up_copies = [fetch.rows(up_hbm, up, i * quarter, quarter) for i in range(4)]
    rest = fetch.rows(up_hbm, up, leaves, leaves - 1)
    tail = [
        fetch(ub_hbm, ub), fetch(rt_hbm, rt),
        fetch(upper_list_hbm, upper_list), fetch(root_list_hbm, root_list),
    ]

    src_copy.wait()
    for t in range(0, leaves, 4):
        if t % quarter == 0:
            rb_copies[t // quarter].wait()
        span = range(t, t + 4)
        outs = quad([src[i].astype(F32) for i in span], [rb[i] for i in span])
        for i, out in zip(span, outs):
            coef_ref[i] = rounded(out)
    for level in range(levels):
        width = leaves >> level
        offset = level_offset(leaves, level)
        if level == 1:
            rest.wait()
        for t in range(0, width, 4):
            if level == 0 and t % quarter == 0:
                up_copies[t // quarter].wait()
            a = offset + t
            parent = offset + width + t // 2
            c = [coef_ref[a + i] for i in range(min(4, width))]
            if width == 2:
                left = jnp.concatenate(c, axis=1)
                out = dot(left, jnp.concatenate([up[a], up[a + 1]], axis=0))
                coef_ref[parent] = rounded(out)
            else:
                left = jnp.concatenate(
                    [jnp.concatenate(c[:2], axis=1), jnp.concatenate(c[2:], axis=1)], axis=0
                )
                out = dot(left, square(up[a], up[a + 2], up[a + 1], up[a + 3]))
                n, m = c[0].shape
                coef_ref[parent] = rounded(out[:n, :m])
                coef_ref[parent + 1] = rounded(out[n:, m:])
    top = 2 * leaves - 2
    group_ref[...] = dot(coef_ref[top], up[top])
    for c in tail:
        c.wait()
    n, m = src.shape[1:]
    left = diagonal(coef_ref[top - 2], coef_ref[top - 1])
    for k in range(0, 4, 2):
        out = dot(left, square(ub[k], ub[k + 1], ub[4 + k], ub[5 + k]))
        top_ref[k] = out[:n, :m]
        top_ref[k + 1] = out[:n, m:]
        top_ref[4 + k] = out[n:, :m]
        top_ref[5 + k] = out[n:, m:]
    for k in range(0, ROOT_TERMS, 2):
        out = dot(coef_ref[top], jnp.concatenate([rt[k], rt[k + 1]], axis=1))
        top_ref[UPPER_TERMS + k] = out[:, :m]
        top_ref[UPPER_TERMS + k + 1] = out[:, m:]
    top_ref[TOP_TERMS] = jnp.zeros((n, m), F32)
    top_ref[TOP_TERMS, 0:2, 0:4] = upper_list[...].astype(F32)
    top_ref[TOP_TERMS, 2:3, 0:4] = root_list[...].astype(F32)


def scatter_steps(left_of, mats, target_of, accs, slots, first, count, step, level, levels, start, span):
    own_index = lax.axis_index("leaf") * lax.axis_size("sub") + lax.axis_index("sub")
    shift = levels - level
    base = (own_index - 1) * (1 << shift)

    def add(replica, target, term):
        place = target - base
        row = lax.shift_right_arithmetic(place, shift) * span + start + (place & ((1 << shift) - 1))
        row = jnp.where(target >= 0, row, 3 * span)
        accs[replica][row] = accs[replica][row] + term

    def body(c, carry):
        for i in range(0, step, 2):
            t = c * step + i
            x, y = left_of(t), left_of(t + 1)
            n, m = x.shape
            left = diagonal(x, y)
            a, b = t * slots, (t + 1) * slots
            for k in range(0, slots, 2):
                out = dot(left, square(mats[a + k], mats[a + k + 1], mats[b + k], mats[b + k + 1]))
                add(0, target_of(t, k), out[:n, :m])
                add(1, target_of(t, k + 1), out[:n, m:])
                add(2, target_of(t + 1, k), out[n:, :m])
                add(3, target_of(t + 1, k + 1), out[n:, m:])
        return carry

    lax.fori_loop(first // step, (first + count) // step, body, 0)


def store_totals(accs, span, refs):
    odd = lax.axis_index("sub") & 1
    for first, ref in zip((2 - 2 * odd, 1, 2 * odd), refs):
        parts = [acc[pl.ds(first * span, span)] for acc in accs]
        ref[0:span] = (parts[0] + parts[1]) + (parts[2] + parts[3])


def near_kernel(
    src_ref, list_hbm, near, far_a, far_own, far_b, order,
    a_ref, own_ref, b_ref, near_list, a0, a1, a2, a3, sem,
):
    leaves = src_ref.shape[0]
    slots = near_list.shape[0]
    fetch = Fetches(sem)
    first = fetch(list_hbm, near_list)
    accs = (a0, a1, a2, a3)
    for acc in accs:
        acc[...] = jnp.zeros(acc.shape, F32)
    for out, part in ((a_ref, far_a), (own_ref, far_own), (b_ref, far_b)):
        out[leaves:] = part[...]
    first.wait()
    scatter_steps(
        lambda t: src_ref[t].astype(F32), near, lambda t, k: near_list[k, t], accs,
        slots, 0, leaves, 8, 0, leaves.bit_length() - 1, 0, leaves,
    )
    store_totals(accs, leaves, (a_ref, own_ref, b_ref))


def far_kernel(
    leaves, coef_ref, list_hbm, far, order, a_ref, own_ref, b_ref, far_list, a0, a1, a2, a3, sem,
):
    levels = leaves.bit_length() - 1
    slots, nodes = far_list.shape
    fetch = Fetches(sem)
    first = fetch(list_hbm, far_list)
    accs = (a0, a1, a2, a3)
    for acc in accs:
        acc[...] = jnp.zeros(acc.shape, F32)
    first.wait()
    for level in range(levels - 1):
        offset = level_offset(leaves, level)
        scatter_steps(
            lambda t: coef_ref[t], far, lambda t, k: far_list[k, t], accs,
            slots, offset, leaves >> level, min(16, leaves >> level), level, levels, offset, nodes,
        )
    store_totals(accs, nodes, (a_ref, own_ref, b_ref))


def group_kernel(g0, g1, g2, g3, top_ref, group_list, blocks, out_ref):
    coef = (g0[...] + g1[...]) + (g2[...] + g3[...])
    parts = exact_parts(coef)
    m = coef.shape[1]
    for k in range(0, GROUP_TERMS, 2):
        out = exact_dot(parts, jnp.concatenate([blocks[k], blocks[k + 1]], axis=1))
        out_ref[TOP_TERMS + k] = out[:, :m]
        out_ref[TOP_TERMS + k + 1] = out[:, m:]
    out_ref[0:TOP_TERMS] = top_ref[0:TOP_TERMS]
    out_ref[TERMS] = top_ref[TOP_TERMS]
    out_ref[TERMS, 3:4, 0:4] = group_list[...].astype(F32)


def pack_kernel(p0, p1, p2, p3, order, keep_ref, send_ref, whole, ids, a0, a1, sem):
    half = keep_ref.shape[0]
    parts = (p0, p1, p2, p3)
    accs = (a0, a1, a0, a1)
    for i, p in enumerate(parts):
        whole[i] = p[TERMS].astype(jnp.int32)
    copy = pltpu.make_async_copy(whole, ids, sem.at[0])
    copy.start()
    for acc in (a0, a1):
        acc[...] = jnp.zeros(acc.shape, F32)
    own_sub = lax.axis_index("sub")
    own_core = lax.axis_index("leaf") & 1
    copy.wait()

    def place(leaf, entry):
        return (leaf & 1) * half + lax.shift_right_arithmetic(leaf, 1) * 4 + entry

    def add(acc, root, entry, term):
        row = place(lax.shift_right_arithmetic(root, 2), entry)
        row = jnp.where((root & 3) == own_sub, row, 2 * half)
        acc[row] = acc[row] + term

    for j in range(UPPER_TERMS):
        for i, (p, acc) in enumerate(zip(parts, accs)):
            node = ids[i, j // 4, j % 4]
            add(acc, lax.shift_right_arithmetic(node, 1), node & 1, p[j])
    for j in range(ROOT_TERMS):
        for i, (p, acc) in enumerate(zip(parts, accs)):
            root = ids[i, 2, j]
            add(acc, root, 2, p[UPPER_TERMS + j])
    for j in range(GROUP_TERMS):
        for i, (p, acc) in enumerate(zip(parts, accs)):
            row = place(ids[i, 3, j], 3)
            acc[row] = acc[row] + p[TOP_TERMS + j]

    def total(first):
        part = pl.ds(first, half)
        return a0[part] + a1[part]

    keep_ref[...] = total(own_core * half)
    send_ref[...] = total((1 - own_core) * half)


def core_kernel(keep_ref, core_ref, out_ref):
    out_ref[...] = (keep_ref[...] + core_ref[...]).reshape(out_ref.shape)


def down_kernel(top, own, from_a, from_b, down, col_hbm, out_ref, col, level_down, sem):
    leaves = out_ref.shape[0]
    levels = leaves.bit_length() - 1
    quarter = leaves // 4
    n, m = out_ref.shape[1:]
    fetch = Fetches(sem)
    col_copies = [fetch.rows(col_hbm, col, i * quarter, quarter) for i in range(4)]

    def total(i):
        return (own[i] + from_a[i]) + from_b[i]

    fields = top[0]
    for i in range(1, top.shape[0]):
        fields = fields + top[i]
    root = 2 * leaves - 2
    level_down[root] = rounded(fields[2] + exact_dot(exact_parts(fields[3]), down[root]))
    out = dot(level_down[root], jnp.concatenate([down[root - 2], down[root - 1]], axis=1))
    level_down[root - 2] = rounded(fields[0] + out[:, :m])
    level_down[root - 1] = rounded(fields[1] + out[:, m:])
    for level in reversed(range(levels - 1)):
        width = leaves >> level
        offset = level_offset(leaves, level)
        for t in range(0, width, 4):
            a = offset + t
            parent = offset + width + t // 2
            left = diagonal(level_down[parent], level_down[parent + 1])
            out = dot(left, square(down[a], down[a + 1], down[a + 2], down[a + 3]))
            outs = (out[:n, :m], out[:n, m:], out[n:, :m], out[n:, m:])
            for i in range(4):
                level_down[a + i] = rounded(total(leaves + a + i) + outs[i])
    for t in range(0, leaves, 4):
        if t % quarter == 0:
            col_copies[t // quarter].wait()
        span = range(t, t + 4)
        outs = quad([level_down[i] for i in span], [col[i] for i in span])
        for i, out in zip(span, outs):
            out_ref[i] = total(i) + out


PARAMS = pltpu.CompilerParams(vmem_limit_bytes=24 * 1024 * 1024)


def cost(us):
    return pl.CostEstimate(flops=int(us * 1e9), bytes_accessed=0, transcendentals=0)


def shards(
    sources, row_basis, col_basis, up_transfer, down_transfer, near_blocks, near_list,
    far_blocks, far_list, upper_blocks, upper_list, root_blocks, root_list, group_blocks, group_list,
):
    in_hbm = functools.partial(pltpu.with_memory_space_constraint, memory_space=pltpu.HBM)
    up_sources, row_basis, up_transfer, col_basis = map(in_hbm, (sources, row_basis, up_transfer, col_basis))
    near_list, far_list, upper_blocks, upper_list, root_blocks, root_list = map(
        in_hbm, (near_list.T, far_list.T, upper_blocks, upper_list, root_blocks, root_list)
    )
    leaves, columns, size = sources.shape
    nodes = up_transfer.shape[0]
    far_slots, far_nodes = far_list.shape
    near_slots = near_list.shape[0]
    groups = lax.axis_size("leaf")
    subs = lax.axis_size("sub")
    devices = groups * subs
    row = (columns, size)

    def shape(*lead):
        return jax.ShapeDtypeStruct(lead + row, F32)

    def buffer(count):
        return pltpu.VMEM((count, size, size), BF16)

    def plane(*lead):
        return pltpu.VMEM(lead + row, F32)

    def copies(count):
        return pltpu.SemaphoreType.DMA((count,))

    def call(kernel, name, us, outs, operands, specs, scratch, out_specs=None, **options):
        return pl.pallas_call(
            kernel,
            out_shape=outs,
            in_specs=specs,
            out_specs=out_specs or jax.tree.map(lambda _: VMEM, outs),
            scratch_shapes=scratch,
            compiler_params=PARAMS,
            cost_estimate=cost(us),
            name=name,
            **options,
        )(*operands)

    accumulators = lambda count: [plane(3 * count + 1)] * REPLICAS

    def permuted(x, axis, target):
        count = lax.axis_size(axis)
        return lax.ppermute(x, axis, [(i, target(i)) for i in range(count)])

    def gathered(x):
        return [x] + [permuted(x, "sub", lambda i, s=s: i ^ s) for s in (2, 1, 3)]

    coef, group, top = call(
        up_kernel, "upward", 4, (shape(nodes), shape(), shape(TOP_TERMS + 1)),
        (up_sources, upper_list, root_list, row_basis, up_transfer, upper_blocks, root_blocks),
        [ANY] * 7,
        [
            pltpu.VMEM((leaves,) + row, BF16),
            pltpu.VMEM(upper_list.shape, jnp.int32), pltpu.VMEM(root_list.shape, jnp.int32),
            buffer(leaves), buffer(nodes), buffer(UPPER_TERMS), buffer(ROOT_TERMS), copies(14),
        ],
    )
    group_parts = gathered(group)
    far_a, far_own, far_b = call(
        functools.partial(far_kernel, leaves), "far", 4, (shape(far_nodes),) * 3,
        (coef, far_list, far_blocks, group),
        [VMEM, ANY, VMEM, ANY],
        [pltpu.SMEM((far_slots, far_nodes), jnp.int32)] + accumulators(far_nodes) + [copies(1)],
    )
    terms = call(
        group_kernel, "group", 1, shape(TERMS + 1), (*group_parts, top, group_list, group_blocks),
        [VMEM] * 7, [],
    )
    term_parts = gathered(terms)
    to_a, own, to_b = call(
        near_kernel, "near", 4, (shape(leaves + far_nodes),) * 3,
        (sources, near_list, near_blocks, far_a, far_own, far_b, terms),
        [VMEM, ANY, VMEM, VMEM, VMEM, VMEM, ANY],
        [pltpu.SMEM((near_slots, leaves), jnp.int32)] + accumulators(leaves) + [copies(1)],
    )
    half = groups // 2 * 4
    everyone = ("leaf", "sub")
    from_a = permuted(to_a, everyone, lambda i: i ^ 1)
    from_b = permuted(to_b, everyone, lambda i: (((i + 1) ^ 1) - 1) % devices)

    keep, send = call(
        pack_kernel, "pack", 0, (shape(half), shape(half)), (*term_parts, own), [VMEM] * 4 + [ANY],
        [pltpu.VMEM((subs,) + row, jnp.int32), pltpu.SMEM((subs,) + row, jnp.int32)] + [plane(2 * half + 1)] * 2
        + [copies(1)],
    )
    from_core = permuted(send, "leaf", lambda i: i ^ 1)
    planes = call(core_kernel, "core", 0, shape(groups // 2, 4), (keep, from_core), [VMEM] * 2, [])
    fields = lax.all_to_all(
        pltpu.with_memory_space_constraint(planes, pltpu.VMEM), "leaf", 0, 0, tiled=True, axis_index_groups=[list(range(c, groups, 2)) for c in range(2)]
    )
    return call(
        down_kernel, "downward", 0, shape(leaves), (fields, own, from_a, from_b, down_transfer, col_basis), [VMEM] * 5 + [ANY],
        [buffer(leaves), plane(nodes), copies(4)],
    )


def solution(mesh):
    blocks = P(("leaf", "sub"), None, None)
    lists = P(("leaf", "sub"), None)
    in_specs = (
        blocks, blocks, blocks, blocks, blocks, blocks, lists,
        blocks, lists, blocks, lists, blocks, lists, blocks, lists,
    )
    return jax.shard_map(shards, mesh=mesh, in_specs=in_specs, out_specs=blocks, check_vma=False)
```
